32 devices in a mesh: groups: 2 (over x), src: 16 (over z, y, core).
Axes of the slice: x: 2, y: 2, z: 4, core: 2. Of those that a mesh axis runs over, the one named last changes fastest.
Arguments:
- src_emb: bfloat16 [8192, 256], P(('groups', 'src')), parts along dimension 0, may hold values from -64 to 64
- dst_emb: bfloat16 [8192, 256], P(('groups', 'src')), parts along dimension 0, may hold values from -64 to 64
- tile_dst: int32 [32, 16], P(('groups', 'src')), parts along dimension 0, may hold values from 0 to 15, as said below
- tile_count: int32 [32], P(('groups', 'src')), parts along dimension 0, may hold values from 1 to 16, 128 in all
- beliefs: bfloat16 [64, 4096], P('groups', 'src'), parts along dimension 0, may hold values from 0.019897461 to 1
- grad_next: bfloat16 [64, 4096], P('groups', 'src'), parts along dimension 0, may hold values from -6 to 6
Outputs:
- next_belief: float32 [64, 4096], P('groups', 'src'), parts along dimension 0
- grad_belief: bfloat16 [64, 4096], P('groups', 'src'), parts along dimension 0
- grad_src: float32 [8192, 256], P(('groups', 'src')), parts along dimension 0
- grad_dst: float32 [8192, 256], P(('groups', 'src')), parts along dimension 0
The draws below stay inside these ranges and needn't reach their ends.
There are 2 independent parts, one for each index of `groups`. The reference program is written for one: setup_inputs(seed, part) draws one part's arguments, and reference() takes and returns one part's arrays. A program takes and returns all parts, laid end to end along the dimension named above; each array names one. Nothing has to cross between parts.
Inputs may be any that keep to these rules, and one draw needn't show every extreme that they name: `tile_dst`: each row holds every destination block exactly once; only its first tile_count entries are listed.
All inputs are finite; a program needn't handle non-finite values. No bound on the sum of `tile_count` on one device may be relied on, other than what follows from the above.
Results may differ from the reference program's by a relative error of at most 0.0057.
Values may be sent and summed in bfloat16 or wider, within the bound.
No kernel may reach another device: no remote copies, remote signals or barrier semaphores. Data moves between devices by JAX's collectives and lax.ppermute only.
A program may use at most 128 MiB of HBM per device.

```python
import math
import jax
import jax.numpy as jnp
import numpy as np
from jax import lax

BLOCK = 256
E = 256
BATCH = 32
STATES = 4096
NBLK = 16


def first_tiles(key):
    keys = jax.random.split(key, NBLK)
    return jax.vmap(lambda one_key: jax.random.permutation(one_key, NBLK))(keys).astype(jnp.int32)


def emb_scale():
    return 0.8 ** 0.5 / E ** 0.25


def row_scales(key, low, high):
    return jnp.exp(jax.random.uniform(key, (STATES, 1), minval=math.log(low), maxval=math.log(high)))


def draw_tile_dst(key, part):
    order = first_tiles(key)
    return order


def draw_dst_emb(key, part):
    key = jax.random.fold_in(key, 2)
    base_key, scale_key = jax.random.split(key)
    scales = row_scales(scale_key, 0.35, 3.5)
    values = jax.random.truncated_normal(base_key, -6.0, 6.0, (STATES, E)) * emb_scale() * scales
    return values.astype(jnp.bfloat16)


def draw_src_emb(key, part):
    key = jax.random.fold_in(key, 3)
    base_key, scale_key = jax.random.split(key, 2)
    scales = row_scales(scale_key, 0.25, 2.5)
    values = jax.random.truncated_normal(base_key, -6.0, 6.0, (STATES, E)) * emb_scale() * scales
    return values.astype(jnp.bfloat16)


def shard_levels(stream_key, shape, shards, smallest, high):
    def one(axis_at, parts):
        steps = jax.random.uniform(jax.random.fold_in(jax.random.fold_in(stream_key, 6), axis_at), (parts,), jnp.float32, smallest / len(shards), high / len(shards))
        return jnp.repeat(jnp.exp(steps), shape[axis_at] // parts).reshape((-1,) + (1,) * (len(shape) - axis_at - 1))

    level = one(*shards[0])
    for cut in shards[1:]:
        level = level * one(*cut)
    return level


def split_up(amount, total, most, skew):
    loads = [(1 << 20) // math.isqrt(rank ** skew) + 1 for rank in range(2, amount + 1)]
    rest, holding = total - most - (amount - 1), [1] * (amount - 1)
    while rest > 0:
        movable = [i for i in range(amount - 1) if holding[i] < most]
        whole, left = sum([loads[i] for i in movable]), rest
        for i in movable:
            extra = min(most - holding[i], max(1, left * loads[i] // whole), rest)
            holding[i] = holding[i] + extra
            rest = rest - extra
    return np.array([most] + holding)


def uneven_parts(stream_key, amount, total, most, lean):
    if amount == 2:
        one = jax.random.randint(stream_key, (), max(1, total - most), min(most, total - 1) + 1)
        return jnp.stack([one, total - one])
    tallies = jnp.asarray(split_up(amount, total, most, lean), jnp.int32)
    couples = (amount - 1) // 2
    giver, sink = tallies[1:1 + 2 * couples:2], tallies[2:2 + 2 * couples:2]
    room = jnp.minimum(giver - 1, most - sink)
    moved = jax.random.randint(jax.random.fold_in(stream_key, 1), (couples,), 0, 1 << 20) % (room + 1)
    tallies = tallies.at[1:1 + 2 * couples:2].set(giver - moved).at[2:2 + 2 * couples:2].set(sink + moved)
    return tallies[jax.random.permutation(jax.random.fold_in(stream_key, 2), amount)]


def gaussian(stream_key, dims, scale, bound, cuts=(), held_as=jnp.bfloat16):
    loudness = shard_levels(stream_key, dims, cuts, -0.22, 0.18) if cuts else 1.0
    drawn = jax.random.normal(stream_key, dims, jnp.float32) * scale * loudness
    return jnp.minimum(jnp.maximum(drawn, -bound), bound).astype(held_as)


def setup_inputs(seed: int = 0, part: int = 0) -> dict:
    seeds = jax.random.split(jax.random.key(seed), 7)
    part_keys = jax.random.split(jax.random.fold_in(seeds[6], part), 7)
    return {
        "src_emb": draw_src_emb(jax.random.fold_in(jax.random.fold_in(seeds[6], part), 71), part),
        "dst_emb": draw_dst_emb(jax.random.fold_in(jax.random.fold_in(seeds[6], part), 71), part),
        "tile_dst": draw_tile_dst(jax.random.fold_in(jax.random.fold_in(seeds[6], part), 71), part),
        "tile_count": uneven_parts(part_keys[3], NBLK, NBLK * NBLK // 2, NBLK, 2).astype(jnp.int32),
        "beliefs": jnp.clip(jnp.exp(math.log(1.0) - 3.9171631 * jax.random.uniform(part_keys[4], (BATCH, STATES), jnp.float32) ** shard_levels(part_keys[4], (BATCH, STATES), ((1, 16),), -0.2, 0.2)), 0.019897461, 1.0).astype(jnp.bfloat16),
        "grad_next": gaussian(part_keys[5], (BATCH, STATES), 1.0, 6.0, ((1, 16),)),
    }


def reference(src_emb, dst_emb, tile_dst, tile_count, beliefs, grad_next):
    block_count = STATES // BLOCK
    dst_blocks = dst_emb.reshape(block_count, BLOCK, E)
    src_blocks = src_emb.reshape(block_count, BLOCK, E)
    grad_blocks = grad_next.reshape(BATCH, block_count, BLOCK)
    belief_blocks = jnp.transpose(beliefs.reshape(BATCH, block_count, BLOCK), (1, 0, 2))
    slot_of_col = jnp.arange(block_count * BLOCK, dtype=jnp.int32) // BLOCK

    def one_block(carried, inputs):
        belief_sum, dst_grads = carried
        src_rows, tile_ids, tile_total, belief_rows = inputs
        panel_rows = dst_blocks[tile_ids].reshape(block_count * BLOCK, E)
        slot_valid = slot_of_col < tile_total
        logits = jnp.dot(src_rows, panel_rows.T, preferred_element_type=jnp.float32)
        masked = jnp.where(slot_valid[None, :], logits, -jnp.inf)
        row_max = jnp.max(masked, axis=1, keepdims=True)
        row_total = jnp.sum(jnp.exp(masked - row_max), axis=1, keepdims=True)
        prob_full = jnp.exp(masked - (row_max + jnp.log(row_total)))
        prob_low = prob_full.astype(jnp.bfloat16)
        contrib = jnp.dot(belief_rows, prob_low, preferred_element_type=jnp.float32)
        belief_sum = belief_sum.at[:, tile_ids].add(contrib.reshape(BATCH, block_count, BLOCK))
        grad_cols = grad_blocks[:, tile_ids].reshape(BATCH, block_count * BLOCK)
        belief_grad = jnp.dot(grad_cols, prob_low.T, preferred_element_type=jnp.float32)
        row_dot = jnp.sum(belief_rows.astype(jnp.float32) * belief_grad, axis=0)
        prob_grad = jnp.dot(belief_rows.T, grad_cols, preferred_element_type=jnp.float32)
        logit_grad = (prob_full * (prob_grad - row_dot[:, None])).astype(jnp.bfloat16)
        src_grad = jnp.dot(logit_grad, panel_rows, preferred_element_type=jnp.float32)
        dst_term = jnp.dot(logit_grad.T, src_rows, preferred_element_type=jnp.float32)
        dst_grads = dst_grads.at[tile_ids].add(dst_term.reshape(block_count, BLOCK, E))
        return (belief_sum, dst_grads), (belief_grad.astype(jnp.bfloat16), src_grad)

    start = (jnp.zeros((BATCH, block_count, BLOCK), jnp.float32), jnp.zeros((block_count, BLOCK, E), jnp.float32))
    final, stacked = lax.scan(one_block, start, (src_blocks, tile_dst.astype(jnp.int32), tile_count.astype(jnp.int32), belief_blocks))
    belief_sum, dst_grads = final
    grad_rows, src_grads = stacked
    grad_belief = jnp.transpose(grad_rows, (1, 0, 2)).reshape(BATCH, STATES)
    return (belief_sum.reshape(BATCH, STATES), grad_belief, src_grads.reshape(STATES, E), dst_grads.reshape(STATES, E))
```

```python
import functools

import jax
import jax.numpy as jnp
from jax import lax
from jax.experimental import pallas as pl
from jax.experimental.pallas import tpu as pltpu
from jax.sharding import PartitionSpec as P

f32 = jnp.float32
bf16 = jnp.bfloat16
unlisted = 1e30
mib = 1 << 20


def grid_of(n):
    bits = n.bit_length() - 1
    n_row = 1 << (bits // 2)
    return n_row, n // n_row


def dot(a, b, dims):
    return lax.dot_general(a, b, (dims, ((), ())), preferred_element_type=f32)


NN = ((1,), (0,))
NT = ((1,), (1,))
TN = ((0,), (0,))


def block_of(index, size):
    return pl.ds(pl.multiple_of(index * size, size), size)


def whole_vmem():
    return pl.BlockSpec(memory_space=pltpu.VMEM)


def anywhere():
    return pl.BlockSpec(memory_space=pl.ANY)


def in_smem():
    return pl.BlockSpec(memory_space=pltpu.SMEM)


def pack_kernel(n, me_ref, tile_ref, count_ref, src_ref, bel_ref, dst_ref, grad_ref, src_pack, dst_pack, listed):
    rows, batch = src_ref.shape[0], bel_ref.shape[0]
    me = me_ref[0]
    for k in range(n):
        listed[pl.ds(tile_ref[0, k] ^ me, 1), :] = jnp.broadcast_to(
            jnp.where(k < count_ref[0], 1.0, 0.0), (1, listed.shape[1])
        ).astype(f32)
    src_pack[:rows] = src_ref[...]
    src_pack[rows : rows + batch] = bel_ref[...]
    src_pack[rows + batch :] = listed[...].astype(bf16)
    dst_pack[:rows] = dst_ref[...]
    dst_pack[rows:] = grad_ref[...]


def pack(n, me, tile_dst, tile_count, src_emb, beliefs, dst_emb, grad_next):
    rows, width = src_emb.shape
    batch = beliefs.shape[0]
    return pl.pallas_call(
        functools.partial(pack_kernel, n),
        out_shape=(
            jax.ShapeDtypeStruct((rows + batch + n, width), bf16),
            jax.ShapeDtypeStruct((rows + batch, width), bf16),
        ),
        in_specs=[in_smem()] * 3 + [whole_vmem()] * 4,
        out_specs=(whole_vmem(), whole_vmem()),
        scratch_shapes=[pltpu.VMEM((n, width), f32)],
        name="pack",
    )(me, tile_dst, tile_count, src_emb, beliefs, dst_emb, grad_next)


def unpack_copies(n_row, n_col, rows, batch, n, src_packs, dst_packs, src_all, bel_all, listed_all, dst_all, grad_all, sems):
    copies = []

    def add(source, target):
        copies.append(pltpu.make_async_copy(source, target, sems.at[len(copies)]))

    for t in range(n_col):
        add(dst_packs[t].at[pl.ds(0, rows)], dst_all.at[pl.ds(t * rows, rows)])
        add(dst_packs[t].at[pl.ds(rows, batch)], grad_all.at[t])
    for s in range(n_row):
        add(src_packs[s].at[pl.ds(0, rows)], src_all.at[pl.ds(s * rows, rows)])
        add(src_packs[s].at[pl.ds(rows, batch)], bel_all.at[:, pl.ds(s * rows, rows)])
        if listed_all is not None:
            add(src_packs[s].at[pl.ds(rows + batch, n)], listed_all.at[s])
    return copies


def unpack_scratch(n_row, n_col, rows, width, batch, n, with_listed):
    return [
        pltpu.VMEM((n_row * rows, width), bf16),
        pltpu.VMEM((batch, n_row * rows), bf16),
        *([pltpu.VMEM((n_row, n, rows), bf16)] if with_listed else []),
        pltpu.VMEM((n_col * rows, width), bf16),
        pltpu.VMEM((n_col, batch, rows), bf16),
        pltpu.SemaphoreType.DMA(((3 if with_listed else 2) * n_row + 2 * n_col,)),
    ]


def stat_rows(n_row):
    return (3 * n_row + 7) // 8 * 8


def score_kernel(n_row, n_col, rows, batch, *refs):
    n = n_row * n_col
    src_packs, refs = refs[:n_row], refs[n_row:]
    dst_packs, refs = refs[:n_col], refs[n_col:]
    prob_ref, refs = refs[0], refs[1:]
    messages, refs = refs[:n_row], refs[n_row:]
    src_all, bel_all, listed_all, dst_all, grad_all, sems, bias, grad_sum = refs
    span = n_row * rows
    copies = unpack_copies(
        n_row, n_col, rows, batch, n, src_packs, dst_packs, src_all, bel_all, listed_all, dst_all, grad_all, sems
    )
    for copy in copies:
        copy.start()
    for copy in copies:
        copy.wait()
    for s in range(n_row):
        listed = (listed_all[s].astype(f32) - 1.0) * unlisted
        for t in range(n_col):
            bias[t, 0:1, s * rows : (s + 1) * rows] = listed[t * n_row + s : t * n_row + s + 1]

    def logits_of(t, top):
        here = block_of(t, rows)
        logits = dot(dst_all[here], src_all[...], NT) + bias[t, 0:1]
        prob_ref[here] = logits
        return jnp.maximum(top, jnp.max(logits.reshape(rows // 8, 8, span), axis=0))

    top = lax.fori_loop(0, n_col, logits_of, jnp.full((8, span), -unlisted, f32))
    top = jnp.max(top, axis=0, keepdims=True)
    grad_sum[...] = jnp.zeros_like(grad_sum)

    def exps_of(t, total):
        here = block_of(t, rows)
        prob = jnp.exp(prob_ref[here] - top)
        prob_ref[here] = prob
        grad_sum[...] += dot(grad_all[t], prob.astype(bf16), NN)
        return total + jnp.sum(prob.reshape(rows // 8, 8, span), axis=0)

    total = lax.fori_loop(0, n_col, exps_of, jnp.zeros((8, span), f32))
    total = jnp.sum(total, axis=0, keepdims=True)
    row_dot = jnp.sum(bel_all[...].astype(f32) * grad_sum[...], axis=0, keepdims=True)
    head = stat_rows(n_row)
    for s in range(n_row):
        messages[s][:head] = jnp.zeros((head, rows), f32)
        for u in range(n_row):
            lanes = slice(u * rows, (u + 1) * rows)
            for kind, value in enumerate((top, total, row_dot)):
                messages[s][kind * n_row + u : kind * n_row + u + 1] = value[:, lanes]
        messages[s][head:] = grad_sum[:, s * rows : (s + 1) * rows]


def scores(n_row, n_col, batch, src_packs, dst_packs):
    n = n_row * n_col
    width = src_packs[0].shape[1]
    rows = dst_packs[0].shape[0] - batch
    message = jax.ShapeDtypeStruct((stat_rows(n_row) + batch, rows), f32)
    tiles = n * rows * rows
    return pl.pallas_call(
        functools.partial(score_kernel, n_row, n_col, rows, batch),
        out_shape=(jax.ShapeDtypeStruct((n_col * rows, n_row * rows), f32),) + (message,) * n_row,
        in_specs=[anywhere()] * (n_row + n_col),
        out_specs=(whole_vmem(),) * (1 + n_row),
        scratch_shapes=unpack_scratch(n_row, n_col, rows, width, batch, n, True)
        + [pltpu.VMEM((n_col, 8, n_row * rows), f32), pltpu.VMEM((batch, n_row * rows), f32)],
        compiler_params=pltpu.CompilerParams(vmem_limit_bytes=max(24 * mib, tiles * 8 // 3)),
        cost_estimate=pl.CostEstimate(
            flops=2 * tiles * (width + batch), bytes_accessed=4 * tiles, transcendentals=tiles
        ),
        name="scores",
    )(*src_packs, *dst_packs)


def gradient_kernel(n_row, n_col, rows, batch, *refs):
    n = n_row * n_col
    src_packs, refs = refs[:n_row], refs[n_row:]
    dst_packs, refs = refs[:n_col], refs[n_col:]
    prob_ref, refs = refs[0], refs[1:]
    messages, refs = refs[:n_row], refs[n_row:]
    belief_out, src_own, dst_own, next_own, refs = refs[0], refs[1], refs[2], refs[3], refs[4:]
    src_send, refs = refs[: n_row - 1], refs[n_row - 1 :]
    dst_send, refs = refs[: n_col - 1], refs[n_col - 1 :]
    src_all, bel_all, dst_all, grad_all, sems, scale, row_dot, logit_grad, dst_sum, next_sum = refs
    copies = unpack_copies(
        n_row, n_col, rows, batch, n, src_packs, dst_packs, src_all, bel_all, None, dst_all, grad_all, sems
    )
    for copy in copies:
        copy.start()
    head = stat_rows(n_row)
    for r in range(n_row):

        def stat(s, kind):
            at = kind * n_row + (r ^ s)
            return messages[s][at : at + 1]

        tops = [stat(s, 0) for s in range(n_row)]
        top = functools.reduce(jnp.maximum, tops)
        parts = [jnp.exp(one - top) for one in tops]
        total = sum(part * stat(s, 1) for s, part in enumerate(parts))
        dots = sum(part * stat(s, 2) for s, part in enumerate(parts))
        inverse = 1.0 / total
        lanes = slice(r * rows, (r + 1) * rows)
        scale[0:1, lanes] = parts[0] * inverse
        row_dot[0:1, lanes] = dots * inverse
        if r == 0:
            belief_out[...] = sum(
                (part * inverse) * messages[s][head:] for s, part in enumerate(parts)
            ).astype(bf16)
    for copy in copies:
        copy.wait()

    def one_block(t, carried):
        here = block_of(t, rows)
        prob = prob_ref[here] * scale[0:1]
        next_sum[t] = dot(bel_all[...], prob.astype(bf16), NT)
        prob_grad = dot(grad_all[t], bel_all[...], TN)
        change = (prob * (prob_grad - row_dot[0:1])).astype(bf16)
        logit_grad[here] = change
        dst_sum[t] = dot(change, src_all[...], NN)
        return carried

    lax.fori_loop(0, n_col, one_block, 0)
    dst_own[...] = dst_sum[0]
    next_own[...] = next_sum[0]
    for t in range(1, n_col):
        dst_send[t - 1][:rows] = dst_sum[t].astype(bf16)
        dst_send[t - 1][rows:] = next_sum[t].astype(bf16)
    for s in range(n_row):
        src_sum = dot(logit_grad[:, s * rows : (s + 1) * rows], dst_all[...], TN)
        if s == 0:
            src_own[...] = src_sum
        else:
            src_send[s - 1][...] = src_sum.astype(bf16)


def gradients(n_row, n_col, batch, src_packs, dst_packs, prob, messages):
    n = n_row * n_col
    width = src_packs[0].shape[1]
    rows = dst_packs[0].shape[0] - batch
    tiles = n * rows * rows
    shape = jax.ShapeDtypeStruct
    return pl.pallas_call(
        functools.partial(gradient_kernel, n_row, n_col, rows, batch),
        out_shape=(
            shape((batch, rows), bf16),
            shape((rows, width), f32),
            shape((rows, width), f32),
            shape((batch, rows), f32),
        )
        + (shape((rows, width), bf16),) * (n_row - 1)
        + (shape((rows + batch, width), bf16),) * (n_col - 1),
        in_specs=[anywhere()] * (n_row + n_col) + [whole_vmem()] * (1 + n_row),
        out_specs=(whole_vmem(),) * (4 + n_row - 1 + n_col - 1),
        scratch_shapes=unpack_scratch(n_row, n_col, rows, width, batch, n, False)
        + [
            pltpu.VMEM((8, n_row * rows), f32),
            pltpu.VMEM((8, n_row * rows), f32),
            pltpu.VMEM((n_col * rows, n_row * rows), bf16),
            pltpu.VMEM((n_col, rows, width), f32),
            pltpu.VMEM((n_col, batch, rows), f32),
        ],
        compiler_params=pltpu.CompilerParams(vmem_limit_bytes=max(24 * mib, tiles * 3)),
        cost_estimate=pl.CostEstimate(
            flops=4 * tiles * (width + batch), bytes_accessed=8 * tiles, transcendentals=0
        ),
        name="gradients",
    )(*src_packs, *dst_packs, prob, *messages)


def total_kernel(n_row, n_col, *refs):
    src_own, dst_own, next_own, refs = refs[0], refs[1], refs[2], refs[3:]
    src_parts, refs = refs[: n_row - 1], refs[n_row - 1 :]
    dst_parts, refs = refs[: n_col - 1], refs[n_col - 1 :]
    src_out, dst_out, next_out = refs
    rows = src_own.shape[0]
    src_out[...] = src_own[...] + sum(part[...].astype(f32) for part in src_parts)
    dst_out[...] = dst_own[...] + sum(part[:rows].astype(f32) for part in dst_parts)
    next_out[...] = next_own[...] + sum(part[rows:].astype(f32) for part in dst_parts)


def totals(n_row, n_col, src_own, dst_own, next_own, src_parts, dst_parts):
    shape = jax.ShapeDtypeStruct
    return pl.pallas_call(
        functools.partial(total_kernel, n_row, n_col),
        out_shape=tuple(shape(own.shape, f32) for own in (src_own, dst_own, next_own)),
        in_specs=[whole_vmem()] * (3 + n_row - 1 + n_col - 1),
        out_specs=(whole_vmem(),) * 3,
        name="totals",
    )(src_own, dst_own, next_own, *src_parts, *dst_parts)


def per_device(n, src_emb, dst_emb, tile_dst, tile_count, beliefs, grad_next):
    n_row, n_col = grid_of(n)
    batch = beliefs.shape[0]
    me = lax.axis_index("src").astype(jnp.int32).reshape(1)

    def swap(array, flip):
        return lax.ppermute(array, "src", [(i, i ^ flip) for i in range(n)])

    src_pack, dst_pack = pack(n, me, tile_dst, tile_count, src_emb, beliefs, dst_emb, grad_next)
    dst_packs = [dst_pack] + [swap(dst_pack, t * n_row) for t in range(1, n_col)]
    src_packs = [src_pack] + [swap(src_pack, s) for s in range(1, n_row)]
    prob, *messages = scores(n_row, n_col, batch, src_packs, dst_packs)
    messages = messages[:1] + [swap(messages[s], s) for s in range(1, n_row)]
    grad_belief, src_own, dst_own, next_own, *shares = gradients(
        n_row, n_col, batch, src_packs, dst_packs, prob, messages
    )
    dst_parts = [swap(shares[n_row - 1 + t - 1], t * n_row) for t in range(1, n_col)]
    src_parts = [swap(shares[s - 1], s) for s in range(1, n_row)]
    grad_src, grad_dst, next_belief = totals(
        n_row, n_col, src_own, dst_own, next_own, src_parts, dst_parts
    )
    return (next_belief, grad_belief, grad_src, grad_dst)


def solution(mesh):
    placed = (
        P(("groups", "src"), None),
        P(("groups", "src"), None),
        P(("groups", "src"), None),
        P(("groups", "src")),
        P("groups", "src"),
        P("groups", "src"),
    )
    return jax.shard_map(
        functools.partial(per_device, mesh.shape["src"]),
        mesh=mesh,
        in_specs=placed,
        out_specs=(
            P("groups", "src"),
            P("groups", "src"),
            P(("groups", "src"), None),
            P(("groups", "src"), None),
        ),
        check_vma=False,
    )
```

```python
import functools

import jax
import jax.numpy as jnp
from jax import lax
from jax.experimental import pallas as pl
from jax.experimental.pallas import tpu as pltpu
from jax.sharding import PartitionSpec as P

f32 = jnp.float32
bf16 = jnp.bfloat16
unlisted = 1e30
mib = 1 << 20


class Grid:
    def __init__(self, n, rows, width, batch):
        row_bits = (n.bit_length() - 1) // 2
        self.n, self.rows, self.width, self.batch = n, rows, width, batch
        self.row_bits = row_bits
        self.n_row = 1 << row_bits
        self.n_col = n // self.n_row
        self.n_far = self.n_col // 2
        self.span = self.n_row * rows
        self.tall = self.n_col * rows
        self.tiles = self.span * self.tall
        self.head = (3 * self.n_row + 7) // 8 * 8

    def row_flip(self, s):
        return s << 1

    def far_flip(self, f):
        return f << (1 + self.row_bits)

    def col_flip(self, t):
        return (t & 1) | self.far_flip(t >> 1)


def dot(a, b, dims):
    return lax.dot_general(a, b, (dims, ((), ())), preferred_element_type=f32)


NN = ((1,), (0,))
NT = ((1,), (1,))
TN = ((0,), (0,))


def block_of(index, size):
    if isinstance(index, int):
        return pl.ds(index * size, size)
    return pl.ds(pl.multiple_of(index * size, size), size)


def for_each(count, body, carried):
    if count <= 4:
        for index in range(count):
            carried = body(index, carried)
        return carried
    return lax.fori_loop(0, count, body, carried)


def in_vmem():
    return pl.BlockSpec(memory_space=pltpu.VMEM)


def anywhere():
    return pl.BlockSpec(memory_space=pl.ANY)


def in_smem():
    return pl.BlockSpec(memory_space=pltpu.SMEM)


shape = jax.ShapeDtypeStruct


def pack_kernel(g, me_ref, tile_ref, count_ref, src_ref, bel_ref, dst_ref, grad_ref, src_pack, dst_pack, listed_out, flags, listed, sems):
    rows, batch = g.rows, g.batch
    moves = [
        (dst_ref, dst_pack.at[pl.ds(0, rows)]),
        (grad_ref, dst_pack.at[pl.ds(rows, batch)]),
        (src_ref, src_pack.at[pl.ds(0, rows)]),
        (bel_ref, src_pack.at[pl.ds(rows, batch)]),
        (listed, src_pack.at[pl.ds(rows + batch, g.n)]),
        (listed, listed_out),
    ]
    copies = [pltpu.make_async_copy(a, b, sems.at[k]) for k, (a, b) in enumerate(moves)]
    for copy in copies[:4]:
        copy.start()
    me = me_ref[0]
    for k in range(g.n):
        flags[pl.ds(tile_ref[0, k] ^ me, 1), :] = jnp.broadcast_to(
            jnp.where(k < count_ref[0], 1.0, 0.0), (1, g.width)
        ).astype(f32)
    listed[...] = flags[...].astype(bf16)
    for copy in copies[4:]:
        copy.start()
    for copy in copies:
        copy.wait()


def pack(g, me, tile_dst, tile_count, src_emb, beliefs, dst_emb, grad_next):
    return pl.pallas_call(
        functools.partial(pack_kernel, g),
        out_shape=(
            shape((g.rows + g.batch + g.n, g.width), bf16),
            shape((g.rows + g.batch, g.width), bf16),
            shape((g.n, g.width), bf16),
        ),
        in_specs=[in_smem()] * 3 + [anywhere()] * 4,
        out_specs=(anywhere(),) * 3,
        scratch_shapes=[
            pltpu.VMEM((g.n, g.width), f32),
            pltpu.VMEM((g.n, g.width), bf16),
            pltpu.SemaphoreType.DMA((6,)),
        ],
        compiler_params=pltpu.CompilerParams(vmem_limit_bytes=2 * mib),
        name="pack",
    )(me, tile_dst, tile_count, src_emb, beliefs, dst_emb, grad_next)


def score_kernel(g, *refs):
    rows, batch = g.rows, g.batch
    src_own, bel_own, listed_own, dst_own, grad_own, refs = *refs[:5], refs[5:]
    src_packs, refs = refs[: g.n_row - 1], refs[g.n_row - 1 :]
    dst_packs, refs = refs[: g.n_col - 1], refs[g.n_col - 1 :]
    src_all, bel_all, dst_all, grad_all, prob_ref, refs = *refs[:5], refs[5:]
    messages, refs = refs[: g.n_row], refs[g.n_row :]
    listed_all, bias, grad_sum, sems = refs
    moves = []
    for s in range(g.n_row):
        here = pl.ds(s * rows, rows)
        if s == 0:
            parts = (src_own, bel_own, listed_own)
        else:
            one = src_packs[s - 1]
            parts = (one.at[pl.ds(0, rows)], one.at[pl.ds(rows, batch)], one.at[pl.ds(rows + batch, g.n)])
        moves += zip(parts, (src_all.at[here], bel_all.at[:, here], listed_all.at[s]))
    for t in range(g.n_col):
        if t == 0:
            parts = (dst_own, grad_own)
        else:
            one = dst_packs[t - 1]
            parts = (one.at[pl.ds(0, rows)], one.at[pl.ds(rows, batch)])
        moves += zip(parts, (dst_all.at[pl.ds(t * rows, rows)], grad_all.at[t]))
    copies = [pltpu.make_async_copy(a, b, sems.at[k]) for k, (a, b) in enumerate(moves)]
    for copy in copies:
        copy.start()
    for copy in copies:
        copy.wait()
    for s in range(g.n_row):
        listed = (listed_all[s].astype(f32) - 1.0) * unlisted
        for t in range(g.n_col):
            v = g.row_flip(s) ^ g.col_flip(t)
            bias[t, 0:1, s * rows : (s + 1) * rows] = listed[v : v + 1]

    def logits_of(t, top):
        here = block_of(t, rows)
        logits = dot(dst_all[here], src_all[...], NT) + bias[t, 0:1]
        prob_ref[here] = logits
        return jnp.maximum(top, jnp.max(logits.reshape(rows // 8, 8, g.span), axis=0))

    top = for_each(g.n_col, logits_of, jnp.full((8, g.span), -unlisted, f32))
    top = jnp.max(top, axis=0, keepdims=True)
    grad_sum[...] = jnp.zeros_like(grad_sum)

    def exps_of(t, total):
        here = block_of(t, rows)
        prob = jnp.exp(prob_ref[here] - top)
        prob_ref[here] = prob
        grad_sum[...] += dot(grad_all[t], prob.astype(bf16), NN)
        return total + jnp.sum(prob.reshape(rows // 8, 8, g.span), axis=0)

    total = for_each(g.n_col, exps_of, jnp.zeros((8, g.span), f32))
    total = jnp.sum(total, axis=0, keepdims=True)
    row_dot = jnp.sum(bel_all[...].astype(f32) * grad_sum[...], axis=0, keepdims=True)
    for s in range(g.n_row):
        messages[s][: g.head] = jnp.zeros((g.head, rows), f32)
        for u in range(g.n_row):
            lanes = slice(u * rows, (u + 1) * rows)
            for kind, value in enumerate((top, total, row_dot)):
                messages[s][kind * g.n_row + u : kind * g.n_row + u + 1] = value[:, lanes]
        messages[s][g.head :] = grad_sum[:, s * rows : (s + 1) * rows]


def scores(g, own, src_packs, dst_packs):
    message = shape((g.head + g.batch, g.rows), f32)
    n_copies = 3 * g.n_row + 2 * g.n_col
    return pl.pallas_call(
        functools.partial(score_kernel, g),
        out_shape=(
            shape((g.span, g.width), bf16),
            shape((g.batch, g.span), bf16),
            shape((g.tall, g.width), bf16),
            shape((g.n_col, g.batch, g.rows), bf16),
            shape((g.tall, g.span), f32),
        )
        + (message,) * g.n_row,
        in_specs=[anywhere()] * (5 + len(src_packs) + len(dst_packs)),
        out_specs=(in_vmem(),) * (5 + g.n_row),
        scratch_shapes=[
            pltpu.VMEM((g.n_row, g.n, g.rows), bf16),
            pltpu.VMEM((g.n_col, 8, g.span), f32),
            pltpu.VMEM((g.batch, g.span), f32),
            pltpu.SemaphoreType.DMA((n_copies,)),
        ],
        compiler_params=pltpu.CompilerParams(vmem_limit_bytes=g.tiles * 8 + 6 * mib),
        cost_estimate=pl.CostEstimate(
            flops=2 * g.tiles * (g.width + g.batch), bytes_accessed=4 * g.tiles, transcendentals=g.tiles
        ),
        name="scores",
    )(*own, *src_packs, *dst_packs)


def logit_kernel(g, *refs):
    rows, batch = g.rows, g.batch
    src_all, bel_all, grad_all, prob_ref, refs = *refs[:4], refs[4:]
    messages, refs = refs[: g.n_row], refs[g.n_row :]
    belief_out, logit_grad, near_send, own_sum, scale, row_dot = refs
    for r in range(g.n_row):

        def stat(s, kind):
            at = kind * g.n_row + (r ^ s)
            return messages[s][at : at + 1]

        tops = [stat(s, 0) for s in range(g.n_row)]
        top = functools.reduce(jnp.maximum, tops)
        parts = [jnp.exp(one - top) for one in tops]
        total = sum(part * stat(s, 1) for s, part in enumerate(parts))
        dots = sum(part * stat(s, 2) for s, part in enumerate(parts))
        inverse = 1.0 / total
        lanes = slice(r * rows, (r + 1) * rows)
        scale[0:1, lanes] = parts[0] * inverse
        row_dot[0:1, lanes] = dots * inverse
        if r == 0:
            belief_out[...] = sum(
                (part * inverse) * messages[s][g.head :] for s, part in enumerate(parts)
            ).astype(bf16)

    def shares_of(t):
        here = block_of(t, rows)
        prob = prob_ref[here] * scale[0:1]
        prob_grad = dot(grad_all[t], bel_all[...], TN)
        change = (prob * (prob_grad - row_dot[0:1])).astype(bf16)
        logit_grad[here] = change
        return dot(change, src_all[...], NN), dot(bel_all[...], prob.astype(bf16), NT)

    def pair(f, carried):
        dst_part, next_part = shares_of(2 * f + 1)
        near_send[f, :rows] = dst_part.astype(bf16)
        near_send[f, rows:] = next_part.astype(bf16)
        dst_part, next_part = shares_of(2 * f)
        own_sum[f, :rows] = dst_part
        own_sum[f, rows:] = next_part
        return carried

    for_each(g.n_far, pair, 0)


def logit_grads(g, src_all, bel_all, grad_all, prob, messages):
    share = (g.n_far, g.rows + g.batch, g.width)
    return pl.pallas_call(
        functools.partial(logit_kernel, g),
        out_shape=(
            shape((g.batch, g.rows), bf16),
            shape((g.tall, g.span), bf16),
            shape(share, bf16),
            shape(share, f32),
        ),
        in_specs=[in_vmem()] * (4 + g.n_row),
        out_specs=(in_vmem(),) * 4,
        scratch_shapes=[pltpu.VMEM((8, g.span), f32)] * 2,
        compiler_params=pltpu.CompilerParams(vmem_limit_bytes=g.tiles * 8 + 6 * mib),
        cost_estimate=pl.CostEstimate(
            flops=2 * g.tiles * (g.width + 2 * g.batch), bytes_accessed=6 * g.tiles, transcendentals=0
        ),
        name="logit_grads",
    )(src_all, bel_all, grad_all, prob, *messages)


def src_kernel(g, logit_grad, dst_all, src_own, *src_send):
    for s in range(g.n_row):
        total = dot(logit_grad[:, s * g.rows : (s + 1) * g.rows], dst_all[...], TN)
        if s == 0:
            src_own[...] = total
        else:
            src_send[s - 1][...] = total.astype(bf16)


def src_shares(g, logit_grad, dst_all):
    return pl.pallas_call(
        functools.partial(src_kernel, g),
        out_shape=(shape((g.rows, g.width), f32),) + (shape((g.rows, g.width), bf16),) * (g.n_row - 1),
        in_specs=[in_vmem()] * 2,
        out_specs=(in_vmem(),) * g.n_row,
        compiler_params=pltpu.CompilerParams(vmem_limit_bytes=g.tiles * 4 + 4 * mib),
        cost_estimate=pl.CostEstimate(
            flops=2 * g.tiles * g.width, bytes_accessed=3 * g.tiles, transcendentals=0
        ),
        name="src_shares",
    )(logit_grad, dst_all)


def fold_kernel(own_sum, near, *far_send):
    for f, send in enumerate(far_send, 1):
        send[...] = (own_sum[f] + near[f].astype(f32)).astype(bf16)


def fold(g, own_sum, near):
    return pl.pallas_call(
        fold_kernel,
        out_shape=(shape(own_sum.shape[1:], bf16),) * (g.n_far - 1),
        in_specs=[in_vmem()] * 2,
        out_specs=(in_vmem(),) * (g.n_far - 1),
        compiler_params=pltpu.CompilerParams(vmem_limit_bytes=6 * mib),
        name="fold",
    )(own_sum, near)


def total_kernel(g, *refs):
    rows = g.rows
    src_own, own_sum, near, refs = *refs[:3], refs[3:]
    src_parts, refs = refs[: g.n_row - 1], refs[g.n_row - 1 :]
    far_parts, refs = refs[: g.n_far - 1], refs[g.n_far - 1 :]
    src_out, dst_out, next_out = refs
    src_out[...] = src_own[...] + sum(part[...].astype(f32) for part in src_parts)
    total = own_sum[0] + near[0].astype(f32)
    total = total + sum(part[...].astype(f32) for part in far_parts)
    dst_out[...] = total[:rows]
    next_out[...] = total[rows:]


def totals(g, src_own, own_sum, near, src_parts, far_parts):
    return pl.pallas_call(
        functools.partial(total_kernel, g),
        out_shape=(
            shape((g.rows, g.width), f32),
            shape((g.rows, g.width), f32),
            shape((g.batch, g.rows), f32),
        ),
        in_specs=[in_vmem()] * (3 + len(src_parts) + len(far_parts)),
        out_specs=(in_vmem(),) * 3,
        compiler_params=pltpu.CompilerParams(vmem_limit_bytes=8 * mib),
        name="totals",
    )(src_own, own_sum, near, *src_parts, *far_parts)


def per_device(n, src_emb, dst_emb, tile_dst, tile_count, beliefs, grad_next):
    g = Grid(n, *src_emb.shape, beliefs.shape[0])
    me = lax.axis_index("src").astype(jnp.int32).reshape(1)

    def swap(array, flip):
        return lax.ppermute(array, "src", [(i, i ^ flip) for i in range(n)])

    src_pack, dst_pack, listed = pack(
        g, me, tile_dst, tile_count, src_emb, beliefs, dst_emb, grad_next
    )
    far_packs = [swap(dst_pack, g.far_flip(f)) for f in range(1, g.n_far)]
    src_packs = [swap(src_pack, g.row_flip(s)) for s in reversed(range(1, g.n_row))][::-1]
    dst_packs = [swap(dst_pack, 1)]
    for one in far_packs:
        dst_packs += [one, swap(one, 1)]
    own = (src_emb, beliefs, listed, dst_emb, grad_next)
    src_all, bel_all, dst_all, grad_all, prob, *messages = scores(g, own, src_packs, dst_packs)
    messages = messages[:1] + [swap(messages[s], g.row_flip(s)) for s in range(1, g.n_row)]
    grad_belief, logit_grad, near_send, own_sum = logit_grads(
        g, src_all, bel_all, grad_all, prob, messages
    )
    near = swap(near_send, 1)
    src_own, *src_send = src_shares(g, logit_grad, dst_all)
    far_send = fold(g, own_sum, near)
    far_parts = [swap(one, g.far_flip(f)) for f, one in enumerate(far_send, 1)]
    src_parts = [swap(src_send[s - 1], g.row_flip(s)) for s in reversed(range(1, g.n_row))]
    grad_src, grad_dst, next_belief = totals(g, src_own, own_sum, near, src_parts, far_parts)
    return (next_belief, grad_belief, grad_src, grad_dst)


def solution(mesh):
    placed = (
        P(("groups", "src"), None),
        P(("groups", "src"), None),
        P(("groups", "src"), None),
        P(("groups", "src")),
        P("groups", "src"),
        P("groups", "src"),
    )
    return jax.shard_map(
        functools.partial(per_device, mesh.shape["src"]),
        mesh=mesh,
        in_specs=placed,
        out_specs=(
            P("groups", "src"),
            P("groups", "src"),
            P(("groups", "src"), None),
            P(("groups", "src"), None),
        ),
        check_vma=False,
    )
```

```python
import functools

import jax
import jax.numpy as jnp
from jax import lax
from jax.experimental import pallas as pl
from jax.experimental.pallas import tpu as pltpu
from jax.sharding import PartitionSpec as P

f32 = jnp.float32
bf16 = jnp.bfloat16
unlisted = 1e30
mib = 1 << 20


class Grid:
    def __init__(self, n, rows, width, batch):
        row_bits = (n.bit_length() - 1) // 2
        self.n, self.rows, self.width, self.batch = n, rows, width, batch
        self.row_bits = row_bits
        self.n_row = 1 << row_bits
        self.n_col = n // self.n_row
        self.n_far = self.n_col // 2
        self.span = self.n_row * rows
        self.tall = self.n_col * rows
        self.tiles = self.span * self.tall
        self.head = (3 * self.n_row + 7) // 8 * 8

    def place(self, me_ref):
        return (me_ref[0] >> 1) & (self.n_row - 1)

    def row_flip(self, s):
        return s << 1

    def far_flip(self, f):
        return f << (1 + self.row_bits)

    def col_flip(self, t):
        return (t & 1) | self.far_flip(t >> 1)


def dot(a, b, dims):
    return lax.dot_general(a, b, (dims, ((), ())), preferred_element_type=f32)


NN = ((1,), (0,))
NT = ((1,), (1,))
TN = ((0,), (0,))


def block_of(index, size):
    if isinstance(index, int):
        return pl.ds(index * size, size)
    return pl.ds(pl.multiple_of(index * size, size), size)


def for_each(count, body, carried):
    if count <= 4:
        for index in range(count):
            carried = body(index, carried)
        return carried
    return lax.fori_loop(0, count, body, carried)


def in_vmem():
    return pl.BlockSpec(memory_space=pltpu.VMEM)


def anywhere():
    return pl.BlockSpec(memory_space=pl.ANY)


def in_hbm():
    return pl.BlockSpec(memory_space=pltpu.HBM)


def in_smem():
    return pl.BlockSpec(memory_space=pltpu.SMEM)


shape = jax.ShapeDtypeStruct


def pack_kernel(g, me_ref, tile_ref, count_ref, src_ref, bel_ref, dst_ref, grad_ref, src_pack, dst_pack, flags, listed, sems):
    rows, batch = g.rows, g.batch
    moves = [
        (dst_ref, dst_pack.at[pl.ds(0, rows)]),
        (grad_ref, dst_pack.at[pl.ds(rows, batch)]),
        (src_ref, src_pack.at[pl.ds(0, rows)]),
        (bel_ref, src_pack.at[pl.ds(rows, batch)]),
        (listed, src_pack.at[pl.ds(rows + batch, g.n)]),
    ]
    copies = [pltpu.make_async_copy(a, b, sems.at[k]) for k, (a, b) in enumerate(moves)]
    for copy in copies[:4]:
        copy.start()
    me = me_ref[0]
    for k in range(g.n):
        flags[pl.ds(tile_ref[0, k] ^ me, 1), :] = jnp.broadcast_to(
            jnp.where(k < count_ref[0], 1.0, 0.0), (1, g.width)
        ).astype(f32)
    listed[...] = flags[...].astype(bf16)
    for copy in copies[4:]:
        copy.start()
    for copy in copies:
        copy.wait()


def pack(g, me, tile_dst, tile_count, src_emb, beliefs, dst_emb, grad_next):
    return pl.pallas_call(
        functools.partial(pack_kernel, g),
        out_shape=(
            shape((g.rows + g.batch + g.n, g.width), bf16),
            shape((g.rows + g.batch, g.width), bf16),
        ),
        in_specs=[in_smem()] * 3 + [in_hbm()] * 4,
        out_specs=(anywhere(),) * 2,
        scratch_shapes=[
            pltpu.VMEM((g.n, g.width), f32),
            pltpu.VMEM((g.n, g.width), bf16),
            pltpu.SemaphoreType.DMA((5,)),
        ],
        compiler_params=pltpu.CompilerParams(vmem_limit_bytes=60 * mib),
        name="pack",
    )(me, tile_dst, tile_count, src_emb, beliefs, dst_emb, grad_next)


def keep_kernel(src_pack, dst_pack, src_out, dst_out):
    src_out[...] = src_pack[...]
    dst_out[...] = dst_pack[...]


def keep(src_pack, dst_pack):
    return pl.pallas_call(
        keep_kernel,
        out_shape=(shape(src_pack.shape, bf16), shape(dst_pack.shape, bf16)),
        in_specs=[in_vmem()] * 2,
        out_specs=(in_vmem(),) * 2,
        compiler_params=pltpu.CompilerParams(vmem_limit_bytes=2 * mib),
        name="keep",
    )(src_pack, dst_pack)


def score_kernel(g, me_ref, *refs):
    rows, batch = g.rows, g.batch
    src_packs, refs = refs[: g.n_row], refs[g.n_row :]
    dst_packs, refs = refs[: g.n_col], refs[g.n_col :]
    src_all, bel_all, dst_all, grad_all, prob_ref, messages, refs = *refs[:6], refs[6:]
    bias, grad_sum = refs
    for t, one in enumerate(dst_packs):
        dst_all[t * rows : (t + 1) * rows] = one[:rows]
        grad_all[t] = one[rows:]
    for s, one in enumerate(src_packs):
        lanes = slice(s * rows, (s + 1) * rows)
        src_all[lanes] = one[:rows]
        bel_all[:, lanes] = one[rows : rows + batch]
        listed = (one[rows + batch :].astype(f32) - 1.0) * unlisted
        for t in range(g.n_col):
            v = g.row_flip(s) ^ g.col_flip(t)
            bias[t, 0:1, lanes] = listed[v : v + 1]

    def logits_of(t, top):
        here = block_of(t, rows)
        logits = dot(dst_all[here], src_all[...], NT) + bias[t, 0:1]
        prob_ref[here] = logits
        return jnp.maximum(top, jnp.max(logits.reshape(rows // 8, 8, g.span), axis=0))

    top = for_each(g.n_col, logits_of, jnp.full((8, g.span), -unlisted, f32))
    top = jnp.max(top, axis=0, keepdims=True)
    grad_sum[...] = jnp.zeros_like(grad_sum)

    def exps_of(t, total):
        here = block_of(t, rows)
        prob = jnp.exp(prob_ref[here] - top)
        prob_ref[here] = prob
        grad_sum[...] += dot(grad_all[t], prob.astype(bf16), NN)
        return total + jnp.sum(prob.reshape(rows // 8, 8, g.span), axis=0)

    total = for_each(g.n_col, exps_of, jnp.zeros((8, g.span), f32))
    total = jnp.sum(total, axis=0, keepdims=True)
    row_dot = jnp.sum(bel_all[...].astype(f32) * grad_sum[...], axis=0, keepdims=True)
    place = g.place(me_ref)
    stats = [jnp.zeros((g.head - 3 * g.n_row, rows), f32)] if g.head > 3 * g.n_row else []
    for s in range(g.n_row):
        parts = [value[:, u * rows : (u + 1) * rows] for value in (top, total, row_dot) for u in range(g.n_row)]
        messages[place ^ s, : g.head] = jnp.concatenate(parts + stats, axis=0)
        messages[place ^ s, g.head :] = grad_sum[:, s * rows : (s + 1) * rows]


def scores(g, me, src_packs, dst_packs):
    return pl.pallas_call(
        functools.partial(score_kernel, g),
        out_shape=(
            shape((g.span, g.width), bf16),
            shape((g.batch, g.span), bf16),
            shape((g.tall, g.width), bf16),
            shape((g.n_col, g.batch, g.rows), bf16),
            shape((g.tall, g.span), f32),
            shape((g.n_row, g.head + g.batch, g.rows), f32),
        ),
        in_specs=[in_smem()] + [in_vmem()] * (len(src_packs) + len(dst_packs)),
        out_specs=(in_vmem(),) * 6,
        scratch_shapes=[
            pltpu.VMEM((g.n_col, 8, g.span), f32),
            pltpu.VMEM((g.batch, g.span), f32),
        ],
        compiler_params=pltpu.CompilerParams(vmem_limit_bytes=g.tiles * 8 + 6 * mib),
        cost_estimate=pl.CostEstimate(
            flops=2 * g.tiles * (g.width + g.batch), bytes_accessed=4 * g.tiles, transcendentals=g.tiles
        ),
        name="scores",
    )(me, *src_packs, *dst_packs)


def logit_kernel(
    g, me_ref, src_all, bel_all, grad_all, prob_ref, messages, belief_out, logit_grad, near_send, own_sum, scale, row_dot
):
    rows = g.rows
    place = g.place(me_ref)
    for r in range(g.n_row):

        def stat(s, kind):
            at = kind * g.n_row + (r ^ s)
            return messages[place ^ s, at : at + 1]

        tops = [stat(s, 0) for s in range(g.n_row)]
        top = functools.reduce(jnp.maximum, tops)
        parts = [jnp.exp(one - top) for one in tops]
        total = sum(part * stat(s, 1) for s, part in enumerate(parts))
        dots = sum(part * stat(s, 2) for s, part in enumerate(parts))
        inverse = 1.0 / total
        lanes = slice(r * rows, (r + 1) * rows)
        scale[0:1, lanes] = parts[0] * inverse
        row_dot[0:1, lanes] = dots * inverse
        if r == 0:
            belief_out[...] = sum(
                (part * inverse) * messages[place ^ s, g.head :] for s, part in enumerate(parts)
            ).astype(bf16)

    def shares_of(t):
        here = block_of(t, rows)
        prob = prob_ref[here] * scale[0:1]
        prob_grad = dot(grad_all[t], bel_all[...], TN)
        change = (prob * (prob_grad - row_dot[0:1])).astype(bf16)
        logit_grad[here] = change
        return dot(change, src_all[...], NN), dot(bel_all[...], prob.astype(bf16), NT)

    def pair(f, carried):
        dst_part, next_part = shares_of(2 * f + 1)
        near_send[f, :rows] = dst_part.astype(bf16)
        near_send[f, rows:] = next_part.astype(bf16)
        dst_part, next_part = shares_of(2 * f)
        own_sum[f, :rows] = dst_part
        own_sum[f, rows:] = next_part
        return carried

    for_each(g.n_far, pair, 0)


def logit_grads(g, me, src_all, bel_all, grad_all, prob, messages):
    share = (g.n_far, g.rows + g.batch, g.width)
    return pl.pallas_call(
        functools.partial(logit_kernel, g),
        out_shape=(
            shape((g.batch, g.rows), bf16),
            shape((g.tall, g.span), bf16),
            shape(share, bf16),
            shape(share, f32),
        ),
        in_specs=[in_smem()] + [in_vmem()] * 5,
        out_specs=(in_vmem(),) * 4,
        scratch_shapes=[pltpu.VMEM((8, g.span), f32)] * 2,
        compiler_params=pltpu.CompilerParams(vmem_limit_bytes=g.tiles * 8 + 6 * mib),
        cost_estimate=pl.CostEstimate(
            flops=2 * g.tiles * (g.width + 2 * g.batch), bytes_accessed=6 * g.tiles, transcendentals=0
        ),
        name="logit_grads",
    )(me, src_all, bel_all, grad_all, prob, messages)


def src_kernel(g, me_ref, logit_grad, dst_all, src_own, src_send):
    place = g.place(me_ref)
    for s in range(g.n_row):
        total = dot(logit_grad[:, s * g.rows : (s + 1) * g.rows], dst_all[...], TN)
        if s == 0:
            src_own[...] = total
            src_send[place] = jnp.zeros(total.shape, bf16)
        else:
            src_send[place ^ s] = total.astype(bf16)


def src_shares(g, me, logit_grad, dst_all):
    return pl.pallas_call(
        functools.partial(src_kernel, g),
        out_shape=(
            shape((g.rows, g.width), f32),
            shape((g.n_row, g.rows, g.width), bf16),
        ),
        in_specs=[in_smem()] + [in_vmem()] * 2,
        out_specs=(in_vmem(),) * 2,
        compiler_params=pltpu.CompilerParams(vmem_limit_bytes=g.tiles * 4 + 4 * mib),
        cost_estimate=pl.CostEstimate(
            flops=2 * g.tiles * g.width, bytes_accessed=3 * g.tiles, transcendentals=0
        ),
        name="src_shares",
    )(me, logit_grad, dst_all)


def fold_kernel(own_sum, near, *far_send):
    for f, send in enumerate(far_send, 1):
        send[...] = (own_sum[f] + near[f].astype(f32)).astype(bf16)


def fold(g, own_sum, near):
    return pl.pallas_call(
        fold_kernel,
        out_shape=(shape(own_sum.shape[1:], bf16),) * (g.n_far - 1),
        in_specs=[in_vmem()] * 2,
        out_specs=(in_vmem(),) * (g.n_far - 1),
        compiler_params=pltpu.CompilerParams(vmem_limit_bytes=6 * mib),
        name="fold",
    )(own_sum, near)


def total_kernel(g, *refs):
    rows = g.rows
    src_own, own_sum, near, src_parts, refs = *refs[:4], refs[4:]
    far_parts, refs = refs[: g.n_far - 1], refs[g.n_far - 1 :]
    src_out, dst_out, next_out = refs
    src_out[...] = src_own[...] + sum(src_parts[p].astype(f32) for p in range(g.n_row))
    total = own_sum[0] + near[0].astype(f32)
    total = total + sum(part[...].astype(f32) for part in far_parts)
    dst_out[...] = total[:rows]
    next_out[...] = total[rows:]


def totals(g, src_own, own_sum, near, src_parts, far_parts):
    return pl.pallas_call(
        functools.partial(total_kernel, g),
        out_shape=(
            shape((g.rows, g.width), f32),
            shape((g.rows, g.width), f32),
            shape((g.batch, g.rows), f32),
        ),
        in_specs=[in_vmem()] * (4 + len(far_parts)),
        out_specs=(in_vmem(),) * 3,
        compiler_params=pltpu.CompilerParams(vmem_limit_bytes=8 * mib),
        name="totals",
    )(src_own, own_sum, near, src_parts, *far_parts)


def per_device(n, src_emb, dst_emb, tile_dst, tile_count, beliefs, grad_next):
    g = Grid(n, *src_emb.shape, beliefs.shape[0])
    me = lax.axis_index("src").astype(jnp.int32).reshape(1)

    def swap(array, flip):
        return lax.ppermute(array, "src", [(i, i ^ flip) for i in range(n)])

    row_groups = [[i ^ g.row_flip(s) for s in range(g.n_row)] for i in range(n) if not (i >> 1) & (g.n_row - 1)]

    def exchange(blocks):
        return lax.all_to_all(blocks, "src", 0, 0, axis_index_groups=row_groups)

    src_pack, dst_pack = pack(
        g, me, tile_dst, tile_count, src_emb, beliefs, dst_emb, grad_next
    )
    far_packs = [swap(dst_pack, g.far_flip(f)) for f in range(1, g.n_far)]
    src_packs = [swap(src_pack, g.row_flip(s)) for s in reversed(range(1, g.n_row))]
    src_kept, dst_kept = keep(src_pack, dst_pack)
    src_packs = [src_kept] + src_packs[::-1]
    dst_packs = [dst_kept, swap(dst_pack, 1)]
    for one in far_packs:
        dst_packs += [one, swap(one, 1)]
    src_all, bel_all, dst_all, grad_all, prob, messages = scores(g, me, src_packs, dst_packs)
    messages = exchange(messages)
    grad_belief, logit_grad, near_send, own_sum = logit_grads(
        g, me, src_all, bel_all, grad_all, prob, messages
    )
    near = swap(near_send, 1)
    src_own, src_send = src_shares(g, me, logit_grad, dst_all)
    far_send = fold(g, own_sum, near)
    far_parts = [swap(one, g.far_flip(f)) for f, one in enumerate(far_send, 1)]
    src_parts = exchange(src_send)
    grad_src, grad_dst, next_belief = totals(g, src_own, own_sum, near, src_parts, far_parts)
    return (next_belief, grad_belief, grad_src, grad_dst)


def solution(mesh):
    placed = (
        P(("groups", "src"), None),
        P(("groups", "src"), None),
        P(("groups", "src"), None),
        P(("groups", "src")),
        P("groups", "src"),
        P("groups", "src"),
    )
    return jax.shard_map(
        functools.partial(per_device, mesh.shape["src"]),
        mesh=mesh,
        in_specs=placed,
        out_specs=(
            P("groups", "src"),
            P("groups", "src"),
            P(("groups", "src"), None),
            P(("groups", "src"), None),
        ),
        check_vma=False,
    )
```

```python
import functools

import jax
import jax.numpy as jnp
from jax import lax
from jax.experimental import pallas as pl
from jax.experimental.pallas import tpu as pltpu
from jax.sharding import PartitionSpec as P

f32 = jnp.float32
bf16 = jnp.bfloat16
unlisted = 1e30
mib = 1 << 20


class Grid:
    def __init__(self, n, rows, width, batch):
        row_bits = (n.bit_length() - 1) // 2
        self.n, self.rows, self.width, self.batch = n, rows, width, batch
        self.row_bits = row_bits
        self.n_row = 1 << row_bits
        self.n_col = n // self.n_row
        self.n_far = self.n_col // 2
        self.span = self.n_row * rows
        self.tall = self.n_col * rows
        self.tiles = self.span * self.tall
        self.head = (3 * self.n_row + 7) // 8 * 8

    def row_flip(self, s):
        return s << 1

    def far_flip(self, f):
        return f << (1 + self.row_bits)

    def col_flip(self, t):
        return (t & 1) | self.far_flip(t >> 1)


def dot(a, b, dims):
    return lax.dot_general(a, b, (dims, ((), ())), preferred_element_type=f32)


NN = ((1,), (0,))
NT = ((1,), (1,))
TN = ((0,), (0,))


def block_of(index, size):
    if isinstance(index, int):
        return pl.ds(index * size, size)
    return pl.ds(pl.multiple_of(index * size, size), size)


def for_each(count, body, carried):
    if count <= 4:
        for index in range(count):
            carried = body(index, carried)
        return carried
    return lax.fori_loop(0, count, body, carried)


def in_vmem():
    return pl.BlockSpec(memory_space=pltpu.VMEM)


def anywhere():
    return pl.BlockSpec(memory_space=pl.ANY)


def in_smem():
    return pl.BlockSpec(memory_space=pltpu.SMEM)


shape = jax.ShapeDtypeStruct


def pack_kernel(g, me_ref, tile_ref, count_ref, src_ref, bel_ref, dst_ref, grad_ref, src_pack, dst_pack, flags):
    rows, batch = g.rows, g.batch
    me = me_ref[0]
    for k in range(g.n):
        flags[pl.ds(tile_ref[0, k] ^ me, 1), :] = jnp.broadcast_to(
            jnp.where(k < count_ref[0], 1.0, 0.0), (1, g.width)
        ).astype(f32)
    src_pack[:rows] = src_ref[...]
    src_pack[rows : rows + batch] = bel_ref[...]
    src_pack[rows + batch :] = flags[...].astype(bf16)
    dst_pack[:rows] = dst_ref[...]
    dst_pack[rows:] = grad_ref[...]


def pack(g, me, tile_dst, tile_count, src_emb, beliefs, dst_emb, grad_next):
    return pl.pallas_call(
        functools.partial(pack_kernel, g),
        out_shape=(
            shape((g.rows + g.batch + g.n, g.width), bf16),
            shape((g.rows + g.batch, g.width), bf16),
        ),
        in_specs=[in_smem()] * 3 + [in_vmem()] * 4,
        out_specs=(in_vmem(),) * 2,
        scratch_shapes=[pltpu.VMEM((g.n, g.width), f32)],
        compiler_params=pltpu.CompilerParams(vmem_limit_bytes=60 * mib),
        name="pack",
    )(me, tile_dst, tile_count, src_emb, beliefs, dst_emb, grad_next)


def keep_kernel(src_pack, dst_pack, src_out, dst_out):
    src_out[...] = src_pack[...]
    dst_out[...] = dst_pack[...]


def keep(src_pack, dst_pack):
    return pl.pallas_call(
        keep_kernel,
        out_shape=(shape(src_pack.shape, bf16), shape(dst_pack.shape, bf16)),
        in_specs=[in_vmem()] * 2,
        out_specs=(in_vmem(),) * 2,
        compiler_params=pltpu.CompilerParams(vmem_limit_bytes=2 * mib),
        name="keep",
    )(src_pack, dst_pack)


def score_kernel(g, *refs):
    rows, batch = g.rows, g.batch
    src_packs, refs = refs[: g.n_row], refs[g.n_row :]
    dst_packs, refs = refs[: g.n_col], refs[g.n_col :]
    src_all, bel_all, dst_all, grad_all, prob_ref, grad_sum, stats, bias = refs
    for t, one in enumerate(dst_packs):
        dst_all[t * rows : (t + 1) * rows] = one[:rows]
        grad_all[t] = one[rows:]
    for s, one in enumerate(src_packs):
        lanes = slice(s * rows, (s + 1) * rows)
        src_all[lanes] = one[:rows]
        bel_all[:, lanes] = one[rows : rows + batch]
        listed = (one[rows + batch :].astype(f32) - 1.0) * unlisted
        for t in range(g.n_col):
            v = g.row_flip(s) ^ g.col_flip(t)
            bias[t, 0:1, lanes] = listed[v : v + 1]

    def logits_of(t, top):
        here = block_of(t, rows)
        logits = dot(dst_all[here], src_all[...], NT) + bias[t, 0:1]
        prob_ref[here] = logits
        return jnp.maximum(top, jnp.max(logits.reshape(rows // 8, 8, g.span), axis=0))

    top = for_each(g.n_col, logits_of, jnp.full((8, g.span), -unlisted, f32))
    top = jnp.max(top, axis=0, keepdims=True)
    grad_sum[...] = jnp.zeros_like(grad_sum)

    def exps_of(t, total):
        here = block_of(t, rows)
        prob = jnp.exp(prob_ref[here] - top)
        prob_ref[here] = prob
        grad_sum[...] += dot(grad_all[t], prob.astype(bf16), NN)
        return total + jnp.sum(prob.reshape(rows // 8, 8, g.span), axis=0)

    total = for_each(g.n_col, exps_of, jnp.zeros((8, g.span), f32))
    total = jnp.sum(total, axis=0, keepdims=True)
    row_dot = jnp.sum(bel_all[...].astype(f32) * grad_sum[...], axis=0, keepdims=True)
    for kind, value in enumerate((top, total, row_dot)):
        for u in range(g.n_row):
            at = kind * g.n_row + u
            stats[at : at + 1] = value[:, u * rows : (u + 1) * rows]
    if g.head > 3 * g.n_row:
        stats[3 * g.n_row :] = jnp.zeros((g.head - 3 * g.n_row, rows), f32)


def scores(g, src_packs, dst_packs):
    return pl.pallas_call(
        functools.partial(score_kernel, g),
        out_shape=(
            shape((g.span, g.width), bf16),
            shape((g.batch, g.span), bf16),
            shape((g.tall, g.width), bf16),
            shape((g.n_col, g.batch, g.rows), bf16),
            shape((g.tall, g.span), f32),
            shape((g.batch, g.span), f32),
            shape((g.head, g.rows), f32),
        ),
        in_specs=[in_vmem()] * (len(src_packs) + len(dst_packs)),
        out_specs=(in_vmem(),) * 7,
        scratch_shapes=[
            pltpu.VMEM((g.n_col, 8, g.span), f32),
        ],
        compiler_params=pltpu.CompilerParams(vmem_limit_bytes=g.tiles * 8 + 6 * mib),
        cost_estimate=pl.CostEstimate(
            flops=2 * g.tiles * (g.width + g.batch), bytes_accessed=4 * g.tiles, transcendentals=g.tiles
        ),
        name="scores",
    )(*src_packs, *dst_packs)


def logit_kernel(g, *refs):
    rows = g.rows
    src_all, bel_all, grad_all, prob_ref, grad_sum, refs = *refs[:5], refs[5:]
    stats, refs = refs[: g.n_row], refs[g.n_row :]
    logit_grad, belief_sum, near_send, own_sum, scale, row_dot = refs
    for r in range(g.n_row):

        def stat(s, kind):
            at = kind * g.n_row + (r ^ s)
            return stats[s][at : at + 1]

        tops = [stat(s, 0) for s in range(g.n_row)]
        top = functools.reduce(jnp.maximum, tops)
        parts = [jnp.exp(one - top) for one in tops]
        total = sum(part * stat(s, 1) for s, part in enumerate(parts))
        dots = sum(part * stat(s, 2) for s, part in enumerate(parts))
        inverse = 1.0 / total
        lanes = slice(r * rows, (r + 1) * rows)
        scale[0:1, lanes] = parts[0] * inverse
        row_dot[0:1, lanes] = dots * inverse
    belief_sum[...] = grad_sum[...] * scale[0:1]

    def shares_of(t):
        here = block_of(t, rows)
        prob = prob_ref[here] * scale[0:1]
        prob_grad = dot(grad_all[t], bel_all[...], TN)
        change = (prob * (prob_grad - row_dot[0:1])).astype(bf16)
        logit_grad[here] = change
        return dot(change, src_all[...], NN), dot(bel_all[...], prob.astype(bf16), NT)

    def pair(f, carried):
        dst_part, next_part = shares_of(2 * f + 1)
        near_send[f, :rows] = dst_part.astype(bf16)
        near_send[f, rows:] = next_part.astype(bf16)
        dst_part, next_part = shares_of(2 * f)
        own_sum[f, :rows] = dst_part
        own_sum[f, rows:] = next_part
        return carried

    for_each(g.n_far, pair, 0)


def logit_grads(g, src_all, bel_all, grad_all, prob, grad_sum, stats):
    share = (g.n_far, g.rows + g.batch, g.width)
    return pl.pallas_call(
        functools.partial(logit_kernel, g),
        out_shape=(
            shape((g.tall, g.span), bf16),
            shape((g.batch, g.span), f32),
            shape(share, bf16),
            shape(share, f32),
        ),
        in_specs=[in_vmem()] * (5 + g.n_row),
        out_specs=(in_vmem(),) * 4,
        scratch_shapes=[pltpu.VMEM((8, g.span), f32)] * 2,
        compiler_params=pltpu.CompilerParams(vmem_limit_bytes=g.tiles * 8 + 6 * mib),
        cost_estimate=pl.CostEstimate(
            flops=2 * g.tiles * (g.width + 2 * g.batch), bytes_accessed=6 * g.tiles, transcendentals=0
        ),
        name="logit_grads",
    )(src_all, bel_all, grad_all, prob, grad_sum, *stats)


def src_kernel(g, logit_grad, belief_sum, dst_all, own_sum, side_send, cross_send):
    for s in range(g.n_row):
        lanes = slice(s * g.rows, (s + 1) * g.rows)
        total = dot(logit_grad[:, lanes], dst_all[...], TN)
        if s % 2 == 0:
            own_sum[s // 2, : g.rows] = total
            own_sum[s // 2, g.rows :] = belief_sum[:, lanes]
            continue
        send = side_send if s == 1 else cross_send.at[s // 2 - 1]
        send[: g.rows] = total.astype(bf16)
        send[g.rows :] = belief_sum[:, lanes].astype(bf16)


def src_shares(g, logit_grad, belief_sum, dst_all):
    share = (g.rows + g.batch, g.width)
    return pl.pallas_call(
        functools.partial(src_kernel, g),
        out_shape=(
            shape((g.n_row // 2,) + share, f32),
            shape(share, bf16),
            shape((g.n_row // 2 - 1,) + share, bf16),
        ),
        in_specs=[in_vmem()] * 3,
        out_specs=(in_vmem(),) * 3,
        compiler_params=pltpu.CompilerParams(vmem_limit_bytes=g.tiles * 4 + 4 * mib),
        cost_estimate=pl.CostEstimate(
            flops=2 * g.tiles * g.width, bytes_accessed=3 * g.tiles, transcendentals=0
        ),
        name="src_shares",
    )(logit_grad, belief_sum, dst_all)


def fold_kernel(first, own_sum, near, after, *sends):
    for f, send in enumerate(sends, 1):
        send[...] = (own_sum[f] + near[f - first].astype(f32)).astype(bf16)


def fold(first, own_sum, near, after):
    n_send = own_sum.shape[0] - 1
    return pl.pallas_call(
        functools.partial(fold_kernel, first),
        out_shape=(shape(own_sum.shape[1:], bf16),) * n_send,
        in_specs=[in_vmem()] * 2 + [anywhere()],
        out_specs=(in_vmem(),) * n_send,
        compiler_params=pltpu.CompilerParams(vmem_limit_bytes=6 * mib),
        name="fold",
    )(own_sum, near, after)


def total_kernel(g, *refs):
    src_sum, side, dst_sum, near, refs = *refs[:4], refs[4:]
    src_parts, refs = refs[: g.n_row // 2 - 1], refs[g.n_row // 2 - 1 :]
    dst_parts, refs = refs[: g.n_far - 1], refs[g.n_far - 1 :]
    src_out, belief_out, dst_out, next_out = refs

    def added(out, rows):
        total = src_sum[0, rows] + side[rows].astype(f32)
        out[...] = (total + sum(part[rows].astype(f32) for part in src_parts)).astype(out.dtype)

    def added_dst(out, rows):
        total = dst_sum[0, rows] + near[0, rows].astype(f32)
        out[...] = total + sum(part[rows].astype(f32) for part in dst_parts)

    added(src_out, slice(0, g.rows))
    added(belief_out, slice(g.rows, g.rows + g.batch))
    added_dst(dst_out, slice(0, g.rows))
    added_dst(next_out, slice(g.rows, g.rows + g.batch))


def totals(g, src_sum, side, dst_sum, near, src_parts, dst_parts):
    return pl.pallas_call(
        functools.partial(total_kernel, g),
        out_shape=(
            shape((g.rows, g.width), f32),
            shape((g.batch, g.rows), bf16),
            shape((g.rows, g.width), f32),
            shape((g.batch, g.rows), f32),
        ),
        in_specs=[in_vmem()] * (4 + len(src_parts) + len(dst_parts)),
        out_specs=(in_vmem(),) * 4,
        compiler_params=pltpu.CompilerParams(vmem_limit_bytes=8 * mib),
        name="totals",
    )(src_sum, side, dst_sum, near, *src_parts, *dst_parts)


def per_device(n, src_emb, dst_emb, tile_dst, tile_count, beliefs, grad_next):
    g = Grid(n, *src_emb.shape, beliefs.shape[0])
    me = lax.axis_index("src").astype(jnp.int32).reshape(1)

    def swap(array, flip):
        return lax.ppermute(array, "src", [(i, i ^ flip) for i in range(n)])

    src_pack, dst_pack = pack(g, me, tile_dst, tile_count, src_emb, beliefs, dst_emb, grad_next)
    src_far = [swap(src_pack, g.row_flip(s)) for s in range(2, g.n_row, 2)]
    dst_far = [swap(dst_pack, g.far_flip(f)) for f in range(1, g.n_far)]
    src_side = swap(src_pack, g.row_flip(1))
    dst_near = swap(dst_pack, 1)
    src_kept, dst_kept = keep(src_pack, dst_pack)
    src_packs, dst_packs = [src_kept, src_side], [dst_kept, dst_near]
    for one in src_far:
        src_packs += [one, swap(one, g.row_flip(1))]
    for one in dst_far:
        dst_packs += [one, swap(one, 1)]
    src_all, bel_all, dst_all, grad_all, prob, grad_sum, stats = scores(g, src_packs, dst_packs)
    all_stats = [stats] + [swap(stats, g.row_flip(s)) for s in range(1, g.n_row)]
    logit_grad, belief_sum, near_send, dst_sum = logit_grads(
        g, src_all, bel_all, grad_all, prob, grad_sum, all_stats
    )
    near = swap(near_send, 1)
    src_sum, side_send, cross_send = src_shares(g, logit_grad, belief_sum, dst_all)
    cross = swap(cross_send, g.row_flip(1))
    dst_folded = fold(0, dst_sum, near, src_sum)
    dst_parts = [swap(one, g.far_flip(f)) for f, one in enumerate(dst_folded, 1)]
    side = swap(side_send, g.row_flip(1))
    src_folded = fold(1, src_sum, cross, dst_folded[0])
    src_parts = [swap(one, g.row_flip(2 * f)) for f, one in enumerate(src_folded, 1)]
    grad_src, grad_belief, grad_dst, next_belief = totals(
        g, src_sum, side, dst_sum, near, src_parts, dst_parts
    )
    return (next_belief, grad_belief, grad_src, grad_dst)


def solution(mesh):
    placed = (
        P(("groups", "src"), None),
        P(("groups", "src"), None),
        P(("groups", "src"), None),
        P(("groups", "src")),
        P("groups", "src"),
        P("groups", "src"),
    )
    return jax.shard_map(
        functools.partial(per_device, mesh.shape["src"]),
        mesh=mesh,
        in_specs=placed,
        out_specs=(
            P("groups", "src"),
            P("groups", "src"),
            P(("groups", "src"), None),
            P(("groups", "src"), None),
        ),
        check_vma=False,
    )
```

```python
import functools

import jax
import jax.numpy as jnp
from jax import lax
from jax.experimental import pallas as pl
from jax.experimental.pallas import tpu as pltpu
from jax.sharding import PartitionSpec as P

f32 = jnp.float32
bf16 = jnp.bfloat16
unlisted = 1e30
mib = 1 << 20


class Grid:
    def __init__(self, n, rows, width, batch):
        row_bits = (n.bit_length() - 1) // 2
        self.n, self.rows, self.width, self.batch = n, rows, width, batch
        self.row_bits = row_bits
        self.n_row = 1 << row_bits
        self.n_col = n // self.n_row
        self.n_far = self.n_col // 2
        self.span = self.n_row * rows
        self.tall = self.n_col * rows
        self.tiles = self.span * self.tall
        self.head = (3 * self.n_row + 7) // 8 * 8

    def row_flip(self, s):
        return s << 1

    def far_flip(self, f):
        return f << (1 + self.row_bits)

    def col_flip(self, t):
        return (t & 1) | self.far_flip(t >> 1)


def dot(a, b, dims):
    return lax.dot_general(a, b, (dims, ((), ())), preferred_element_type=f32)


NN = ((1,), (0,))
NT = ((1,), (1,))
TN = ((0,), (0,))


def block_of(index, size):
    if isinstance(index, int):
        return pl.ds(index * size, size)
    return pl.ds(pl.multiple_of(index * size, size), size)


def for_each(count, body, carried):
    if count <= 4:
        for index in range(count):
            carried = body(index, carried)
        return carried
    return lax.fori_loop(0, count, body, carried)


def in_vmem():
    return pl.BlockSpec(memory_space=pltpu.VMEM)


def anywhere():
    return pl.BlockSpec(memory_space=pl.ANY)


def in_smem():
    return pl.BlockSpec(memory_space=pltpu.SMEM)


shape = jax.ShapeDtypeStruct


def pack_kernel(g, me_ref, tile_ref, count_ref, src_ref, bel_ref, dst_ref, grad_ref, src_pack, dst_pack, flags):
    rows, batch = g.rows, g.batch
    me = me_ref[0]
    for k in range(g.n):
        flags[pl.ds(tile_ref[0, k] ^ me, 1), :] = jnp.broadcast_to(
            jnp.where(k < count_ref[0], 1.0, 0.0), (1, g.width)
        ).astype(f32)
    src_pack[:rows] = src_ref[...]
    src_pack[rows : rows + batch] = bel_ref[...]
    src_pack[rows + batch :] = flags[...].astype(bf16)
    dst_pack[:rows] = dst_ref[...]
    dst_pack[rows:] = grad_ref[...]


def pack(g, me, tile_dst, tile_count, src_emb, beliefs, dst_emb, grad_next):
    return pl.pallas_call(
        functools.partial(pack_kernel, g),
        out_shape=(
            shape((g.rows + g.batch + g.n, g.width), bf16),
            shape((g.rows + g.batch, g.width), bf16),
        ),
        in_specs=[in_smem()] * 3 + [in_vmem()] * 4,
        out_specs=(in_vmem(),) * 2,
        scratch_shapes=[pltpu.VMEM((g.n, g.width), f32)],
        compiler_params=pltpu.CompilerParams(vmem_limit_bytes=60 * mib),
        name="pack",
    )(me, tile_dst, tile_count, src_emb, beliefs, dst_emb, grad_next)


def keep_kernel(src_pack, dst_pack, src_out, dst_out):
    src_out[...] = src_pack[...]
    dst_out[...] = dst_pack[...]


def keep(src_pack, dst_pack):
    return pl.pallas_call(
        keep_kernel,
        out_shape=(shape(src_pack.shape, bf16), shape(dst_pack.shape, bf16)),
        in_specs=[in_vmem()] * 2,
        out_specs=(in_vmem(),) * 2,
        compiler_params=pltpu.CompilerParams(vmem_limit_bytes=2 * mib),
        name="keep",
    )(src_pack, dst_pack)


def hand_kernel(one, after, out):
    out[...] = one[...]


def hand(one, after):
    return pl.pallas_call(
        hand_kernel,
        out_shape=shape(one.shape, one.dtype),
        in_specs=[in_vmem(), anywhere()],
        out_specs=in_vmem(),
        compiler_params=pltpu.CompilerParams(vmem_limit_bytes=mib),
        name="hand",
    )(one, after)


def score_kernel(g, s, src_pack, *refs):
    rows, batch = g.rows, g.batch
    dst_packs, refs = refs[: g.n_col], refs[g.n_col :]
    prob_ref, grad_sum, stats = refs
    listed = (src_pack[rows + batch :].astype(f32) - 1.0) * unlisted
    top = jnp.full((8, rows), -unlisted, f32)
    for t in range(g.n_col):
        v = g.row_flip(s) ^ g.col_flip(t)
        logits = dot(dst_packs[t][:rows], src_pack[:rows], NT) + listed[v : v + 1]
        prob_ref[t * rows : (t + 1) * rows] = logits
        top = jnp.maximum(top, jnp.max(logits.reshape(rows // 8, 8, rows), axis=0))
    top = jnp.max(top, axis=0, keepdims=True)
    total = jnp.zeros((8, rows), f32)
    grads = jnp.zeros((batch, rows), f32)
    for t in range(g.n_col):
        here = slice(t * rows, (t + 1) * rows)
        prob = jnp.exp(prob_ref[here] - top)
        prob_ref[here] = prob
        grads = grads + dot(dst_packs[t][rows:], prob.astype(bf16), NN)
        total = total + jnp.sum(prob.reshape(rows // 8, 8, rows), axis=0)
    grad_sum[...] = grads
    stats[0:1] = top
    stats[1:2] = jnp.sum(total, axis=0, keepdims=True)
    stats[2:3] = jnp.sum(src_pack[rows : rows + batch].astype(f32) * grads, axis=0, keepdims=True)


def scores(g, s, src_pack, dst_packs):
    tiles = g.tall * g.rows
    return pl.pallas_call(
        functools.partial(score_kernel, g, s),
        out_shape=(
            shape((g.tall, g.rows), f32),
            shape((g.batch, g.rows), f32),
            shape((3, g.rows), f32),
        ),
        in_specs=[in_vmem()] * (1 + g.n_col),
        out_specs=(in_vmem(),) * 3,
        compiler_params=pltpu.CompilerParams(vmem_limit_bytes=tiles * 8 + 4 * mib),
        cost_estimate=pl.CostEstimate(
            flops=2 * tiles * (g.width + g.batch), bytes_accessed=4 * tiles, transcendentals=tiles
        ),
        name="scores",
    )(src_pack, *dst_packs)


def join_kernel(g, *refs):
    stats, out = refs[:-1], refs[-1]
    for s, one in enumerate(stats):
        for kind in range(3):
            at = kind * g.n_row + s
            out[at : at + 1] = one[kind : kind + 1]
    if g.head > 3 * g.n_row:
        out[3 * g.n_row :] = jnp.zeros((g.head - 3 * g.n_row, g.rows), f32)


def join(g, stats):
    return pl.pallas_call(
        functools.partial(join_kernel, g),
        out_shape=shape((g.head, g.rows), f32),
        in_specs=[in_vmem()] * g.n_row,
        out_specs=in_vmem(),
        compiler_params=pltpu.CompilerParams(vmem_limit_bytes=mib),
        name="join",
    )(*stats)


def stage_kernel(g, *refs):
    rows, batch = g.rows, g.batch
    src_packs, refs = refs[: g.n_row], refs[g.n_row :]
    dst_packs, refs = refs[: g.n_col], refs[g.n_col :]
    src_all, bel_all, dst_all, prob_grad = refs
    for t, one in enumerate(dst_packs):
        dst_all[t * rows : (t + 1) * rows] = one[:rows]
    for s, one in enumerate(src_packs):
        lanes = slice(s * rows, (s + 1) * rows)
        src_all[lanes] = one[:rows]
        bel_all[:, lanes] = one[rows : rows + batch]
    for t, one in enumerate(dst_packs):
        prob_grad[t * rows : (t + 1) * rows] = dot(one[rows:], bel_all[...], TN)


def stage(g, src_packs, dst_packs):
    return pl.pallas_call(
        functools.partial(stage_kernel, g),
        out_shape=(
            shape((g.span, g.width), bf16),
            shape((g.batch, g.span), bf16),
            shape((g.tall, g.width), bf16),
            shape((g.tall, g.span), f32),
        ),
        in_specs=[in_vmem()] * (g.n_row + g.n_col),
        out_specs=(in_vmem(),) * 4,
        compiler_params=pltpu.CompilerParams(vmem_limit_bytes=g.tiles * 4 + 4 * mib),
        cost_estimate=pl.CostEstimate(
            flops=2 * g.tiles * g.batch, bytes_accessed=4 * g.tiles, transcendentals=0
        ),
        name="stage",
    )(*src_packs, *dst_packs)


def logit_kernel(g, me_ref, *refs):
    rows = g.rows
    place = (me_ref[0] >> 1) & (g.n_row - 1)
    src_all, bel_all, prob_grad, refs = *refs[:3], refs[3:]
    probs, refs = refs[: g.n_row], refs[g.n_row :]
    grad_sums, refs = refs[: g.n_row], refs[g.n_row :]
    stats, refs = refs[0], refs[1:]
    logit_grad, belief_sum, near_send, own_sum, scale, row_dot = refs
    for r in range(g.n_row):

        def stat(s, kind):
            at = kind * g.n_row + (r ^ s)
            return stats[at : at + 1, block_of(place ^ s, rows)]

        tops = [stat(s, 0) for s in range(g.n_row)]
        top = functools.reduce(jnp.maximum, tops)
        parts = [jnp.exp(one - top) for one in tops]
        total = sum(part * stat(s, 1) for s, part in enumerate(parts))
        dots = sum(part * stat(s, 2) for s, part in enumerate(parts))
        inverse = 1.0 / total
        lanes = slice(r * rows, (r + 1) * rows)
        scale[0:1, lanes] = parts[0] * inverse
        row_dot[0:1, lanes] = dots * inverse
        belief_sum[:, lanes] = grad_sums[r][...] * scale[0:1, lanes]

    def shares_of(t):
        here = block_of(t, rows)
        prob = jnp.concatenate([one[here] for one in probs], axis=1) * scale[0:1]
        change = (prob * (prob_grad[here] - row_dot[0:1])).astype(bf16)
        logit_grad[here] = change
        return dot(change, src_all[...], NN), dot(bel_all[...], prob.astype(bf16), NT)

    def pair(f, carried):
        dst_part, next_part = shares_of(2 * f + 1)
        near_send[f, :rows] = dst_part.astype(bf16)
        near_send[f, rows:] = next_part.astype(bf16)
        dst_part, next_part = shares_of(2 * f)
        own_sum[f, :rows] = dst_part
        own_sum[f, rows:] = next_part
        return carried

    for_each(g.n_far, pair, 0)


def logit_grads(g, src_all, bel_all, prob_grad, probs, grad_sums, stats, me):
    share = (g.n_far, g.rows + g.batch, g.width)
    return pl.pallas_call(
        functools.partial(logit_kernel, g),
        out_shape=(
            shape((g.tall, g.span), bf16),
            shape((g.batch, g.span), f32),
            shape(share, bf16),
            shape(share, f32),
        ),
        in_specs=[in_smem()] + [in_vmem()] * (4 + 2 * g.n_row),
        out_specs=(in_vmem(),) * 4,
        scratch_shapes=[pltpu.VMEM((8, g.span), f32)] * 2,
        compiler_params=pltpu.CompilerParams(vmem_limit_bytes=g.tiles * 4 + 8 * mib),
        cost_estimate=pl.CostEstimate(
            flops=2 * g.tiles * (g.width + g.batch), bytes_accessed=6 * g.tiles, transcendentals=0
        ),
        name="logit_grads",
    )(me, src_all, bel_all, prob_grad, *probs, *grad_sums, stats)


def src_kernel(g, logit_grad, belief_sum, dst_all, own_sum, side_send, cross_send):
    for s in range(g.n_row):
        lanes = slice(s * g.rows, (s + 1) * g.rows)
        total = dot(logit_grad[:, lanes], dst_all[...], TN)
        if s % 2 == 0:
            own_sum[s // 2, : g.rows] = total
            own_sum[s // 2, g.rows :] = belief_sum[:, lanes]
            continue
        send = side_send if s == 1 else cross_send.at[s // 2 - 1]
        send[: g.rows] = total.astype(bf16)
        send[g.rows :] = belief_sum[:, lanes].astype(bf16)


def src_shares(g, logit_grad, belief_sum, dst_all):
    share = (g.rows + g.batch, g.width)
    return pl.pallas_call(
        functools.partial(src_kernel, g),
        out_shape=(
            shape((g.n_row // 2,) + share, f32),
            shape(share, bf16),
            shape((g.n_row // 2 - 1,) + share, bf16),
        ),
        in_specs=[in_vmem()] * 3,
        out_specs=(in_vmem(),) * 3,
        compiler_params=pltpu.CompilerParams(vmem_limit_bytes=g.tiles * 4 + 4 * mib),
        cost_estimate=pl.CostEstimate(
            flops=2 * g.tiles * g.width, bytes_accessed=3 * g.tiles, transcendentals=0
        ),
        name="src_shares",
    )(logit_grad, belief_sum, dst_all)


def fold_kernel(first, n_send, own_sum, near, after, *refs):
    for f in range(1, n_send + 1):
        refs[-n_send + f - 1][...] = (own_sum[f] + near[f - first].astype(f32)).astype(bf16)
    if len(refs) > n_send:
        refs[1][...] = refs[0][...]


def fold(first, own_sum, near, after, handed=None):
    n_send = own_sum.shape[0] - 1
    out_shape = (shape(own_sum.shape[1:], bf16),) * n_send
    extra = []
    if handed is not None:
        out_shape = (shape(handed.shape, bf16),) + out_shape
        extra = [handed]
    return pl.pallas_call(
        functools.partial(fold_kernel, first, n_send),
        out_shape=out_shape,
        in_specs=[in_vmem()] * 2 + [anywhere()] + [in_vmem()] * len(extra),
        out_specs=(in_vmem(),) * len(out_shape),
        compiler_params=pltpu.CompilerParams(vmem_limit_bytes=6 * mib),
        name="fold",
    )(own_sum, near, after, *extra)


def total_kernel(rows, own, near, *refs):
    parts, outs, token = refs[:-4], refs[-3:-1], refs[-1]
    near = near.at[0] if len(near.shape) == 3 else near

    def added(out, here):
        total = own[0, here] + near[here].astype(f32)
        out[...] = (total + sum(part[here].astype(f32) for part in parts)).astype(out.dtype)

    added(outs[0], slice(0, rows))
    added(outs[1], slice(rows, None))
    token[...] = jnp.zeros(token.shape, f32)


def totals(g, own, near, parts, after, small_dtype):
    return pl.pallas_call(
        functools.partial(total_kernel, g.rows),
        out_shape=(
            shape((g.rows, g.width), f32),
            shape((g.batch, g.rows), small_dtype),
            shape((8, 128), f32),
        ),
        in_specs=[in_vmem()] * (2 + len(parts)) + [anywhere()],
        out_specs=(in_vmem(),) * 3,
        compiler_params=pltpu.CompilerParams(vmem_limit_bytes=6 * mib),
        name="totals",
    )(own, near, *parts, after)


def per_device(n, src_emb, dst_emb, tile_dst, tile_count, beliefs, grad_next):
    g = Grid(n, *src_emb.shape, beliefs.shape[0])
    me = lax.axis_index("src").astype(jnp.int32).reshape(1)

    def swap(array, flip):
        return lax.ppermute(array, "src", [(i, i ^ flip) for i in range(n)])

    src_pack, dst_pack = pack(g, me, tile_dst, tile_count, src_emb, beliefs, dst_emb, grad_next)
    src_far = [swap(src_pack, g.row_flip(s)) for s in range(2, g.n_row, 2)]
    dst_far = [swap(dst_pack, g.far_flip(f)) for f in range(1, g.n_far)]
    src_side = swap(src_pack, g.row_flip(1))
    dst_near = swap(dst_pack, 1)
    src_kept, dst_kept = keep(src_pack, dst_pack)
    src_packs, dst_packs = [src_kept, src_side], [dst_kept, dst_near]
    for one in src_far:
        src_packs += [one, swap(hand(one, src_side), g.row_flip(1))]
    for one in dst_far:
        dst_packs += [one, swap(hand(one, dst_near), 1)]
    scored = [scores(g, s, one, dst_packs) for s, one in enumerate(src_packs)]
    probs, grad_sums, stats = zip(*scored)
    stats = join(g, stats)
    groups = [[i ^ g.row_flip(s) for s in range(g.n_row)] for i in range(n) if not (i >> 1) & (g.n_row - 1)]
    all_stats = lax.all_gather(stats, "src", axis=1, tiled=True, axis_index_groups=groups)
    src_all, bel_all, dst_all, prob_grad = stage(g, src_packs, dst_packs)
    logit_grad, belief_sum, near_send, dst_sum = logit_grads(
        g, src_all, bel_all, prob_grad, probs, grad_sums, all_stats, me
    )
    near = swap(near_send, 1)
    src_sum, side_send, cross_send = src_shares(g, logit_grad, belief_sum, dst_all)
    cross = swap(cross_send, g.row_flip(1))
    dst_folded = fold(0, dst_sum, near, src_sum)
    dst_parts = [swap(one, g.far_flip(f)) for f, one in enumerate(dst_folded, 1)]
    side_send, *src_folded = fold(1, src_sum, cross, dst_folded[0], side_send)
    src_parts = [swap(one, g.row_flip(2 * f)) for f, one in enumerate(src_folded, 1)]
    side = swap(side_send, g.row_flip(1))
    grad_dst, next_belief, token = totals(g, dst_sum, near, dst_parts, src_sum, f32)
    grad_src, grad_belief, _ = totals(g, src_sum, side, src_parts, token, bf16)
    return (next_belief, grad_belief, grad_src, grad_dst)


def solution(mesh):
    placed = (
        P(("groups", "src"), None),
        P(("groups", "src"), None),
        P(("groups", "src"), None),
        P(("groups", "src")),
        P("groups", "src"),
        P("groups", "src"),
    )
    return jax.shard_map(
        functools.partial(per_device, mesh.shape["src"]),
        mesh=mesh,
        in_specs=placed,
        out_specs=(
            P("groups", "src"),
            P("groups", "src"),
            P(("groups", "src"), None),
            P(("groups", "src"), None),
        ),
        check_vma=False,
    )
```

```python
import functools

import jax
import jax.numpy as jnp
from jax import lax
from jax.experimental import pallas as pl
from jax.experimental.pallas import tpu as pltpu
from jax.sharding import PartitionSpec as P

f32 = jnp.float32
bf16 = jnp.bfloat16
unlisted = 1e30
mib = 1 << 20


class Grid:
    def __init__(self, n, rows, width, batch):
        row_bits = (n.bit_length() - 1) // 2
        self.n, self.rows, self.width, self.batch = n, rows, width, batch
        self.row_bits = row_bits
        self.n_row = 1 << row_bits
        self.n_col = n // self.n_row
        self.n_far = self.n_col // 2
        self.span = self.n_row * rows
        self.tall = self.n_col * rows
        self.tiles = self.span * self.tall
        self.head = (3 * self.n_row + 7) // 8 * 8

    def row_flip(self, s):
        return s << 1

    def far_flip(self, f):
        return f << (1 + self.row_bits)

    def col_flip(self, t):
        return (t & 1) | self.far_flip(t >> 1)


def dot(a, b, dims):
    return lax.dot_general(a, b, (dims, ((), ())), preferred_element_type=f32)


NN = ((1,), (0,))
NT = ((1,), (1,))
TN = ((0,), (0,))


def block_of(index, size):
    if isinstance(index, int):
        return pl.ds(index * size, size)
    return pl.ds(pl.multiple_of(index * size, size), size)


def for_each(count, body, carried):
    if count <= 4:
        for index in range(count):
            carried = body(index, carried)
        return carried
    return lax.fori_loop(0, count, body, carried)


def in_vmem():
    return pl.BlockSpec(memory_space=pltpu.VMEM)


def anywhere():
    return pl.BlockSpec(memory_space=pl.ANY)


def in_smem():
    return pl.BlockSpec(memory_space=pltpu.SMEM)


shape = jax.ShapeDtypeStruct


def pack_kernel(g, me_ref, tile_ref, count_ref, src_ref, bel_ref, dst_ref, grad_ref, src_pack, dst_pack, flags):
    rows, batch = g.rows, g.batch
    me = me_ref[0]
    for k in range(g.n):
        flags[pl.ds(tile_ref[0, k] ^ me, 1), :] = jnp.broadcast_to(
            jnp.where(k < count_ref[0], 1.0, 0.0), (1, g.width)
        ).astype(f32)
    src_pack[:rows] = src_ref[...]
    src_pack[rows : rows + batch] = bel_ref[...]
    src_pack[rows + batch :] = flags[...].astype(bf16)
    dst_pack[:rows] = dst_ref[...]
    dst_pack[rows:] = grad_ref[...]


def pack(g, me, tile_dst, tile_count, src_emb, beliefs, dst_emb, grad_next):
    return pl.pallas_call(
        functools.partial(pack_kernel, g),
        out_shape=(
            shape((g.rows + g.batch + g.n, g.width), bf16),
            shape((g.rows + g.batch, g.width), bf16),
        ),
        in_specs=[in_smem()] * 3 + [in_vmem()] * 4,
        out_specs=(in_vmem(),) * 2,
        scratch_shapes=[pltpu.VMEM((g.n, g.width), f32)],
        compiler_params=pltpu.CompilerParams(vmem_limit_bytes=60 * mib),
        name="pack",
    )(me, tile_dst, tile_count, src_emb, beliefs, dst_emb, grad_next)


def keep_kernel(src_pack, dst_pack, src_out, dst_out):
    src_out[...] = src_pack[...]
    dst_out[...] = dst_pack[...]


def keep(src_pack, dst_pack):
    return pl.pallas_call(
        keep_kernel,
        out_shape=(shape(src_pack.shape, bf16), shape(dst_pack.shape, bf16)),
        in_specs=[in_vmem()] * 2,
        out_specs=(in_vmem(),) * 2,
        compiler_params=pltpu.CompilerParams(vmem_limit_bytes=2 * mib),
        name="keep",
    )(src_pack, dst_pack)


def hand_kernel(one, *refs):
    refs[-1][...] = one[...]


def hand(one, *after):
    return pl.pallas_call(
        hand_kernel,
        out_shape=shape(one.shape, one.dtype),
        in_specs=[in_vmem()] + [anywhere()] * len(after),
        out_specs=in_vmem(),
        compiler_params=pltpu.CompilerParams(vmem_limit_bytes=mib),
        name="hand",
    )(one, *after)


def score_kernel(g, s, src_pack, *refs):
    rows, batch = g.rows, g.batch
    dst_packs, refs = refs[: g.n_col], refs[g.n_col :]
    prob_ref, grad_sum, stats = refs[-3:]
    listed = (src_pack[rows + batch :].astype(f32) - 1.0) * unlisted
    top = jnp.full((8, rows), -unlisted, f32)
    for t in range(g.n_col):
        v = g.row_flip(s) ^ g.col_flip(t)
        logits = dot(dst_packs[t][:rows], src_pack[:rows], NT) + listed[v : v + 1]
        prob_ref[t * rows : (t + 1) * rows] = logits
        top = jnp.maximum(top, jnp.max(logits.reshape(rows // 8, 8, rows), axis=0))
    top = jnp.max(top, axis=0, keepdims=True)
    total = jnp.zeros((8, rows), f32)
    grads = jnp.zeros((batch, rows), f32)
    for t in range(g.n_col):
        here = slice(t * rows, (t + 1) * rows)
        prob = jnp.exp(prob_ref[here] - top)
        prob_ref[here] = prob
        grads = grads + dot(dst_packs[t][rows:], prob.astype(bf16), NN)
        total = total + jnp.sum(prob.reshape(rows // 8, 8, rows), axis=0)
    grad_sum[...] = grads
    stats[0:1] = top
    stats[1:2] = jnp.sum(total, axis=0, keepdims=True)
    stats[2:3] = jnp.sum(src_pack[rows : rows + batch].astype(f32) * grads, axis=0, keepdims=True)


def scores(g, s, src_pack, dst_packs, *after):
    tiles = g.tall * g.rows
    return pl.pallas_call(
        functools.partial(score_kernel, g, s),
        out_shape=(
            shape((g.tall, g.rows), f32),
            shape((g.batch, g.rows), f32),
            shape((3, g.rows), f32),
        ),
        in_specs=[in_vmem()] * (1 + g.n_col) + [anywhere()] * len(after),
        out_specs=(in_vmem(),) * 3,
        compiler_params=pltpu.CompilerParams(vmem_limit_bytes=tiles * 8 + 4 * mib),
        name="scores",
    )(src_pack, *dst_packs, *after)


def join_kernel(g, *refs):
    stats, out = refs[:-1], refs[-1]
    for s, one in enumerate(stats):
        for kind in range(3):
            at = kind * g.n_row + s
            out[at : at + 1] = one[kind : kind + 1]
    if g.head > 3 * g.n_row:
        out[3 * g.n_row :] = jnp.zeros((g.head - 3 * g.n_row, g.rows), f32)


def join(g, stats):
    return pl.pallas_call(
        functools.partial(join_kernel, g),
        out_shape=shape((g.head, g.rows), f32),
        in_specs=[in_vmem()] * g.n_row,
        out_specs=in_vmem(),
        compiler_params=pltpu.CompilerParams(vmem_limit_bytes=mib),
        name="join",
    )(*stats)


def merge_kernel(g, flip, one, other, out):
    for u in range(g.n_row):
        tops = one[u : u + 1], other[u ^ flip : (u ^ flip) + 1]
        top = jnp.maximum(*tops)
        parts = [jnp.exp(value - top) for value in tops]
        out[u : u + 1] = top
        for kind in (1, 2):
            a, b = kind * g.n_row + u, kind * g.n_row + (u ^ flip)
            out[a : a + 1] = parts[0] * one[a : a + 1] + parts[1] * other[b : b + 1]
    if g.head > 3 * g.n_row:
        out[3 * g.n_row :] = jnp.zeros((g.head - 3 * g.n_row, g.rows), f32)


def merge(g, flip, one, other):
    return pl.pallas_call(
        functools.partial(merge_kernel, g, flip),
        out_shape=shape((g.head, g.rows), f32),
        in_specs=[in_vmem()] * 2,
        out_specs=in_vmem(),
        compiler_params=pltpu.CompilerParams(vmem_limit_bytes=mib),
        name="merge",
    )(one, other)


def stage_kernel(g, *refs):
    rows, batch = g.rows, g.batch
    src_packs, refs = refs[: g.n_row], refs[g.n_row :]
    dst_packs, refs = refs[: g.n_col], refs[g.n_col :]
    src_all, bel_all, dst_all, prob_grad = refs
    for t, one in enumerate(dst_packs):
        dst_all[t * rows : (t + 1) * rows] = one[:rows]
    for s, one in enumerate(src_packs):
        lanes = slice(s * rows, (s + 1) * rows)
        src_all[lanes] = one[:rows]
        bel_all[:, lanes] = one[rows : rows + batch]
    for t, one in enumerate(dst_packs):
        prob_grad[t * rows : (t + 1) * rows] = dot(one[rows:], bel_all[...], TN)


def stage(g, src_packs, dst_packs):
    return pl.pallas_call(
        functools.partial(stage_kernel, g),
        out_shape=(
            shape((g.span, g.width), bf16),
            shape((g.batch, g.span), bf16),
            shape((g.tall, g.width), bf16),
            shape((g.tall, g.span), f32),
        ),
        in_specs=[in_vmem()] * (g.n_row + g.n_col),
        out_specs=(in_vmem(),) * 4,
        compiler_params=pltpu.CompilerParams(vmem_limit_bytes=g.tiles * 4 + 4 * mib),
        cost_estimate=pl.CostEstimate(
            flops=2 * g.tiles * g.batch, bytes_accessed=4 * g.tiles, transcendentals=0
        ),
        name="stage",
    )(*src_packs, *dst_packs)


def logit_kernel(g, *refs):
    rows = g.rows
    src_all, bel_all, prob_grad, refs = *refs[:3], refs[3:]
    probs, refs = refs[: g.n_row], refs[g.n_row :]
    grad_sums, refs = refs[: g.n_row], refs[g.n_row :]
    own, joint, logit_grad, belief_sum, near_send, own_sum, scale, row_dot = refs
    for r in range(g.n_row):
        lanes = slice(r * rows, (r + 1) * rows)
        top, total, dots = (joint[kind * g.n_row + r : kind * g.n_row + r + 1] for kind in range(3))
        inverse = 1.0 / total
        scale[0:1, lanes] = jnp.exp(own[r : r + 1] - top) * inverse
        row_dot[0:1, lanes] = dots * inverse
        belief_sum[:, lanes] = grad_sums[r][...] * scale[0:1, lanes]

    def shares_of(t):
        here = block_of(t, rows)
        prob = jnp.concatenate([one[here] for one in probs], axis=1) * scale[0:1]
        change = (prob * (prob_grad[here] - row_dot[0:1])).astype(bf16)
        logit_grad[here] = change
        return dot(change, src_all[...], NN), dot(bel_all[...], prob.astype(bf16), NT)

    def pair(f, carried):
        dst_part, next_part = shares_of(2 * f + 1)
        near_send[f, :rows] = dst_part.astype(bf16)
        near_send[f, rows:] = next_part.astype(bf16)
        dst_part, next_part = shares_of(2 * f)
        own_sum[f, :rows] = dst_part
        own_sum[f, rows:] = next_part
        return carried

    for_each(g.n_far, pair, 0)


def logit_grads(g, src_all, bel_all, prob_grad, probs, grad_sums, own, joint):
    share = (g.n_far, g.rows + g.batch, g.width)
    return pl.pallas_call(
        functools.partial(logit_kernel, g),
        out_shape=(
            shape((g.tall, g.span), bf16),
            shape((g.batch, g.span), f32),
            shape(share, bf16),
            shape(share, f32),
        ),
        in_specs=[in_vmem()] * (5 + 2 * g.n_row),
        out_specs=(in_vmem(),) * 4,
        scratch_shapes=[pltpu.VMEM((8, g.span), f32)] * 2,
        compiler_params=pltpu.CompilerParams(vmem_limit_bytes=g.tiles * 4 + 8 * mib),
        cost_estimate=pl.CostEstimate(
            flops=2 * g.tiles * (g.width + g.batch), bytes_accessed=6 * g.tiles, transcendentals=0
        ),
        name="logit_grads",
    )(src_all, bel_all, prob_grad, *probs, *grad_sums, own, joint)


def src_kernel(g, logit_grad, belief_sum, dst_all, *outs):
    for s in reversed(range(g.n_row)):
        lanes = slice(s * g.rows, (s + 1) * g.rows)
        total = dot(logit_grad[:, lanes], dst_all[...], TN)
        outs[s][: g.rows] = total.astype(outs[s].dtype)
        outs[s][g.rows :] = belief_sum[:, lanes].astype(outs[s].dtype)


def src_shares(g, logit_grad, belief_sum, dst_all):
    share = (g.rows + g.batch, g.width)
    return pl.pallas_call(
        functools.partial(src_kernel, g),
        out_shape=(shape(share, f32),) + (shape(share, bf16),) * (g.n_row - 1),
        in_specs=[in_vmem()] * 3,
        out_specs=(in_vmem(),) * g.n_row,
        compiler_params=pltpu.CompilerParams(vmem_limit_bytes=g.tiles * 4 + 4 * mib),
        cost_estimate=pl.CostEstimate(
            flops=2 * g.tiles * g.width, bytes_accessed=3 * g.tiles, transcendentals=0
        ),
        name="src_shares",
    )(logit_grad, belief_sum, dst_all)


def fold_kernel(own_sum, near, after, *sends):
    for f, send in enumerate(sends, 1):
        send[...] = (own_sum[f] + near[f].astype(f32)).astype(bf16)


def fold(own_sum, near, after):
    n_send = own_sum.shape[0] - 1
    return pl.pallas_call(
        fold_kernel,
        out_shape=(shape(own_sum.shape[1:], bf16),) * n_send,
        in_specs=[in_vmem()] * 2 + [anywhere()],
        out_specs=(in_vmem(),) * n_send,
        compiler_params=pltpu.CompilerParams(vmem_limit_bytes=6 * mib),
        name="fold",
    )(own_sum, near, after)


def total_kernel(g, *refs):
    src_own, dst_sum, near, refs = *refs[:3], refs[3:]
    src_parts, refs = refs[: g.n_row - 1], refs[g.n_row - 1 :]
    dst_parts, refs = refs[: g.n_far - 1], refs[g.n_far - 1 :]
    src_out, belief_out, dst_out, next_out = refs

    def added(out, here, own, parts):
        total = own[here] + sum(part[here].astype(f32) for part in parts)
        out[...] = total.astype(out.dtype)

    big, small = slice(0, g.rows), slice(g.rows, g.rows + g.batch)
    added(src_out, big, src_own, src_parts)
    added(belief_out, small, src_own, src_parts)
    added(dst_out, big, dst_sum.at[0], (near.at[0], *dst_parts))
    added(next_out, small, dst_sum.at[0], (near.at[0], *dst_parts))


def totals(g, src_own, dst_sum, near, src_parts, dst_parts):
    return pl.pallas_call(
        functools.partial(total_kernel, g),
        out_shape=(
            shape((g.rows, g.width), f32),
            shape((g.batch, g.rows), bf16),
            shape((g.rows, g.width), f32),
            shape((g.batch, g.rows), f32),
        ),
        in_specs=[in_vmem()] * (3 + len(src_parts) + len(dst_parts)),
        out_specs=(in_vmem(),) * 4,
        compiler_params=pltpu.CompilerParams(vmem_limit_bytes=8 * mib),
        name="totals",
    )(src_own, dst_sum, near, *src_parts, *dst_parts)


def per_device(n, src_emb, dst_emb, tile_dst, tile_count, beliefs, grad_next):
    g = Grid(n, *src_emb.shape, beliefs.shape[0])
    me = lax.axis_index("src").astype(jnp.int32).reshape(1)

    def swap(array, flip):
        return lax.ppermute(array, "src", [(i, i ^ flip) for i in range(n)])

    src_pack, dst_pack = pack(g, me, tile_dst, tile_count, src_emb, beliefs, dst_emb, grad_next)
    dst_far = [swap(dst_pack, g.far_flip(f)) for f in range(1, g.n_far)]
    src_rest = [swap(src_pack, g.row_flip(s)) for s in reversed(range(1, g.n_row))][::-1]
    dst_near = swap(dst_pack, 1)
    src_kept, dst_kept = keep(src_pack, dst_pack)
    src_packs, dst_packs = [src_kept] + src_rest, [dst_kept, dst_near]
    for one in dst_far:
        dst_packs += [one, swap(hand(one, dst_near, src_kept), 1)]
    scored = []
    for s, one in enumerate(src_packs):
        scored.append(scores(g, s, one, dst_packs, *[last[2] for last in scored[-1:]]))
    probs, grad_sums, stats = zip(*scored)
    own = joint = join(g, stats)
    src_all, bel_all, dst_all, prob_grad = stage(g, src_packs, dst_packs)
    for bit in range(g.row_bits):
        joint = merge(g, 1 << bit, joint, swap(joint, g.row_flip(1 << bit)))
    logit_grad, belief_sum, near_send, dst_sum = logit_grads(
        g, src_all, bel_all, prob_grad, probs, grad_sums, own, joint
    )
    near = swap(near_send, 1)
    src_own, *src_send = src_shares(g, logit_grad, belief_sum, dst_all)
    src_parts = [swap(src_send[s - 1], g.row_flip(s)) for s in reversed(range(1, g.n_row))]
    dst_folded = fold(dst_sum, near, src_own)
    dst_parts = [swap(one, g.far_flip(f)) for f, one in enumerate(dst_folded, 1)]
    grad_src, grad_belief, grad_dst, next_belief = totals(
        g, src_own, dst_sum, near, src_parts, dst_parts
    )
    return (next_belief, grad_belief, grad_src, grad_dst)


def solution(mesh):
    placed = (
        P(("groups", "src"), None),
        P(("groups", "src"), None),
        P(("groups", "src"), None),
        P(("groups", "src")),
        P("groups", "src"),
        P("groups", "src"),
    )
    return jax.shard_map(
        functools.partial(per_device, mesh.shape["src"]),
        mesh=mesh,
        in_specs=placed,
        out_specs=(
            P("groups", "src"),
            P("groups", "src"),
            P(("groups", "src"), None),
            P(("groups", "src"), None),
        ),
        check_vma=False,
    )
```

```python
import functools

import jax
import jax.numpy as jnp
from jax import lax
from jax.experimental import pallas as pl
from jax.experimental.pallas import tpu as pltpu
from jax.sharding import PartitionSpec as P

f32 = jnp.float32
bf16 = jnp.bfloat16
unlisted = 1e30
mib = 1 << 20


class Grid:
    def __init__(self, n, rows, width, batch):
        row_bits = (n.bit_length() - 1) // 2
        self.n, self.rows, self.width, self.batch = n, rows, width, batch
        self.row_bits = row_bits
        self.n_row = 1 << row_bits
        self.n_col = n // self.n_row
        self.n_far = self.n_col // 2
        self.span = self.n_row * rows
        self.tall = self.n_col * rows
        self.tiles = self.span * self.tall
        self.head = (3 * self.n_row + 7) // 8 * 8
        self.late = list(range(3, self.n_row, 2))
        self.early = [s for s in range(self.n_row) if s not in self.late]
        self.order = self.early + self.late

    def row_flip(self, s):
        return s << 1

    def far_flip(self, f):
        return f << (1 + self.row_bits)

    def col_flip(self, t):
        return (t & 1) | self.far_flip(t >> 1)


def dot(a, b, dims):
    return lax.dot_general(a, b, (dims, ((), ())), preferred_element_type=f32)


NN = ((1,), (0,))
NT = ((1,), (1,))
TN = ((0,), (0,))


def block_of(index, size):
    if isinstance(index, int):
        return pl.ds(index * size, size)
    return pl.ds(pl.multiple_of(index * size, size), size)


def for_each(count, body, carried):
    if count <= 4:
        for index in range(count):
            carried = body(index, carried)
        return carried
    return lax.fori_loop(0, count, body, carried)


def in_vmem():
    return pl.BlockSpec(memory_space=pltpu.VMEM)


def anywhere():
    return pl.BlockSpec(memory_space=pl.ANY)


def in_smem():
    return pl.BlockSpec(memory_space=pltpu.SMEM)


shape = jax.ShapeDtypeStruct


def pack_kernel(g, me_ref, tile_ref, count_ref, src_ref, bel_ref, dst_ref, grad_ref, src_pack, dst_pack, flags):
    rows, batch = g.rows, g.batch
    me = me_ref[0]
    for k in range(g.n):
        flags[pl.ds(tile_ref[0, k] ^ me, 1), :] = jnp.broadcast_to(
            jnp.where(k < count_ref[0], 1.0, 0.0), (1, g.width)
        ).astype(f32)
    src_pack[:rows] = src_ref[...]
    src_pack[rows : rows + batch] = bel_ref[...]
    src_pack[rows + batch :] = flags[...].astype(bf16)
    dst_pack[:rows] = dst_ref[...]
    dst_pack[rows:] = grad_ref[...]


def pack(g, me, tile_dst, tile_count, src_emb, beliefs, dst_emb, grad_next):
    return pl.pallas_call(
        functools.partial(pack_kernel, g),
        out_shape=(
            shape((g.rows + g.batch + g.n, g.width), bf16),
            shape((g.rows + g.batch, g.width), bf16),
        ),
        in_specs=[in_smem()] * 3 + [in_vmem()] * 4,
        out_specs=(in_vmem(),) * 2,
        scratch_shapes=[pltpu.VMEM((g.n, g.width), f32)],
        compiler_params=pltpu.CompilerParams(vmem_limit_bytes=60 * mib),
        name="pack",
    )(me, tile_dst, tile_count, src_emb, beliefs, dst_emb, grad_next)


def keep_kernel(src_pack, dst_pack, src_out, dst_out):
    src_out[...] = src_pack[...]
    dst_out[...] = dst_pack[...]


def keep(src_pack, dst_pack):
    return pl.pallas_call(
        keep_kernel,
        out_shape=(shape(src_pack.shape, bf16), shape(dst_pack.shape, bf16)),
        in_specs=[in_vmem()] * 2,
        out_specs=(in_vmem(),) * 2,
        compiler_params=pltpu.CompilerParams(vmem_limit_bytes=2 * mib),
        name="keep",
    )(src_pack, dst_pack)


def hand_kernel(one, *refs):
    refs[-1][...] = one[...]


def hand(one, *after):
    return pl.pallas_call(
        hand_kernel,
        out_shape=shape(one.shape, one.dtype),
        in_specs=[in_vmem()] + [anywhere()] * len(after),
        out_specs=in_vmem(),
        compiler_params=pltpu.CompilerParams(vmem_limit_bytes=mib),
        name="hand",
    )(one, *after)


def score_kernel(g, slots, *refs):
    rows, batch = g.rows, g.batch
    src_packs, refs = refs[: len(slots)], refs[len(slots) :]
    dst_packs, refs = refs[: g.n_col], refs[g.n_col :]
    prob_ref, grad_sum, stats, src_all, bel_all = refs[-5:]
    span = len(slots) * rows
    listed = []
    for p, one in enumerate(src_packs):
        lanes = slice(p * rows, (p + 1) * rows)
        src_all[lanes] = one[:rows]
        bel_all[:, lanes] = one[rows : rows + batch]
        listed.append((one[rows + batch :].astype(f32) - 1.0) * unlisted)
    top = jnp.full((8, span), -unlisted, f32)
    for t in range(g.n_col):
        flips = [g.row_flip(s) ^ g.col_flip(t) for s in slots]
        bias = jnp.concatenate([one[v : v + 1] for one, v in zip(listed, flips)], axis=1)
        logits = dot(dst_packs[t][:rows], src_all[...], NT) + bias
        prob_ref[t * rows : (t + 1) * rows] = logits
        top = jnp.maximum(top, jnp.max(logits.reshape(rows // 8, 8, span), axis=0))
    top = jnp.max(top, axis=0, keepdims=True)
    total = jnp.zeros((8, span), f32)
    grad_sum[...] = jnp.zeros(grad_sum.shape, f32)
    for t in range(g.n_col):
        here = slice(t * rows, (t + 1) * rows)
        prob = jnp.exp(prob_ref[here] - top)
        prob_ref[here] = prob
        grad_sum[...] += dot(dst_packs[t][rows:], prob.astype(bf16), NN)
        total = total + jnp.sum(prob.reshape(rows // 8, 8, span), axis=0)
    stats[0:1] = top
    stats[1:2] = jnp.sum(total, axis=0, keepdims=True)
    stats[2:3] = jnp.sum(bel_all[...].astype(f32) * grad_sum[...], axis=0, keepdims=True)


def scores(g, slots, src_packs, dst_packs, *after):
    span = len(slots) * g.rows
    return pl.pallas_call(
        functools.partial(score_kernel, g, slots),
        out_shape=(
            shape((g.tall, span), f32),
            shape((g.batch, span), f32),
            shape((3, span), f32),
        ),
        in_specs=[in_vmem()] * (len(slots) + g.n_col) + [anywhere()] * len(after),
        out_specs=(in_vmem(),) * 3,
        scratch_shapes=[pltpu.VMEM((span, g.width), bf16), pltpu.VMEM((g.batch, span), bf16)],
        compiler_params=pltpu.CompilerParams(vmem_limit_bytes=g.tall * span * 8 + 4 * mib),
        name="scores",
    )(*[src_packs[s] for s in slots], *dst_packs, *after)


def join_kernel(g, early, late, out):
    for p, s in enumerate(g.order):
        part, q = (early, p) if p < len(g.early) else (late, p - len(g.early))
        for kind in range(3):
            at = kind * g.n_row + s
            out[at : at + 1] = part[kind : kind + 1, q * g.rows : (q + 1) * g.rows]
    if g.head > 3 * g.n_row:
        out[3 * g.n_row :] = jnp.zeros((g.head - 3 * g.n_row, g.rows), f32)


def join(g, early, late):
    return pl.pallas_call(
        functools.partial(join_kernel, g),
        out_shape=shape((g.head, g.rows), f32),
        in_specs=[in_vmem()] * 2,
        out_specs=in_vmem(),
        compiler_params=pltpu.CompilerParams(vmem_limit_bytes=mib),
        name="join",
    )(early, late)


def stage_kernel(g, *refs):
    rows, batch = g.rows, g.batch
    src_packs, refs = refs[: g.n_row], refs[g.n_row :]
    dst_packs, refs = refs[: g.n_col], refs[g.n_col :]
    src_all, bel_all, dst_all, prob_grad = refs
    for t, one in enumerate(dst_packs):
        dst_all[t * rows : (t + 1) * rows] = one[:rows]
    for s, one in enumerate(src_packs):
        lanes = slice(s * rows, (s + 1) * rows)
        src_all[lanes] = one[:rows]
        bel_all[:, lanes] = one[rows : rows + batch]
    for t, one in enumerate(dst_packs):
        prob_grad[t * rows : (t + 1) * rows] = dot(one[rows:], bel_all[...], TN)


def stage(g, src_packs, dst_packs):
    return pl.pallas_call(
        functools.partial(stage_kernel, g),
        out_shape=(
            shape((g.span, g.width), bf16),
            shape((g.batch, g.span), bf16),
            shape((g.tall, g.width), bf16),
            shape((g.tall, g.span), f32),
        ),
        in_specs=[in_vmem()] * (g.n_row + g.n_col),
        out_specs=(in_vmem(),) * 4,
        compiler_params=pltpu.CompilerParams(vmem_limit_bytes=g.tiles * 4 + 4 * mib),
        cost_estimate=pl.CostEstimate(
            flops=2 * g.tiles * g.batch, bytes_accessed=4 * g.tiles, transcendentals=0
        ),
        name="stage",
    )(*[src_packs[s] for s in g.order], *dst_packs)


def logit_kernel(g, *refs):
    rows = g.rows
    src_all, bel_all, prob_grad, refs = *refs[:3], refs[3:]
    probs, grad_sums, refs = refs[:2], refs[2:4], refs[4:]
    stats, refs = refs[: g.n_row], refs[g.n_row :]
    logit_grad, belief_sum, near_send, own_sum, scale, row_dot = refs
    for p, r in enumerate(g.order):

        def stat(s, kind):
            at = kind * g.n_row + (r ^ s)
            return stats[s][at : at + 1]

        tops = [stat(s, 0) for s in range(g.n_row)]
        top = functools.reduce(jnp.maximum, tops)
        parts = [jnp.exp(one - top) for one in tops]
        total = sum(part * stat(s, 1) for s, part in enumerate(parts))
        dots = sum(part * stat(s, 2) for s, part in enumerate(parts))
        inverse = 1.0 / total
        lanes = slice(p * rows, (p + 1) * rows)
        scale[0:1, lanes] = parts[0] * inverse
        row_dot[0:1, lanes] = dots * inverse
    edge = len(g.early) * rows
    belief_sum[:, :edge] = grad_sums[0][...] * scale[0:1, :edge]
    belief_sum[:, edge:] = grad_sums[1][...] * scale[0:1, edge:]

    def shares_of(t):
        here = block_of(t, rows)
        prob = jnp.concatenate([one[here] for one in probs], axis=1) * scale[0:1]
        change = (prob * (prob_grad[here] - row_dot[0:1])).astype(bf16)
        logit_grad[here] = change
        return dot(change, src_all[...], NN), dot(bel_all[...], prob.astype(bf16), NT)

    def pair(f, carried):
        dst_part, next_part = shares_of(2 * f + 1)
        near_send[f, :rows] = dst_part.astype(bf16)
        near_send[f, rows:] = next_part.astype(bf16)
        dst_part, next_part = shares_of(2 * f)
        own_sum[f, :rows] = dst_part
        own_sum[f, rows:] = next_part
        return carried

    for_each(g.n_far, pair, 0)


def logit_grads(g, src_all, bel_all, prob_grad, probs, grad_sums, stats):
    share = (g.n_far, g.rows + g.batch, g.width)
    return pl.pallas_call(
        functools.partial(logit_kernel, g),
        out_shape=(
            shape((g.tall, g.span), bf16),
            shape((g.batch, g.span), f32),
            shape(share, bf16),
            shape(share, f32),
        ),
        in_specs=[in_vmem()] * (7 + g.n_row),
        out_specs=(in_vmem(),) * 4,
        scratch_shapes=[pltpu.VMEM((8, g.span), f32)] * 2,
        compiler_params=pltpu.CompilerParams(vmem_limit_bytes=g.tiles * 4 + 8 * mib),
        cost_estimate=pl.CostEstimate(
            flops=2 * g.tiles * (g.width + g.batch), bytes_accessed=6 * g.tiles, transcendentals=0
        ),
        name="logit_grads",
    )(src_all, bel_all, prob_grad, *probs, *grad_sums, *stats)


def src_kernel(g, logit_grad, belief_sum, dst_all, *outs):
    for p, s in enumerate(g.order):
        lanes = slice(p * g.rows, (p + 1) * g.rows)
        total = dot(logit_grad[:, lanes], dst_all[...], TN)
        outs[s][: g.rows] = total.astype(outs[s].dtype)
        outs[s][g.rows :] = belief_sum[:, lanes].astype(outs[s].dtype)


def src_shares(g, logit_grad, belief_sum, dst_all):
    share = (g.rows + g.batch, g.width)
    return pl.pallas_call(
        functools.partial(src_kernel, g),
        out_shape=(shape(share, f32),) + (shape(share, bf16),) * (g.n_row - 1),
        in_specs=[in_vmem()] * 3,
        out_specs=(in_vmem(),) * g.n_row,
        compiler_params=pltpu.CompilerParams(vmem_limit_bytes=g.tiles * 4 + 4 * mib),
        cost_estimate=pl.CostEstimate(
            flops=2 * g.tiles * g.width, bytes_accessed=3 * g.tiles, transcendentals=0
        ),
        name="src_shares",
    )(logit_grad, belief_sum, dst_all)


def fold_kernel(n_send, own_sum, near, *refs):
    handed = refs[: (len(refs) - n_send) // 2]
    sends = refs[len(handed) : len(handed) + n_send]
    for f, send in enumerate(sends, 1):
        send[...] = (own_sum[f] + near[f].astype(f32)).astype(bf16)
    for one, out in zip(handed, refs[len(handed) + n_send :]):
        out[...] = one[...]


def fold(own_sum, near, handed):
    n_send = own_sum.shape[0] - 1
    out_shape = (shape(own_sum.shape[1:], bf16),) * n_send
    out_shape += tuple(shape(one.shape, one.dtype) for one in handed)
    outs = pl.pallas_call(
        functools.partial(fold_kernel, n_send),
        out_shape=out_shape,
        in_specs=[in_vmem()] * (2 + len(handed)),
        out_specs=(in_vmem(),) * len(out_shape),
        compiler_params=pltpu.CompilerParams(vmem_limit_bytes=8 * mib),
        name="fold",
    )(own_sum, near, *handed)
    return outs[:n_send], outs[n_send:]


def total_kernel(g, *refs):
    src_own, dst_sum, near, refs = *refs[:3], refs[3:]
    dst_parts, refs = refs[: g.n_far - 1], refs[g.n_far - 1 :]
    src_parts, refs = refs[: g.n_row - 1], refs[g.n_row - 1 :]
    src_out, belief_out, dst_out, next_out = refs

    def added(out, here, own, parts):
        total = own[here] + sum(part[here].astype(f32) for part in parts)
        out[...] = total.astype(out.dtype)

    big, small = slice(0, g.rows), slice(g.rows, g.rows + g.batch)
    added(src_out, big, src_own, src_parts)
    added(belief_out, small, src_own, src_parts)
    added(dst_out, big, dst_sum.at[0], (near.at[0], *dst_parts))
    added(next_out, small, dst_sum.at[0], (near.at[0], *dst_parts))


def totals(g, src_own, dst_sum, near, src_parts, dst_parts):
    return pl.pallas_call(
        functools.partial(total_kernel, g),
        out_shape=(
            shape((g.rows, g.width), f32),
            shape((g.batch, g.rows), bf16),
            shape((g.rows, g.width), f32),
            shape((g.batch, g.rows), f32),
        ),
        in_specs=[in_vmem()] * (3 + len(src_parts) + len(dst_parts)),
        out_specs=(in_vmem(),) * 4,
        compiler_params=pltpu.CompilerParams(vmem_limit_bytes=8 * mib),
        name="totals",
    )(src_own, dst_sum, near, *dst_parts, *src_parts)


def per_device(n, src_emb, dst_emb, tile_dst, tile_count, beliefs, grad_next):
    g = Grid(n, *src_emb.shape, beliefs.shape[0])
    me = lax.axis_index("src").astype(jnp.int32).reshape(1)

    def swap(array, flip):
        return lax.ppermute(array, "src", [(i, i ^ flip) for i in range(n)])

    src_pack, dst_pack = pack(g, me, tile_dst, tile_count, src_emb, beliefs, dst_emb, grad_next)
    src_far = [swap(src_pack, g.row_flip(s)) for s in g.early[2:]]
    dst_far = [swap(dst_pack, g.far_flip(f)) for f in range(1, g.n_far)]
    src_side = swap(src_pack, g.row_flip(1))
    dst_near = swap(dst_pack, 1)
    src_kept, dst_kept = keep(src_pack, dst_pack)
    src_packs, dst_packs = [src_kept, src_side], [dst_kept, dst_near]
    for one in src_far:
        handed = hand(one, src_side, src_kept)
        src_packs += [one, swap(handed, g.row_flip(1))]
    for one in dst_far:
        dst_packs += [one, swap(hand(one, dst_near, handed), 1)]
    early = scores(g, g.early, src_packs, dst_packs)
    late = scores(g, g.late, src_packs, dst_packs, early[2])
    probs, grad_sums, stats = zip(early, late)
    stats = join(g, *stats)
    all_stats = [stats] + [swap(stats, g.row_flip(s)) for s in range(1, g.n_row)]
    src_all, bel_all, dst_all, prob_grad = stage(g, src_packs, dst_packs)
    logit_grad, belief_sum, near_send, dst_sum = logit_grads(
        g, src_all, bel_all, prob_grad, probs, grad_sums, all_stats
    )
    near = swap(near_send, 1)
    src_own, *src_send = src_shares(g, logit_grad, belief_sum, dst_all)
    dst_folded, src_send = fold(dst_sum, near, src_send)
    dst_parts = [swap(one, g.far_flip(f)) for f, one in enumerate(dst_folded, 1)]
    src_parts = [swap(src_send[s - 1], g.row_flip(s)) for s in reversed(range(1, g.n_row))]
    grad_src, grad_belief, grad_dst, next_belief = totals(
        g, src_own, dst_sum, near, src_parts, dst_parts
    )
    return (next_belief, grad_belief, grad_src, grad_dst)


def solution(mesh):
    placed = (
        P(("groups", "src"), None),
        P(("groups", "src"), None),
        P(("groups", "src"), None),
        P(("groups", "src")),
        P("groups", "src"),
        P("groups", "src"),
    )
    return jax.shard_map(
        functools.partial(per_device, mesh.shape["src"]),
        mesh=mesh,
        in_specs=placed,
        out_specs=(
            P("groups", "src"),
            P("groups", "src"),
            P(("groups", "src"), None),
            P(("groups", "src"), None),
        ),
        check_vma=False,
    )
```

```python
import functools

import jax
import jax.numpy as jnp
from jax import lax
from jax.experimental import pallas as pl
from jax.experimental.pallas import tpu as pltpu
from jax.sharding import PartitionSpec as P

f32 = jnp.float32
bf16 = jnp.bfloat16
unlisted = 1e30
mib = 1 << 20


class Grid:
    def __init__(self, n, rows, width, batch):
        row_bits = (n.bit_length() - 1) // 2
        self.n, self.rows, self.width, self.batch = n, rows, width, batch
        self.row_bits = row_bits
        self.n_row = 1 << row_bits
        self.n_col = n // self.n_row
        self.n_far = self.n_col // 2
        self.span = self.n_row * rows
        self.tall = self.n_col * rows
        self.tiles = self.span * self.tall
        self.head = (3 * self.n_row + 7) // 8 * 8
        self.late = list(range(3, self.n_row, 2))
        self.early = [s for s in range(self.n_row) if s not in self.late]
        self.order = self.early + self.late

    def row_flip(self, s):
        return s << 1

    def far_flip(self, f):
        return f << (1 + self.row_bits)

    def col_flip(self, t):
        return (t & 1) | self.far_flip(t >> 1)


def dot(a, b, dims):
    return lax.dot_general(a, b, (dims, ((), ())), preferred_element_type=f32)


NN = ((1,), (0,))
NT = ((1,), (1,))
TN = ((0,), (0,))


def block_of(index, size):
    if isinstance(index, int):
        return pl.ds(index * size, size)
    return pl.ds(pl.multiple_of(index * size, size), size)


def for_each(count, body, carried):
    if count <= 4:
        for index in range(count):
            carried = body(index, carried)
        return carried
    return lax.fori_loop(0, count, body, carried)


def in_vmem():
    return pl.BlockSpec(memory_space=pltpu.VMEM)


def anywhere():
    return pl.BlockSpec(memory_space=pl.ANY)


def in_smem():
    return pl.BlockSpec(memory_space=pltpu.SMEM)


shape = jax.ShapeDtypeStruct


def pack_kernel(g, me_ref, tile_ref, count_ref, src_ref, bel_ref, dst_ref, grad_ref, src_pack, dst_pack, flags):
    rows, batch = g.rows, g.batch
    me = me_ref[0]
    for k in range(g.n):
        flags[pl.ds(tile_ref[0, k] ^ me, 1), :] = jnp.broadcast_to(
            jnp.where(k < count_ref[0], 1.0, 0.0), (1, g.width)
        ).astype(f32)
    src_pack[:rows] = src_ref[...]
    src_pack[rows : rows + batch] = bel_ref[...]
    src_pack[rows + batch :] = flags[...].astype(bf16)
    dst_pack[:rows] = dst_ref[...]
    dst_pack[rows:] = grad_ref[...]


def pack(g, me, tile_dst, tile_count, src_emb, beliefs, dst_emb, grad_next):
    return pl.pallas_call(
        functools.partial(pack_kernel, g),
        out_shape=(
            shape((g.rows + g.batch + g.n, g.width), bf16),
            shape((g.rows + g.batch, g.width), bf16),
        ),
        in_specs=[in_smem()] * 3 + [in_vmem()] * 4,
        out_specs=(in_vmem(),) * 2,
        scratch_shapes=[pltpu.VMEM((g.n, g.width), f32)],
        compiler_params=pltpu.CompilerParams(vmem_limit_bytes=60 * mib),
        name="pack",
    )(me, tile_dst, tile_count, src_emb, beliefs, dst_emb, grad_next)


def keep_kernel(src_pack, dst_pack, src_out, dst_out):
    src_out[...] = src_pack[...]
    dst_out[...] = dst_pack[...]


def keep(src_pack, dst_pack):
    return pl.pallas_call(
        keep_kernel,
        out_shape=(shape(src_pack.shape, bf16), shape(dst_pack.shape, bf16)),
        in_specs=[in_vmem()] * 2,
        out_specs=(in_vmem(),) * 2,
        compiler_params=pltpu.CompilerParams(vmem_limit_bytes=2 * mib),
        name="keep",
    )(src_pack, dst_pack)


def hand_kernel(one, *refs):
    refs[-1][...] = one[...]


def hand(one, *after):
    return pl.pallas_call(
        hand_kernel,
        out_shape=shape(one.shape, one.dtype),
        in_specs=[in_vmem()] + [anywhere()] * len(after),
        out_specs=in_vmem(),
        compiler_params=pltpu.CompilerParams(vmem_limit_bytes=mib),
        name="hand",
    )(one, *after)


def score_kernel(g, slots, *refs):
    rows, batch = g.rows, g.batch
    src_packs, refs = refs[: len(slots)], refs[len(slots) :]
    dst_packs, refs = refs[: g.n_col], refs[g.n_col :]
    prob_ref, grad_sum, stats, src_all, bel_all = refs[-5:]
    span = len(slots) * rows
    listed = []
    for p, one in enumerate(src_packs):
        lanes = slice(p * rows, (p + 1) * rows)
        src_all[lanes] = one[:rows]
        bel_all[:, lanes] = one[rows : rows + batch]
        listed.append((one[rows + batch :].astype(f32) - 1.0) * unlisted)
    top = jnp.full((8, span), -unlisted, f32)
    for t in range(g.n_col):
        flips = [g.row_flip(s) ^ g.col_flip(t) for s in slots]
        bias = jnp.concatenate([one[v : v + 1] for one, v in zip(listed, flips)], axis=1)
        logits = dot(dst_packs[t][:rows], src_all[...], NT) + bias
        prob_ref[t * rows : (t + 1) * rows] = logits
        top = jnp.maximum(top, jnp.max(logits.reshape(rows // 8, 8, span), axis=0))
    top = jnp.max(top, axis=0, keepdims=True)
    total = jnp.zeros((8, span), f32)
    grad_sum[...] = jnp.zeros(grad_sum.shape, f32)
    for t in range(g.n_col):
        here = slice(t * rows, (t + 1) * rows)
        prob = jnp.exp(prob_ref[here] - top)
        prob_ref[here] = prob
        grad_sum[...] += dot(dst_packs[t][rows:], prob.astype(bf16), NN)
        total = total + jnp.sum(prob.reshape(rows // 8, 8, span), axis=0)
    stats[0:1] = top
    stats[1:2] = jnp.sum(total, axis=0, keepdims=True)
    stats[2:3] = jnp.sum(bel_all[...].astype(f32) * grad_sum[...], axis=0, keepdims=True)


def scores(g, slots, src_packs, dst_packs, *after):
    span = len(slots) * g.rows
    return pl.pallas_call(
        functools.partial(score_kernel, g, slots),
        out_shape=(
            shape((g.tall, span), f32),
            shape((g.batch, span), f32),
            shape((3, span), f32),
        ),
        in_specs=[in_vmem()] * (len(slots) + g.n_col) + [anywhere()] * len(after),
        out_specs=(in_vmem(),) * 3,
        scratch_shapes=[pltpu.VMEM((span, g.width), bf16), pltpu.VMEM((g.batch, span), bf16)],
        compiler_params=pltpu.CompilerParams(vmem_limit_bytes=g.tall * span * 8 + 4 * mib),
        name="scores",
    )(*[src_packs[s] for s in slots], *dst_packs, *after)


def join_kernel(g, early, late, out):
    for p, s in enumerate(g.order):
        part, q = (early, p) if p < len(g.early) else (late, p - len(g.early))
        for kind in range(3):
            at = kind * g.n_row + s
            out[at : at + 1] = part[kind : kind + 1, q * g.rows : (q + 1) * g.rows]
    if g.head > 3 * g.n_row:
        out[3 * g.n_row :] = jnp.zeros((g.head - 3 * g.n_row, g.rows), f32)


def join(g, early, late):
    return pl.pallas_call(
        functools.partial(join_kernel, g),
        out_shape=shape((g.head, g.rows), f32),
        in_specs=[in_vmem()] * 2,
        out_specs=in_vmem(),
        compiler_params=pltpu.CompilerParams(vmem_limit_bytes=mib),
        name="join",
    )(early, late)


def stage_kernel(g, *refs):
    rows, batch = g.rows, g.batch
    src_packs, refs = refs[: g.n_row], refs[g.n_row :]
    dst_packs, refs = refs[: g.n_col], refs[g.n_col :]
    src_all, bel_all, dst_all, prob_grad = refs
    for t, one in enumerate(dst_packs):
        dst_all[t * rows : (t + 1) * rows] = one[:rows]
    for s, one in enumerate(src_packs):
        lanes = slice(s * rows, (s + 1) * rows)
        src_all[lanes] = one[:rows]
        bel_all[:, lanes] = one[rows : rows + batch]
    for t, one in enumerate(dst_packs):
        prob_grad[t * rows : (t + 1) * rows] = dot(one[rows:], bel_all[...], TN)


def stage(g, src_packs, dst_packs):
    return pl.pallas_call(
        functools.partial(stage_kernel, g),
        out_shape=(
            shape((g.span, g.width), bf16),
            shape((g.batch, g.span), bf16),
            shape((g.tall, g.width), bf16),
            shape((g.tall, g.span), f32),
        ),
        in_specs=[in_vmem()] * (g.n_row + g.n_col),
        out_specs=(in_vmem(),) * 4,
        compiler_params=pltpu.CompilerParams(vmem_limit_bytes=g.tiles * 4 + 4 * mib),
        cost_estimate=pl.CostEstimate(
            flops=2 * g.tiles * g.batch, bytes_accessed=4 * g.tiles, transcendentals=0
        ),
        name="stage",
    )(*[src_packs[s] for s in g.order], *dst_packs)


def logit_kernel(g, *refs):
    rows = g.rows
    src_all, bel_all, prob_grad, refs = *refs[:3], refs[3:]
    probs, grad_sums, refs = refs[:2], refs[2:4], refs[4:]
    stats, refs = refs[: g.n_row], refs[g.n_row :]
    logit_grad, belief_sum, near_send, next_sum, scale, row_dot = refs
    for p, r in enumerate(g.order):

        def stat(s, kind):
            at = kind * g.n_row + (r ^ s)
            return stats[s][at : at + 1]

        tops = [stat(s, 0) for s in range(g.n_row)]
        top = functools.reduce(jnp.maximum, tops)
        parts = [jnp.exp(one - top) for one in tops]
        total = sum(part * stat(s, 1) for s, part in enumerate(parts))
        dots = sum(part * stat(s, 2) for s, part in enumerate(parts))
        inverse = 1.0 / total
        lanes = slice(p * rows, (p + 1) * rows)
        scale[0:1, lanes] = parts[0] * inverse
        row_dot[0:1, lanes] = dots * inverse
    edge = len(g.early) * rows
    belief_sum[:, :edge] = grad_sums[0][...] * scale[0:1, :edge]
    belief_sum[:, edge:] = grad_sums[1][...] * scale[0:1, edge:]

    def change_of(t):
        here = block_of(t, rows)
        prob = jnp.concatenate([one[here] for one in probs], axis=1) * scale[0:1]
        logit_grad[here] = (prob * (prob_grad[here] - row_dot[0:1])).astype(bf16)
        return dot(bel_all[...], prob.astype(bf16), NT)

    def pair(f, carried):
        near_send[f, rows:] = change_of(2 * f + 1).astype(bf16)
        near_send[f, :rows] = dot(logit_grad[block_of(2 * f + 1, rows)], src_all[...], NN).astype(bf16)
        next_sum[f] = change_of(2 * f)
        return carried

    for_each(g.n_far, pair, 0)


def logit_grads(g, src_all, bel_all, prob_grad, probs, grad_sums, stats):
    share = (g.n_far, g.rows + g.batch, g.width)
    return pl.pallas_call(
        functools.partial(logit_kernel, g),
        out_shape=(
            shape((g.tall, g.span), bf16),
            shape((g.batch, g.span), f32),
            shape(share, bf16),
            shape((g.n_far, g.batch, g.rows), f32),
        ),
        in_specs=[in_vmem()] * (7 + g.n_row),
        out_specs=(in_vmem(),) * 4,
        scratch_shapes=[pltpu.VMEM((8, g.span), f32)] * 2,
        compiler_params=pltpu.CompilerParams(vmem_limit_bytes=g.tiles * 4 + 8 * mib),
        cost_estimate=pl.CostEstimate(
            flops=2 * g.tiles * (g.width + g.batch), bytes_accessed=6 * g.tiles, transcendentals=0
        ),
        name="logit_grads",
    )(src_all, bel_all, prob_grad, *probs, *grad_sums, *stats)


def own_kernel(g, logit_grad, src_all, next_sum, after, own_sum):
    for f in range(g.n_far):
        here = slice(2 * f * g.rows, (2 * f + 1) * g.rows)
        own_sum[f, : g.rows] = dot(logit_grad[here], src_all[...], NN)
        own_sum[f, g.rows :] = next_sum[f]


def own_shares(g, logit_grad, src_all, next_sum, after):
    return pl.pallas_call(
        functools.partial(own_kernel, g),
        out_shape=shape((g.n_far, g.rows + g.batch, g.width), f32),
        in_specs=[in_vmem()] * 3 + [anywhere()],
        out_specs=in_vmem(),
        compiler_params=pltpu.CompilerParams(vmem_limit_bytes=g.tiles * 4 + 4 * mib),
        name="own_shares",
    )(logit_grad, src_all, next_sum, after)


def src_kernel(g, slots, logit_grad, belief_sum, dst_all, after, *outs):
    for s, out in zip(slots, outs):
        p = g.order.index(s)
        lanes = slice(p * g.rows, (p + 1) * g.rows)
        total = dot(logit_grad[:, lanes], dst_all[...], TN)
        out[: g.rows] = total.astype(out.dtype)
        out[g.rows :] = belief_sum[:, lanes].astype(out.dtype)


def src_shares(g, slots, logit_grad, belief_sum, dst_all, after):
    kinds = [f32 if s % 2 == 0 else bf16 for s in slots]
    return pl.pallas_call(
        functools.partial(src_kernel, g, slots),
        out_shape=tuple(shape((g.rows + g.batch, g.width), kind) for kind in kinds),
        in_specs=[in_vmem()] * 3 + [anywhere()],
        out_specs=(in_vmem(),) * len(slots),
        compiler_params=pltpu.CompilerParams(vmem_limit_bytes=g.tiles * 4 + 4 * mib),
        name="src_shares",
    )(logit_grad, belief_sum, dst_all, after)


def fold_kernel(n_send, owns, nears, *refs):
    for own, near, send in zip(owns, nears, refs[-n_send:]):
        send[...] = (own[...] + near[...].astype(f32)).astype(bf16)


def dst_fold_kernel(n_send, own_sum, near, after, *sends):
    fold_kernel(n_send, [own_sum.at[f + 1] for f in range(n_send)], [near.at[f + 1] for f in range(n_send)], *sends)


def dst_fold(own_sum, near, after):
    n_send = own_sum.shape[0] - 1
    return pl.pallas_call(
        functools.partial(dst_fold_kernel, n_send),
        out_shape=(shape(own_sum.shape[1:], bf16),) * n_send,
        in_specs=[in_vmem()] * 2 + [anywhere()],
        out_specs=(in_vmem(),) * n_send,
        compiler_params=pltpu.CompilerParams(vmem_limit_bytes=8 * mib),
        name="dst_fold",
    )(own_sum, near, after)


def src_fold_kernel(n_send, *refs):
    side, side_out = refs[2 * n_send], refs[2 * n_send + 1]
    side_out[...] = side[...]
    fold_kernel(n_send, refs[:n_send], refs[n_send : 2 * n_send], *refs[2 * n_send + 2 :])


def src_fold(owns, crosses, side):
    n_send = len(owns)
    return pl.pallas_call(
        functools.partial(src_fold_kernel, n_send),
        out_shape=(shape(side.shape, bf16),) * (1 + n_send),
        in_specs=[in_vmem()] * (2 * n_send + 1),
        out_specs=(in_vmem(),) * (1 + n_send),
        compiler_params=pltpu.CompilerParams(vmem_limit_bytes=8 * mib),
        name="src_fold",
    )(*owns, *crosses, side)


def total_kernel(g, *refs):
    src_own, dst_sum, near, refs = *refs[:3], refs[3:]
    dst_parts, src_parts = refs[: g.n_far - 1], refs[g.n_far - 1 : -4]
    src_out, belief_out, dst_out, next_out = refs[-4:]

    def added(out, here, own, parts):
        total = own[here] + sum(part[here].astype(f32) for part in parts)
        out[...] = total.astype(out.dtype)

    big, small = slice(0, g.rows), slice(g.rows, g.rows + g.batch)
    added(src_out, big, src_own, src_parts)
    added(belief_out, small, src_own, src_parts)
    added(dst_out, big, dst_sum.at[0], (near.at[0], *dst_parts))
    added(next_out, small, dst_sum.at[0], (near.at[0], *dst_parts))


def totals(g, src_own, dst_sum, near, dst_parts, src_parts):
    return pl.pallas_call(
        functools.partial(total_kernel, g),
        out_shape=(
            shape((g.rows, g.width), f32),
            shape((g.batch, g.rows), bf16),
            shape((g.rows, g.width), f32),
            shape((g.batch, g.rows), f32),
        ),
        in_specs=[in_vmem()] * (3 + len(src_parts) + len(dst_parts)),
        out_specs=(in_vmem(),) * 4,
        compiler_params=pltpu.CompilerParams(vmem_limit_bytes=8 * mib),
        name="totals",
    )(src_own, dst_sum, near, *dst_parts, *src_parts)


def per_device(n, src_emb, dst_emb, tile_dst, tile_count, beliefs, grad_next):
    g = Grid(n, *src_emb.shape, beliefs.shape[0])
    me = lax.axis_index("src").astype(jnp.int32).reshape(1)

    def swap(array, flip):
        return lax.ppermute(array, "src", [(i, i ^ flip) for i in range(n)])

    src_pack, dst_pack = pack(g, me, tile_dst, tile_count, src_emb, beliefs, dst_emb, grad_next)
    src_far = [swap(src_pack, g.row_flip(s)) for s in g.early[2:]]
    dst_far = [swap(dst_pack, g.far_flip(f)) for f in range(1, g.n_far)]
    src_side = swap(src_pack, g.row_flip(1))
    dst_near = swap(dst_pack, 1)
    src_kept, dst_kept = keep(src_pack, dst_pack)
    src_packs, dst_packs = [src_kept, src_side], [dst_kept, dst_near]
    for one in src_far:
        handed = hand(one, src_side, src_kept)
        src_packs += [one, swap(handed, g.row_flip(1))]
    for one in dst_far:
        dst_packs += [one, swap(hand(one, dst_near, handed), 1)]
    early = scores(g, g.early, src_packs, dst_packs)
    late = scores(g, g.late, src_packs, dst_packs, early[2])
    probs, grad_sums, stats = zip(early, late)
    stats = join(g, *stats)
    all_stats = [stats] + [swap(stats, g.row_flip(s)) for s in range(1, g.n_row)]
    src_all, bel_all, dst_all, prob_grad = stage(g, src_packs, dst_packs)
    logit_grad, belief_sum, near_send, next_sum = logit_grads(
        g, src_all, bel_all, prob_grad, probs, grad_sums, all_stats
    )
    near = swap(near_send, 1)
    cross_send = src_shares(g, g.late, logit_grad, belief_sum, dst_all, near_send)
    crosses = [swap(one, g.row_flip(1)) for one in cross_send]
    dst_sum = own_shares(g, logit_grad, src_all, next_sum, cross_send[0])
    dst_folded = dst_fold(dst_sum, near, cross_send[0])
    dst_parts = [hand(swap(one, g.far_flip(f))) for f, one in enumerate(dst_folded, 1)]
    src_own, side, *src_rest = src_shares(
        g, g.early, logit_grad, belief_sum, dst_all, dst_folded[0]
    )
    side, *src_folded = src_fold(src_rest, crosses, side)
    src_parts = [swap(one, g.row_flip(s)) for one, s in zip(src_folded, g.early[2:])]
    src_parts.append(swap(side, g.row_flip(1)))
    grad_src, grad_belief, grad_dst, next_belief = totals(
        g, src_own, dst_sum, near, dst_parts, src_parts
    )
    return (next_belief, grad_belief, grad_src, grad_dst)


def solution(mesh):
    placed = (
        P(("groups", "src"), None),
        P(("groups", "src"), None),
        P(("groups", "src"), None),
        P(("groups", "src")),
        P("groups", "src"),
        P("groups", "src"),
    )
    return jax.shard_map(
        functools.partial(per_device, mesh.shape["src"]),
        mesh=mesh,
        in_specs=placed,
        out_specs=(
            P("groups", "src"),
            P("groups", "src"),
            P(("groups", "src"), None),
            P(("groups", "src"), None),
        ),
        check_vma=False,
    )
```

```python
import functools

import jax
import jax.numpy as jnp
from jax import lax
from jax.experimental import pallas as pl
from jax.experimental.pallas import tpu as pltpu
from jax.sharding import PartitionSpec as P

f32 = jnp.float32
bf16 = jnp.bfloat16
unlisted = 1e30
mib = 1 << 20


class Grid:
    def __init__(self, n, rows, width, batch):
        bits = n.bit_length() - 1
        row_bits = max(1, bits // 2 - 1)
        self.n, self.rows, self.width, self.batch = n, rows, width, batch
        self.n_row = 1 << row_bits
        self.n_col = n // self.n_row
        self.span = self.n_row * rows
        self.packet = rows + batch
        self.head = (3 * self.n_row + 7) // 8 * 8
        even = range(0, self.n_col, 2)
        self.early = [t for t in even if t & (t - 1) == 0]
        self.late = [t for t in even if t & (t - 1)]
        self.groups = [self.early[:2], self.early[2:], self.late]
        both = [group + [t + 1 for t in group] for group in self.groups]
        self.parts = [both[0] + both[1], both[2]]
        self.spots = {t: (2 * k + (t & 1), group.index(t & ~1)) for k, group in enumerate(self.groups) for t in both[k]}
        top = self.n_col // 2
        self.far = [t for t in range(top, self.n_col, 2)]
        self.near = [t for t in range(0, top, 2)]

    def row_flip(self, s):
        return s * self.n_col

    def where(self, t):
        part = 0 if t in self.parts[0] else 1
        return part, self.parts[part].index(t)


def low_bit(t):
    return t & -t


def dot(a, b, dims):
    return lax.dot_general(a, b, (dims, ((), ())), preferred_element_type=f32)


NN = ((1,), (0,))
NT = ((1,), (1,))
TN = ((0,), (0,))


def in_vmem():
    return pl.BlockSpec(memory_space=pltpu.VMEM)


def anywhere():
    return pl.BlockSpec(memory_space=pl.ANY)


def in_smem():
    return pl.BlockSpec(memory_space=pltpu.SMEM)


shape = jax.ShapeDtypeStruct


def call(name, kernel, out_shape, operands, after=(), scratch=(), limit=8 * mib):
    many = isinstance(out_shape, tuple)
    return pl.pallas_call(
        kernel,
        out_shape=out_shape,
        in_specs=[in_vmem()] * len(operands) + [anywhere()] * len(after),
        out_specs=(in_vmem(),) * len(out_shape) if many else in_vmem(),
        scratch_shapes=list(scratch),
        compiler_params=pltpu.CompilerParams(vmem_limit_bytes=limit),
        name=name,
    )(*operands, *after)


def pack_kernel(g, me_ref, tile_ref, count_ref, src_ref, bel_ref, dst_ref, grad_ref, src_pack, dst_pack, flags):
    rows, batch = g.rows, g.batch
    me = me_ref[0]
    for k in range(g.n):
        flags[pl.ds(tile_ref[0, k] ^ me, 1), :] = jnp.broadcast_to(
            jnp.where(k < count_ref[0], 1.0, 0.0), (1, g.width)
        ).astype(f32)
    src_pack[:rows] = src_ref[...]
    src_pack[rows : rows + batch] = bel_ref[...]
    src_pack[rows + batch :] = flags[...].astype(bf16)
    dst_pack[:rows] = dst_ref[...]
    dst_pack[rows:] = grad_ref[...]


def pack(g, me, tile_dst, tile_count, src_emb, beliefs, dst_emb, grad_next):
    return pl.pallas_call(
        functools.partial(pack_kernel, g),
        out_shape=(
            shape((g.rows + g.batch + g.n, g.width), bf16),
            shape((g.rows + g.batch, g.width), bf16),
        ),
        in_specs=[in_smem()] * 3 + [in_vmem()] * 4,
        out_specs=(in_vmem(),) * 2,
        scratch_shapes=[pltpu.VMEM((g.n, g.width), f32)],
        compiler_params=pltpu.CompilerParams(vmem_limit_bytes=60 * mib),
        name="pack",
    )(me, tile_dst, tile_count, src_emb, beliefs, dst_emb, grad_next)


def keep(src_pack, dst_pack):
    def kernel(src_ref, dst_ref, src_out, dst_out):
        src_out[...] = src_ref[...]
        dst_out[...] = dst_ref[...]

    outs = (shape(src_pack.shape, bf16), shape(dst_pack.shape, bf16))
    return call("keep", kernel, outs, [src_pack, dst_pack], limit=2 * mib)


def hand(one, *after):
    def kernel(one_ref, *refs):
        refs[-1][...] = one_ref[...]

    return call("hand", kernel, shape(one.shape, one.dtype), [one], after, limit=2 * mib)


def stack(packs, *after):
    def kernel(*refs):
        for i in range(len(packs)):
            refs[-1][i] = refs[i][...]

    out = shape((len(packs),) + packs[0].shape, packs[0].dtype)
    return call("stack", kernel, out, packs, after)


def score_kernel(g, slots, *refs):
    rows, batch, span = g.rows, g.batch, g.span
    src_packs, stacks = refs[: g.n_row], refs[g.n_row :]
    prob_ref, grad_sum, stats, src_all, bel_all = refs[-5:]
    first = g.spots[slots[0]][0]
    listed = []
    for s, one in enumerate(src_packs):
        lanes = slice(s * rows, (s + 1) * rows)
        src_all[lanes] = one[:rows]
        bel_all[:, lanes] = one[rows : rows + batch]
        listed.append((one[rows + batch :].astype(f32) - 1.0) * unlisted)

    def packet(t):
        stack, place = g.spots[t]
        return stacks[stack - first].at[place]

    top = jnp.full((8, span), -unlisted, f32)
    for i, t in enumerate(slots):
        flips = [g.row_flip(s) | t for s in range(g.n_row)]
        bias = jnp.concatenate([one[v : v + 1] for one, v in zip(listed, flips)], axis=1)
        logits = dot(packet(t)[:rows], src_all[...], NT) + bias
        prob_ref[i * rows : (i + 1) * rows] = logits
        top = jnp.maximum(top, jnp.max(logits.reshape(rows // 8, 8, span), axis=0))
    top = jnp.max(top, axis=0, keepdims=True)
    total = jnp.zeros((8, span), f32)
    grad_sum[...] = jnp.zeros(grad_sum.shape, f32)
    for i, t in enumerate(slots):
        here = slice(i * rows, (i + 1) * rows)
        prob = jnp.exp(prob_ref[here] - top)
        prob_ref[here] = prob
        grad_sum[...] += dot(packet(t)[rows:], prob.astype(bf16), NN)
        total = total + jnp.sum(prob.reshape(rows // 8, 8, span), axis=0)
    stats[0:1] = top
    stats[1:2] = jnp.sum(total, axis=0, keepdims=True)
    stats[2:3] = jnp.sum(bel_all[...].astype(f32) * grad_sum[...], axis=0, keepdims=True)


def scores(g, slots, src_packs, stacks, *after):
    tall = len(slots) * g.rows
    outs = (shape((tall, g.span), f32), shape((g.batch, g.span), f32), shape((3, g.span), f32))
    scratch = [pltpu.VMEM((g.span, g.width), bf16), pltpu.VMEM((g.batch, g.span), bf16)]
    kernel = functools.partial(score_kernel, g, slots)
    operands = [*src_packs, *stacks]
    return call("scores", kernel, outs, operands, after, scratch, tall * g.span * 8 + 6 * mib)


def merged(stats):
    tops = [one[0:1] for one in stats]
    top = functools.reduce(jnp.maximum, tops)
    factors = [jnp.exp(one - top) for one in tops]
    total = sum(factor * one[1:2] for factor, one in zip(factors, stats))
    dots = sum(factor * one[2:3] for factor, one in zip(factors, stats))
    return top, total, dots


def join(g, stats):
    def kernel(*refs):
        out = refs[-1]
        for kind, value in enumerate(merged(refs[:-1])):
            for s in range(g.n_row):
                at = kind * g.n_row + s
                out[at : at + 1] = value[:, s * g.rows : (s + 1) * g.rows]
        if g.head > 3 * g.n_row:
            out[3 * g.n_row :] = jnp.zeros((g.head - 3 * g.n_row, g.rows), f32)

    return call("join", kernel, shape((g.head, g.rows), f32), stats, limit=2 * mib)


def stage(g, src_packs, stacks):
    rows, batch = g.rows, g.batch

    def kernel(*refs):
        src_refs, stack_refs = refs[: g.n_row], refs[g.n_row : -4]
        src_all, bel_all, *prob_grads = refs[-4:]
        for s, one in enumerate(src_refs):
            lanes = slice(s * rows, (s + 1) * rows)
            src_all[lanes] = one[:rows]
            bel_all[:, lanes] = one[rows : rows + batch]
        for slots, out in zip(g.parts, prob_grads):
            for i, t in enumerate(slots):
                stack, place = g.spots[t]
                out[i * rows : (i + 1) * rows] = dot(stack_refs[stack][place, rows:], bel_all[...], TN)

    outs = (
        shape((g.span, g.width), bf16),
        shape((batch, g.span), bf16),
        *[shape((len(part) * rows, g.span), f32) for part in g.parts],
    )
    limit = g.n * rows * rows * 4 + 8 * mib
    return call("stage", kernel, outs, [*src_packs, *stacks], limit=limit)


def norms(g, stats, grad_sums, messages):
    def kernel(*refs):
        part_stats, part_sums, everyone = refs[:2], refs[2:4], refs[4 : 4 + g.n_row]
        factors, belief_sum = refs[-2:]
        for s in range(g.n_row):
            lanes = slice(s * g.rows, (s + 1) * g.rows)

            def row(u, kind):
                at = kind * g.n_row + (s ^ u)
                return everyone[u][at : at + 1]

            tops = [row(u, 0) for u in range(g.n_row)]
            top = functools.reduce(jnp.maximum, tops)
            shares = [jnp.exp(one - top) for one in tops]
            inverse = 1.0 / sum(share * row(u, 1) for u, share in enumerate(shares))
            for part, one in enumerate(part_stats):
                factors[part : part + 1, lanes] = jnp.exp(one[0:1, lanes] - top) * inverse
            dots = sum(share * row(u, 2) for u, share in enumerate(shares))
            factors[2:3, lanes] = dots * inverse
        belief_sum[...] = part_sums[0][...] * factors[0:1] + part_sums[1][...] * factors[1:2]

    outs = (shape((8, g.span), f32), shape((g.batch, g.span), f32))
    return call("norms", kernel, outs, [*stats, *grad_sums, *messages], limit=4 * mib)


def column_shares(g, slots, kind, factors, probs, prob_grads, src_all, bel_all, *after):
    rows = g.rows

    def kernel(factors, *refs):
        probs, prob_grads, (src_all, bel_all) = refs[:2], refs[2:4], refs[4:6]
        change_ref, share_ref = refs[-2:]
        for i, t in enumerate(slots):
            part, place = g.where(t)
            here = slice(place * rows, (place + 1) * rows)
            prob = probs[part][here] * factors[part : part + 1]
            change = (prob * (prob_grads[part][here] - factors[2:3])).astype(bf16)
            change_ref[i * rows : (i + 1) * rows] = change
            share_ref[i, :rows] = dot(change, src_all[...], NN).astype(kind)
            share_ref[i, rows:] = dot(bel_all[...], prob.astype(bf16), NT).astype(kind)

    outs = (
        shape((len(slots) * rows, g.span), bf16),
        shape((len(slots), g.packet, g.width), kind),
    )
    operands = [factors, *probs, *prob_grads, src_all, bel_all]
    return call("column_shares", kernel, outs, operands, after, limit=g.n * rows * rows * 8 + 6 * mib)


def row_shares(g, slots, kind, changes, order, stacks, belief_sum, *after):
    rows = g.rows

    def kernel(*refs):
        changes = refs[: len(order)]
        stack_refs = refs[len(order) : len(order) + len(stacks)]
        belief_sum = refs[len(order) + len(stacks)]
        for s, out in zip(slots, refs[-len(slots) :]):
            lanes = slice(s * rows, (s + 1) * rows)
            total = 0.0
            for change, columns in zip(changes, order):
                for i, t in enumerate(columns):
                    stack, place = g.spots[t]
                    packet = stack_refs[stack][place, :rows]
                    total = total + dot(change[i * rows : (i + 1) * rows, lanes], packet, TN)
            out[:rows] = total.astype(kind)
            out[rows:] = belief_sum[:, lanes].astype(kind)

    outs = (shape((g.packet, g.width), kind),) * len(slots)
    operands = [*changes, *stacks, belief_sum]
    return call("row_shares", kernel, outs, operands, after, limit=g.n * rows * rows * 4 + 6 * mib)


def fold(own, near, i, others, *after):
    def kernel(own_ref, near_ref, *refs):
        total = own_ref[i] + near_ref[i].astype(f32)
        for one in refs[: len(others)]:
            total = total + one[...].astype(f32)
        refs[-1][...] = total.astype(bf16)

    return call("fold", kernel, shape(own.shape[1:], bf16), [own, near, *others], after)


def totals(g, src_own, src_others, dst_own, dst_near, dst_others):
    def kernel(*refs):
        src_out, belief_out, dst_out, next_out = refs[-4:]
        src_refs, dst_refs = refs[: 1 + len(src_others)], refs[1 + len(src_others) : -4]

        def added(out, here, own, others):
            total = own[here] + sum(one[here].astype(f32) for one in others)
            out[...] = total.astype(out.dtype)

        big, small = slice(0, g.rows), slice(g.rows, g.packet)
        dst_refs = [dst_refs[0].at[0], dst_refs[1].at[0], *dst_refs[2:]]
        added(src_out, big, src_refs[0], src_refs[1:])
        added(belief_out, small, src_refs[0], src_refs[1:])
        added(dst_out, big, dst_refs[0], dst_refs[1:])
        added(next_out, small, dst_refs[0], dst_refs[1:])

    outs = (
        shape((g.rows, g.width), f32),
        shape((g.batch, g.rows), bf16),
        shape((g.rows, g.width), f32),
        shape((g.batch, g.rows), f32),
    )
    operands = [src_own, *src_others, dst_own, dst_near, *dst_others]
    return call("totals", kernel, outs, operands, limit=12 * mib)


def per_device(n, src_emb, dst_emb, tile_dst, tile_count, beliefs, grad_next):
    g = Grid(n, *src_emb.shape, beliefs.shape[0])
    me = lax.axis_index("src").astype(jnp.int32).reshape(1)

    def swap(array, flip):
        return lax.ppermute(array, "src", [(i, i ^ flip) for i in range(n)])

    src_pack, dst_pack = pack(g, me, tile_dst, tile_count, src_emb, beliefs, dst_emb, grad_next)
    src_others = [swap(src_pack, g.row_flip(s)) for s in range(1, g.n_row)]
    packets = {t: swap(dst_pack, t) for t in reversed(g.early[1:])}
    src_kept, packets[0] = keep(src_pack, dst_pack)
    src_packs = [src_kept] + src_others
    first = g.early[1]
    for t in g.early[2:]:
        packets[t] = hand(packets[t], packets[first], src_kept)
    for t in sorted(g.late, key=lambda t: bin(t).count("1")):
        packets[t] = swap(packets[t ^ low_bit(t)], low_bit(t))
    stacks = []
    for k, slots in enumerate(g.groups):
        own = stack([packets[t] for t in slots], *(src_others if k == 1 else ()))
        stacks += [own, swap(own, 1)]

    scored = [scores(g, g.parts[0], src_packs, stacks[:4])]
    scored.append(scores(g, g.parts[1], src_packs, stacks[4:], scored[0][2]))
    probs, grad_sums, stats = zip(*scored)
    message = join(g, stats)
    messages = [message] + [swap(message, g.row_flip(s)) for s in range(1, g.n_row)]
    src_all, bel_all, *prob_grads = stage(g, src_packs, stacks)
    factors, belief_sum = norms(g, stats, grad_sums, messages)

    def columns(slots, kind, *after):
        return column_shares(g, slots, kind, factors, probs, prob_grads, src_all, bel_all, *after)

    odd_far, odd_near = ([t + 1 for t in slots] for slots in (g.far, g.near))
    change_of_far_odd, far_send = columns(odd_far, bf16)
    far_got = swap(far_send, 1)
    change_of_far, far_own = columns(g.far, f32, far_send)
    change_of_near_odd, near_send = columns(odd_near, bf16, far_own)
    near_got = swap(near_send, 1)
    change_of_near, near_own = columns(g.near, f32, near_send)
    changes = [change_of_far_odd, change_of_far, change_of_near_odd, change_of_near]
    order = [odd_far, g.far, odd_near, g.near]

    got = {t: [] for t in range(0, g.n_col, 2)}
    last = near_send
    for t in reversed(range(2, g.n_col, 2)):
        own, near, slots = (far_own, far_got, g.far) if t in g.far else (near_own, near_got, g.near)
        send = fold(own, near, slots.index(t), got[t], last)
        got[t ^ low_bit(t)].append(swap(send, low_bit(t)))
        if t == g.n_col - 2:
            rest = list(range(1, g.n_row))
            src_send = row_shares(g, rest, bf16, changes, order, stacks, belief_sum, send)
            src_got = [swap(one, g.row_flip(s)) for one, s in zip(src_send, rest)]
            (src_own,) = row_shares(g, [0], f32, changes, order, stacks, belief_sum, src_send[0])
        last = send
    grad_src, grad_belief, grad_dst, next_belief = totals(
        g, src_own, src_got, near_own, near_got, got[0][::-1]
    )
    return (next_belief, grad_belief, grad_src, grad_dst)


def solution(mesh):
    placed = (
        P(("groups", "src"), None),
        P(("groups", "src"), None),
        P(("groups", "src"), None),
        P(("groups", "src")),
        P("groups", "src"),
        P("groups", "src"),
    )
    return jax.shard_map(
        functools.partial(per_device, mesh.shape["src"]),
        mesh=mesh,
        in_specs=placed,
        out_specs=(
            P("groups", "src"),
            P("groups", "src"),
            P(("groups", "src"), None),
            P(("groups", "src"), None),
        ),
        check_vma=False,
    )
```

```python
import functools

import jax
import jax.numpy as jnp
from jax import lax
from jax.experimental import pallas as pl
from jax.experimental.pallas import tpu as pltpu
from jax.sharding import PartitionSpec as P

f32 = jnp.float32
bf16 = jnp.bfloat16
unlisted = 1e30
mib = 1 << 20


class Grid:
    def __init__(self, n, rows, width, batch):
        bits = n.bit_length() - 1
        row_bits = max(1, bits // 2 - 1)
        self.n, self.rows, self.width, self.batch = n, rows, width, batch
        self.n_row = 1 << row_bits
        self.n_col = n // self.n_row
        self.span = self.n_row * rows
        self.packet = rows + batch
        self.head = (3 * self.n_row + 7) // 8 * 8
        even = range(0, self.n_col, 2)
        self.early = [t for t in even if t & (t - 1) == 0]
        self.late = [t for t in even if t & (t - 1)]
        self.groups = [self.early[2:], [2], [0], self.late]
        both = [group + [t + 1 for t in group] for group in self.groups]
        self.parts = [both[0] + both[1] + both[2], both[3]]
        self.spots = {t: (2 * k + (t & 1), group.index(t & ~1)) for k, group in enumerate(self.groups) for t in both[k]}
        top = self.n_col // 2
        self.far = [t for t in range(top, self.n_col, 2)]
        self.near = [t for t in range(0, top, 2)]

    def row_flip(self, s):
        return s * self.n_col

    def where(self, t):
        part = 0 if t in self.parts[0] else 1
        return part, self.parts[part].index(t)


def low_bit(t):
    return t & -t


def dot(a, b, dims):
    return lax.dot_general(a, b, (dims, ((), ())), preferred_element_type=f32)


NN = ((1,), (0,))
NT = ((1,), (1,))
TN = ((0,), (0,))


def in_vmem():
    return pl.BlockSpec(memory_space=pltpu.VMEM)


def anywhere():
    return pl.BlockSpec(memory_space=pl.ANY)


def in_smem():
    return pl.BlockSpec(memory_space=pltpu.SMEM)


shape = jax.ShapeDtypeStruct


def call(name, kernel, out_shape, operands, after=(), scratch=(), limit=8 * mib):
    many = isinstance(out_shape, tuple)
    return pl.pallas_call(
        kernel,
        out_shape=out_shape,
        in_specs=[in_vmem()] * len(operands) + [anywhere()] * len(after),
        out_specs=(in_vmem(),) * len(out_shape) if many else in_vmem(),
        scratch_shapes=list(scratch),
        compiler_params=pltpu.CompilerParams(vmem_limit_bytes=limit),
        name=name,
    )(*operands, *after)


def pack_kernel(g, me_ref, tile_ref, count_ref, src_ref, bel_ref, dst_ref, grad_ref, src_pack, dst_pack, flags):
    rows, batch = g.rows, g.batch
    me = me_ref[0]
    for k in range(g.n):
        flags[pl.ds(tile_ref[0, k] ^ me, 1), :] = jnp.broadcast_to(
            jnp.where(k < count_ref[0], 1.0, 0.0), (1, g.width)
        ).astype(f32)
    src_pack[:rows] = src_ref[...]
    src_pack[rows : rows + batch] = bel_ref[...]
    src_pack[rows + batch :] = flags[...].astype(bf16)
    dst_pack[:rows] = dst_ref[...]
    dst_pack[rows:] = grad_ref[...]


def pack(g, me, tile_dst, tile_count, src_emb, beliefs, dst_emb, grad_next):
    return pl.pallas_call(
        functools.partial(pack_kernel, g),
        out_shape=(
            shape((g.rows + g.batch + g.n, g.width), bf16),
            shape((g.rows + g.batch, g.width), bf16),
        ),
        in_specs=[in_smem()] * 3 + [in_vmem()] * 4,
        out_specs=(in_vmem(),) * 2,
        scratch_shapes=[pltpu.VMEM((g.n, g.width), f32)],
        compiler_params=pltpu.CompilerParams(vmem_limit_bytes=60 * mib),
        name="pack",
    )(me, tile_dst, tile_count, src_emb, beliefs, dst_emb, grad_next)


def keep(src_pack, dst_pack):
    def kernel(src_ref, dst_ref, src_out, dst_out):
        src_out[...] = src_ref[...]
        dst_out[...] = dst_ref[...]

    outs = (shape(src_pack.shape, bf16), shape(dst_pack.shape, bf16))
    return call("keep", kernel, outs, [src_pack, dst_pack], limit=2 * mib)


def hand(one, *after):
    def kernel(one_ref, *refs):
        refs[-1][...] = one_ref[...]

    return call("hand", kernel, shape(one.shape, one.dtype), [one], after, limit=2 * mib)


def paired(block, small, *after):
    def kernel(block_ref, small_ref, *refs):
        refs[-1][: block.shape[0]] = block_ref[...]
        refs[-1][block.shape[0] :] = small_ref[...]

    out = shape((block.shape[0] + small.shape[0], block.shape[1]), bf16)
    return call("paired", kernel, out, [block, small], after, limit=2 * mib)


def stack(packs, *after):
    def kernel(*refs):
        for i in range(len(packs)):
            refs[-1][i] = refs[i][...]

    out = shape((len(packs),) + packs[0].shape, packs[0].dtype)
    return call("stack", kernel, out, packs, after)


def score_kernel(g, row_slots, slots, *refs):
    rows, batch, span = g.rows, g.batch, len(row_slots) * g.rows
    src_packs, stacks = refs[: len(row_slots)], refs[len(row_slots) :]
    prob_ref, grad_sum, stats, src_all, bel_all = refs[-5:]
    first = g.spots[slots[0]][0]
    listed = []
    for p, one in enumerate(src_packs):
        lanes = slice(p * rows, (p + 1) * rows)
        src_all[lanes] = one[:rows]
        bel_all[:, lanes] = one[rows : rows + batch]
        listed.append((one[rows + batch :].astype(f32) - 1.0) * unlisted)

    def packet(t):
        stack, place = g.spots[t]
        return stacks[stack - first].at[place]

    top = jnp.full((8, span), -unlisted, f32)
    for i, t in enumerate(slots):
        flips = [g.row_flip(s) | t for s in row_slots]
        bias = jnp.concatenate([one[v : v + 1] for one, v in zip(listed, flips)], axis=1)
        logits = dot(packet(t)[:rows], src_all[...], NT) + bias
        prob_ref[i * rows : (i + 1) * rows] = logits
        top = jnp.maximum(top, jnp.max(logits.reshape(rows // 8, 8, span), axis=0))
    top = jnp.max(top, axis=0, keepdims=True)
    total = jnp.zeros((8, span), f32)
    grad_sum[...] = jnp.zeros(grad_sum.shape, f32)
    for i, t in enumerate(slots):
        here = slice(i * rows, (i + 1) * rows)
        prob = jnp.exp(prob_ref[here] - top)
        prob_ref[here] = prob
        grad_sum[...] += dot(packet(t)[rows:], prob.astype(bf16), NN)
        total = total + jnp.sum(prob.reshape(rows // 8, 8, span), axis=0)
    stats[0:1] = top
    stats[1:2] = jnp.sum(total, axis=0, keepdims=True)
    stats[2:3] = jnp.sum(bel_all[...].astype(f32) * grad_sum[...], axis=0, keepdims=True)


def scores(g, row_slots, slots, src_packs, stacks, *after):
    tall, span = len(slots) * g.rows, len(row_slots) * g.rows
    outs = (shape((tall, span), f32), shape((g.batch, span), f32), shape((3, span), f32))
    scratch = [pltpu.VMEM((span, g.width), bf16), pltpu.VMEM((g.batch, span), bf16)]
    kernel = functools.partial(score_kernel, g, row_slots, slots)
    operands = [*[src_packs[s] for s in row_slots], *stacks]
    return call("scores", kernel, outs, operands, after, scratch, tall * span * 8 + 6 * mib)


def flat(parts):
    return [one for part in parts for one in part]


def unflat(refs, parts):
    out = []
    for part in parts:
        out.append(refs[: len(part)])
        refs = refs[len(part) :]
    return out, refs


def wide(refs, here=slice(None)):
    return jnp.concatenate([one[here] for one in refs], axis=1)


def merged(stats):
    tops = [one[0:1] for one in stats]
    top = functools.reduce(jnp.maximum, tops)
    factors = [jnp.exp(one - top) for one in tops]
    total = sum(factor * one[1:2] for factor, one in zip(factors, stats))
    dots = sum(factor * one[2:3] for factor, one in zip(factors, stats))
    return top, total, dots


def join(g, stats):
    def kernel(*refs):
        out = refs[-1]
        parts, _ = unflat(refs, stats)
        for kind, value in enumerate(merged([wide(one) for one in parts])):
            for s in range(g.n_row):
                at = kind * g.n_row + s
                out[at : at + 1] = value[:, s * g.rows : (s + 1) * g.rows]
        if g.head > 3 * g.n_row:
            out[3 * g.n_row :] = jnp.zeros((g.head - 3 * g.n_row, g.rows), f32)

    return call("join", kernel, shape((g.head, g.rows), f32), flat(stats), limit=2 * mib)


def stage(g, src_packs, stacks):
    rows, batch = g.rows, g.batch

    def kernel(*refs):
        src_refs, stack_refs = refs[: g.n_row], refs[g.n_row : -4]
        src_all, bel_all, *prob_grads = refs[-4:]
        for s, one in enumerate(src_refs):
            lanes = slice(s * rows, (s + 1) * rows)
            src_all[lanes] = one[:rows]
            bel_all[:, lanes] = one[rows : rows + batch]
        for slots, out in zip(g.parts, prob_grads):
            for i, t in enumerate(slots):
                stack, place = g.spots[t]
                out[i * rows : (i + 1) * rows] = dot(stack_refs[stack][place, rows:], bel_all[...], TN)

    outs = (
        shape((g.span, g.width), bf16),
        shape((batch, g.span), bf16),
        *[shape((len(part) * rows, g.span), f32) for part in g.parts],
    )
    limit = g.n * rows * rows * 4 + 8 * mib
    return call("stage", kernel, outs, [*src_packs, *stacks], limit=limit)


def norms(g, stats, grad_sums, messages):
    def kernel(*refs):
        part_stats, refs = unflat(refs, stats)
        part_sums, refs = unflat(refs, grad_sums)
        everyone, (factors, belief_sum) = refs[: g.n_row], refs[-2:]
        part_stats = [wide(one) for one in part_stats]
        for s in range(g.n_row):
            lanes = slice(s * g.rows, (s + 1) * g.rows)

            def row(u, kind):
                at = kind * g.n_row + (s ^ u)
                return everyone[u][at : at + 1]

            tops = [row(u, 0) for u in range(g.n_row)]
            top = functools.reduce(jnp.maximum, tops)
            shares = [jnp.exp(one - top) for one in tops]
            inverse = 1.0 / sum(share * row(u, 1) for u, share in enumerate(shares))
            for part, one in enumerate(part_stats):
                factors[part : part + 1, lanes] = jnp.exp(one[0:1, lanes] - top) * inverse
            dots = sum(share * row(u, 2) for u, share in enumerate(shares))
            factors[2:3, lanes] = dots * inverse
        belief_sum[...] = wide(part_sums[0]) * factors[0:1] + wide(part_sums[1]) * factors[1:2]

    outs = (shape((8, g.span), f32), shape((g.batch, g.span), f32))
    return call("norms", kernel, outs, [*flat(stats), *flat(grad_sums), *messages], limit=4 * mib)


def column_shares(g, slots, kind, factors, probs, prob_grads, src_all, bel_all, *after):
    rows = g.rows

    def kernel(factors, *refs):
        prob_refs, refs = unflat(refs, probs)
        prob_grads, (src_all, bel_all), (change_ref, share_ref) = refs[:2], refs[2:4], refs[-2:]
        for i, t in enumerate(slots):
            part, place = g.where(t)
            here = slice(place * rows, (place + 1) * rows)
            prob = wide(prob_refs[part], here) * factors[part : part + 1]
            change = (prob * (prob_grads[part][here] - factors[2:3])).astype(bf16)
            change_ref[i * rows : (i + 1) * rows] = change
            share_ref[i, :rows] = dot(change, src_all[...], NN).astype(kind)
            share_ref[i, rows:] = dot(bel_all[...], prob.astype(bf16), NT).astype(kind)

    outs = (
        shape((len(slots) * rows, g.span), bf16),
        shape((len(slots), g.packet, g.width), kind),
    )
    operands = [factors, *flat(probs), *prob_grads, src_all, bel_all]
    return call("column_shares", kernel, outs, operands, after, limit=g.n * rows * rows * 8 + 6 * mib)


def row_shares(g, slots, kind, changes, order, stacks, belief_sum, *after):
    rows = g.rows

    def kernel(*refs):
        changes = refs[: len(order)]
        stack_refs = refs[len(order) : len(order) + len(stacks)]
        belief_sum = refs[len(order) + len(stacks)]
        for s, out in zip(slots, refs[-len(slots) :]):
            lanes = slice(s * rows, (s + 1) * rows)
            total = 0.0
            for change, columns in zip(changes, order):
                for i, t in enumerate(columns):
                    stack, place = g.spots[t]
                    packet = stack_refs[stack][place, :rows]
                    total = total + dot(change[i * rows : (i + 1) * rows, lanes], packet, TN)
            out[:rows] = total.astype(kind)
            out[rows:] = belief_sum[:, lanes].astype(kind)

    outs = (shape((g.packet, g.width), kind),) * len(slots)
    operands = [*changes, *stacks, belief_sum]
    return call("row_shares", kernel, outs, operands, after, limit=g.n * rows * rows * 4 + 6 * mib)


def fold(own, near, i, others, *after):
    def kernel(own_ref, near_ref, *refs):
        total = own_ref[i] + near_ref[i].astype(f32)
        for one in refs[: len(others)]:
            total = total + one[...].astype(f32)
        refs[-1][...] = total.astype(bf16)

    return call("fold", kernel, shape(own.shape[1:], bf16), [own, near, *others], after)


def totals(g, src_own, src_others, dst_own, dst_near, dst_others):
    def kernel(*refs):
        src_out, belief_out, dst_out, next_out = refs[-4:]
        src_refs, dst_refs = refs[: 1 + len(src_others)], refs[1 + len(src_others) : -4]

        def added(out, here, own, others):
            total = own[here] + sum(one[here].astype(f32) for one in others)
            out[...] = total.astype(out.dtype)

        big, small = slice(0, g.rows), slice(g.rows, g.packet)
        dst_refs = [dst_refs[0].at[0], dst_refs[1].at[0], *dst_refs[2:]]
        added(src_out, big, src_refs[0], src_refs[1:])
        added(belief_out, small, src_refs[0], src_refs[1:])
        added(dst_out, big, dst_refs[0], dst_refs[1:])
        added(next_out, small, dst_refs[0], dst_refs[1:])

    outs = (
        shape((g.rows, g.width), f32),
        shape((g.batch, g.rows), bf16),
        shape((g.rows, g.width), f32),
        shape((g.batch, g.rows), f32),
    )
    operands = [src_own, *src_others, dst_own, dst_near, *dst_others]
    return call("totals", kernel, outs, operands, limit=12 * mib)


def per_device(n, src_emb, dst_emb, tile_dst, tile_count, beliefs, grad_next):
    g = Grid(n, *src_emb.shape, beliefs.shape[0])
    me = lax.axis_index("src").astype(jnp.int32).reshape(1)

    def swap(array, flip):
        return lax.ppermute(array, "src", [(i, i ^ flip) for i in range(n)])

    raw = {t: (swap(dst_emb, t), swap(grad_next, t)) for t in g.early[2:]}
    src_pack, dst_pack = pack(g, me, tile_dst, tile_count, src_emb, beliefs, dst_emb, grad_next)
    src_others = [swap(src_pack, g.row_flip(s)) for s in range(1, g.n_row)]
    src_kept, dst_kept = keep(src_pack, dst_pack)
    src_packs = [src_kept] + src_others
    packets = {0: dst_kept, 2: swap(dst_pack, 2)}
    for t, (block, small) in raw.items():
        packets[t] = paired(block, small, src_kept)
    for t in sorted(g.late, key=lambda t: bin(t).count("1")):
        packets[t] = swap(packets[t ^ low_bit(t)], low_bit(t))
    stacks = []
    for k, slots in enumerate(g.groups):
        own = stack([packets[t] for t in slots], *(src_others if k == 1 else ()))
        stacks += [own, swap(own, 1)]

    own, others = [0], list(range(1, g.n_row))
    scored = [scores(g, own, g.parts[0], src_packs, stacks[:-2])]
    scored.append(scores(g, others, g.parts[0], src_packs, stacks[:-2], scored[0][2]))
    scored.append(scores(g, own + others, g.parts[1], src_packs, stacks[-2:], scored[1][2]))
    probs, grad_sums, stats = ([list(each[:2]), list(each[2:])] for each in zip(*scored))
    message = join(g, stats)
    messages = [message] + [swap(message, g.row_flip(s)) for s in range(1, g.n_row)]
    src_all, bel_all, *prob_grads = stage(g, src_packs, stacks)
    factors, belief_sum = norms(g, stats, grad_sums, messages)

    def columns(slots, kind, *after):
        return column_shares(g, slots, kind, factors, probs, prob_grads, src_all, bel_all, *after)

    odd_far, odd_near = ([t + 1 for t in slots] for slots in (g.far, g.near))
    change_of_far_odd, far_send = columns(odd_far, bf16)
    far_got = swap(far_send, 1)
    change_of_far, far_own = columns(g.far, f32, far_send)
    change_of_near_odd, near_send = columns(odd_near, bf16, far_own)
    near_got = swap(near_send, 1)
    change_of_near, near_own = columns(g.near, f32, near_send)
    changes = [change_of_far_odd, change_of_far, change_of_near_odd, change_of_near]
    order = [odd_far, g.far, odd_near, g.near]

    got = {t: [] for t in range(0, g.n_col, 2)}
    last = near_send
    for t in reversed(range(2, g.n_col, 2)):
        own, near, slots = (far_own, far_got, g.far) if t in g.far else (near_own, near_got, g.near)
        send = fold(own, near, slots.index(t), got[t], last)
        one = swap(send, low_bit(t))
        got[t ^ low_bit(t)].append(hand(one) if low_bit(t) > 2 else one)
        if t == g.n_col - 2:
            rest = list(range(1, g.n_row))
            src_send = row_shares(g, rest, bf16, changes, order, stacks, belief_sum, send)
            src_got = [swap(one, g.row_flip(s)) for one, s in zip(src_send, rest)]
        elif t == 4:
            (src_own,) = row_shares(g, [0], f32, changes, order, stacks, belief_sum, send)
            send = src_own
        last = send
    grad_src, grad_belief, grad_dst, next_belief = totals(
        g, src_own, src_got, near_own, near_got, got[0]
    )
    return (next_belief, grad_belief, grad_src, grad_dst)


def solution(mesh):
    placed = (
        P(("groups", "src"), None),
        P(("groups", "src"), None),
        P(("groups", "src"), None),
        P(("groups", "src")),
        P("groups", "src"),
        P("groups", "src"),
    )
    return jax.shard_map(
        functools.partial(per_device, mesh.shape["src"]),
        mesh=mesh,
        in_specs=placed,
        out_specs=(
            P("groups", "src"),
            P("groups", "src"),
            P(("groups", "src"), None),
            P(("groups", "src"), None),
        ),
        check_vma=False,
    )
```

```python
import functools

import jax
import jax.numpy as jnp
from jax import lax
from jax.experimental import pallas as pl
from jax.experimental.pallas import tpu as pltpu
from jax.sharding import PartitionSpec as P

f32 = jnp.float32
bf16 = jnp.bfloat16
unlisted = 1e30
mib = 1 << 20


class Grid:
    def __init__(self, n, rows, width, batch):
        bits = n.bit_length() - 1
        row_bits = max(1, bits // 2 - 1)
        self.n, self.rows, self.width, self.batch = n, rows, width, batch
        self.n_row = 1 << row_bits
        self.n_col = n // self.n_row
        self.span = self.n_row * rows
        self.packet = rows + batch
        self.head = (3 * self.n_row + 7) // 8 * 8
        even = range(0, self.n_col, 2)
        self.early = [t for t in even if t & (t - 1) == 0]
        self.late = [t for t in even if t & (t - 1)]
        self.groups = [self.early[2:], [2], [0], self.late]
        both = [group + [t + 1 for t in group] for group in self.groups]
        self.parts = [both[0] + both[1] + both[2], both[3]]
        self.spots = {t: (2 * k + (t & 1), group.index(t & ~1)) for k, group in enumerate(self.groups) for t in both[k]}
        top = self.n_col // 2
        self.far = [t for t in range(top, self.n_col, 2)]
        self.near = [t for t in range(0, top, 2)]

    def row_flip(self, s):
        return s * self.n_col

    def where(self, t):
        part = 0 if t in self.parts[0] else 1
        return part, self.parts[part].index(t)


def low_bit(t):
    return t & -t


def dot(a, b, dims):
    return lax.dot_general(a, b, (dims, ((), ())), preferred_element_type=f32)


NN = ((1,), (0,))
NT = ((1,), (1,))
TN = ((0,), (0,))


def in_vmem():
    return pl.BlockSpec(memory_space=pltpu.VMEM)


def anywhere():
    return pl.BlockSpec(memory_space=pl.ANY)


def in_smem():
    return pl.BlockSpec(memory_space=pltpu.SMEM)


shape = jax.ShapeDtypeStruct


def call(name, kernel, out_shape, operands, after=(), scratch=(), limit=8 * mib):
    many = isinstance(out_shape, tuple)
    return pl.pallas_call(
        kernel,
        out_shape=out_shape,
        in_specs=[in_vmem()] * len(operands) + [anywhere()] * len(after),
        out_specs=(in_vmem(),) * len(out_shape) if many else in_vmem(),
        scratch_shapes=list(scratch),
        compiler_params=pltpu.CompilerParams(vmem_limit_bytes=limit),
        name=name,
    )(*operands, *after)


def pack_kernel(g, tile_ref, count_ref, src_ref, bel_ref, dst_ref, grad_ref, src_pack, dst_pack, flags):
    rows, batch = g.rows, g.batch
    me = lax.axis_index("src")
    count = jnp.broadcast_to(count_ref[...], (1, g.width))
    for k in range(g.n):
        flags[pl.ds(tile_ref[0, k] ^ me, 1), :] = jnp.where(count > k, 1.0, 0.0).astype(f32)
    src_pack[:rows] = src_ref[...]
    src_pack[rows : rows + batch] = bel_ref[...]
    src_pack[rows + batch :] = flags[...].astype(bf16)
    dst_pack[:rows] = dst_ref[...]
    dst_pack[rows:] = grad_ref[...]


def pack(g, tile_dst, tile_count, src_emb, beliefs, dst_emb, grad_next):
    return pl.pallas_call(
        functools.partial(pack_kernel, g),
        out_shape=(
            shape((g.rows + g.batch + g.n, g.width), bf16),
            shape((g.rows + g.batch, g.width), bf16),
        ),
        in_specs=[in_smem()] + [in_vmem()] * 5,
        out_specs=(in_vmem(),) * 2,
        scratch_shapes=[pltpu.VMEM((g.n, g.width), f32)],
        compiler_params=pltpu.CompilerParams(vmem_limit_bytes=60 * mib),
        name="pack",
    )(tile_dst, tile_count.reshape(1, 1), src_emb, beliefs, dst_emb, grad_next)


def keep(src_pack, dst_pack, *after):
    def kernel(src_ref, dst_ref, *refs):
        refs[-2][...] = src_ref[...]
        refs[-1][...] = dst_ref[...]

    outs = (shape(src_pack.shape, bf16), shape(dst_pack.shape, bf16))
    return call("keep", kernel, outs, [src_pack, dst_pack], after, limit=2 * mib)


def hand(one, *after):
    def kernel(one_ref, *refs):
        refs[-1][...] = one_ref[...]

    return call("hand", kernel, shape(one.shape, one.dtype), [one], after, limit=2 * mib)


def paired(block, small, *after):
    def kernel(block_ref, small_ref, *refs):
        refs[-1][: block.shape[0]] = block_ref[...]
        refs[-1][block.shape[0] :] = small_ref[...]

    out = shape((block.shape[0] + small.shape[0], block.shape[1]), bf16)
    return call("paired", kernel, out, [block, small], after, limit=2 * mib)


def stack(packs, *after):
    def kernel(*refs):
        for i in range(len(packs)):
            refs[-1][i] = refs[i][...]

    out = shape((len(packs),) + packs[0].shape, packs[0].dtype)
    return call("stack", kernel, out, packs, after)


def score_kernel(g, row_slots, slots, *refs):
    rows, batch, span = g.rows, g.batch, len(row_slots) * g.rows
    src_packs, stacks = refs[: len(row_slots)], refs[len(row_slots) :]
    prob_ref, grad_sum, stats, src_all, bel_all = refs[-5:]
    first = g.spots[slots[0]][0]
    listed = []
    for p, one in enumerate(src_packs):
        lanes = slice(p * rows, (p + 1) * rows)
        src_all[lanes] = one[:rows]
        bel_all[:, lanes] = one[rows : rows + batch]
        listed.append((one[rows + batch :].astype(f32) - 1.0) * unlisted)

    def packet(t):
        stack, place = g.spots[t]
        return stacks[stack - first].at[place]

    top = jnp.full((8, span), -unlisted, f32)
    for i, t in enumerate(slots):
        flips = [g.row_flip(s) | t for s in row_slots]
        bias = jnp.concatenate([one[v : v + 1] for one, v in zip(listed, flips)], axis=1)
        logits = dot(packet(t)[:rows], src_all[...], NT) + bias
        prob_ref[i * rows : (i + 1) * rows] = logits
        top = jnp.maximum(top, jnp.max(logits.reshape(rows // 8, 8, span), axis=0))
    top = jnp.max(top, axis=0, keepdims=True)
    total = jnp.zeros((8, span), f32)
    grad_sum[...] = jnp.zeros(grad_sum.shape, f32)
    for i, t in enumerate(slots):
        here = slice(i * rows, (i + 1) * rows)
        prob = jnp.exp(prob_ref[here] - top)
        prob_ref[here] = prob
        grad_sum[...] += dot(packet(t)[rows:], prob.astype(bf16), NN)
        total = total + jnp.sum(prob.reshape(rows // 8, 8, span), axis=0)
    stats[0:1] = top
    stats[1:2] = jnp.sum(total, axis=0, keepdims=True)
    stats[2:3] = jnp.sum(bel_all[...].astype(f32) * grad_sum[...], axis=0, keepdims=True)


def scores(g, row_slots, slots, src_packs, stacks, *after):
    tall, span = len(slots) * g.rows, len(row_slots) * g.rows
    outs = (shape((tall, span), f32), shape((g.batch, span), f32), shape((3, span), f32))
    scratch = [pltpu.VMEM((span, g.width), bf16), pltpu.VMEM((g.batch, span), bf16)]
    kernel = functools.partial(score_kernel, g, row_slots, slots)
    operands = [*[src_packs[s] for s in row_slots], *stacks]
    return call("scores", kernel, outs, operands, after, scratch, tall * span * 8 + 6 * mib)


def flat(parts):
    return [one for part in parts for one in part]


def unflat(refs, parts):
    out = []
    for part in parts:
        out.append(refs[: len(part)])
        refs = refs[len(part) :]
    return out, refs


def wide(refs, here=slice(None)):
    return jnp.concatenate([one[here] for one in refs], axis=1)


def merged(stats):
    tops = [one[0:1] for one in stats]
    top = functools.reduce(jnp.maximum, tops)
    factors = [jnp.exp(one - top) for one in tops]
    total = sum(factor * one[1:2] for factor, one in zip(factors, stats))
    dots = sum(factor * one[2:3] for factor, one in zip(factors, stats))
    return top, total, dots


def join(g, stats):
    def kernel(*refs):
        out = refs[-1]
        parts, _ = unflat(refs, stats)
        for kind, value in enumerate(merged([wide(one) for one in parts])):
            for s in range(g.n_row):
                at = kind * g.n_row + s
                out[at : at + 1] = value[:, s * g.rows : (s + 1) * g.rows]
        if g.head > 3 * g.n_row:
            out[3 * g.n_row :] = jnp.zeros((g.head - 3 * g.n_row, g.rows), f32)

    return call("join", kernel, shape((g.head, g.rows), f32), flat(stats), limit=2 * mib)


def stage(g, src_packs, stacks):
    rows, batch = g.rows, g.batch

    def kernel(*refs):
        src_refs, stack_refs = refs[: g.n_row], refs[g.n_row : -4]
        src_all, bel_all, *prob_grads = refs[-4:]
        for s, one in enumerate(src_refs):
            lanes = slice(s * rows, (s + 1) * rows)
            src_all[lanes] = one[:rows]
            bel_all[:, lanes] = one[rows : rows + batch]
        for slots, out in zip(g.parts, prob_grads):
            for i, t in enumerate(slots):
                stack, place = g.spots[t]
                out[i * rows : (i + 1) * rows] = dot(stack_refs[stack][place, rows:], bel_all[...], TN)

    outs = (
        shape((g.span, g.width), bf16),
        shape((batch, g.span), bf16),
        *[shape((len(part) * rows, g.span), f32) for part in g.parts],
    )
    limit = g.n * rows * rows * 4 + 8 * mib
    return call("stage", kernel, outs, [*src_packs, *stacks], limit=limit)


def norms(g, stats, grad_sums, messages):
    def kernel(*refs):
        part_stats, refs = unflat(refs, stats)
        part_sums, refs = unflat(refs, grad_sums)
        everyone, (factors, belief_sum) = refs[: g.n_row], refs[-2:]
        part_stats = [wide(one) for one in part_stats]
        for s in range(g.n_row):
            lanes = slice(s * g.rows, (s + 1) * g.rows)

            def row(u, kind):
                at = kind * g.n_row + (s ^ u)
                return everyone[u][at : at + 1]

            tops = [row(u, 0) for u in range(g.n_row)]
            top = functools.reduce(jnp.maximum, tops)
            shares = [jnp.exp(one - top) for one in tops]
            inverse = 1.0 / sum(share * row(u, 1) for u, share in enumerate(shares))
            for part, one in enumerate(part_stats):
                factors[part : part + 1, lanes] = jnp.exp(one[0:1, lanes] - top) * inverse
            dots = sum(share * row(u, 2) for u, share in enumerate(shares))
            factors[2:3, lanes] = dots * inverse
        belief_sum[...] = wide(part_sums[0]) * factors[0:1] + wide(part_sums[1]) * factors[1:2]

    outs = (shape((8, g.span), f32), shape((g.batch, g.span), f32))
    return call("norms", kernel, outs, [*flat(stats), *flat(grad_sums), *messages], limit=4 * mib)


def column_shares(g, slots, kind, factors, probs, prob_grads, src_all, bel_all, *after):
    rows = g.rows

    def kernel(factors, *refs):
        prob_refs, refs = unflat(refs, probs)
        prob_grads, (src_all, bel_all), (change_ref, share_ref) = refs[:2], refs[2:4], refs[-2:]
        for i, t in enumerate(slots):
            part, place = g.where(t)
            here = slice(place * rows, (place + 1) * rows)
            prob = wide(prob_refs[part], here) * factors[part : part + 1]
            change = (prob * (prob_grads[part][here] - factors[2:3])).astype(bf16)
            change_ref[i * rows : (i + 1) * rows] = change
            share_ref[i, :rows] = dot(change, src_all[...], NN).astype(kind)
            share_ref[i, rows:] = dot(bel_all[...], prob.astype(bf16), NT).astype(kind)

    outs = (
        shape((len(slots) * rows, g.span), bf16),
        shape((len(slots), g.packet, g.width), kind),
    )
    operands = [factors, *flat(probs), *prob_grads, src_all, bel_all]
    return call("column_shares", kernel, outs, operands, after, limit=g.n * rows * rows * 8 + 6 * mib)


def row_shares(g, slots, kind, changes, order, stacks, belief_sum, *after):
    rows = g.rows

    def kernel(*refs):
        changes = refs[: len(order)]
        stack_refs = refs[len(order) : len(order) + len(stacks)]
        belief_sum = refs[len(order) + len(stacks)]
        for s, out in zip(slots, refs[-len(slots) :]):
            lanes = slice(s * rows, (s + 1) * rows)
            total = 0.0
            for change, columns in zip(changes, order):
                for i, t in enumerate(columns):
                    stack, place = g.spots[t]
                    packet = stack_refs[stack][place, :rows]
                    total = total + dot(change[i * rows : (i + 1) * rows, lanes], packet, TN)
            out[:rows] = total.astype(kind)
            out[rows:] = belief_sum[:, lanes].astype(kind)

    outs = (shape((g.packet, g.width), kind),) * len(slots)
    operands = [*changes, *stacks, belief_sum]
    return call("row_shares", kernel, outs, operands, after, limit=g.n * rows * rows * 4 + 6 * mib)


def fold(own, near, i, others, *after):
    def kernel(own_ref, near_ref, *refs):
        total = own_ref[i] + near_ref[i].astype(f32)
        for one in refs[: len(others)]:
            total = total + one[...].astype(f32)
        refs[-1][...] = total.astype(bf16)

    return call("fold", kernel, shape(own.shape[1:], bf16), [own, near, *others], after)


def totals(g, src_own, src_others, dst_own, dst_near, dst_others):
    def kernel(*refs):
        src_out, belief_out, dst_out, next_out = refs[-4:]
        src_refs, dst_refs = refs[: 1 + len(src_others)], refs[1 + len(src_others) : -4]

        def added(out, here, own, others):
            total = own[here] + sum(one[here].astype(f32) for one in others)
            out[...] = total.astype(out.dtype)

        big, small = slice(0, g.rows), slice(g.rows, g.packet)
        dst_refs = [dst_refs[0].at[0], dst_refs[1].at[0], *dst_refs[2:]]
        added(src_out, big, src_refs[0], src_refs[1:])
        added(belief_out, small, src_refs[0], src_refs[1:])
        added(dst_out, big, dst_refs[0], dst_refs[1:])
        added(next_out, small, dst_refs[0], dst_refs[1:])

    outs = (
        shape((g.rows, g.width), f32),
        shape((g.batch, g.rows), bf16),
        shape((g.rows, g.width), f32),
        shape((g.batch, g.rows), f32),
    )
    operands = [src_own, *src_others, dst_own, dst_near, *dst_others]
    return call("totals", kernel, outs, operands, limit=12 * mib)


def per_device(n, src_emb, dst_emb, tile_dst, tile_count, beliefs, grad_next):
    g = Grid(n, *src_emb.shape, beliefs.shape[0])

    def swap(array, flip):
        return lax.ppermute(array, "src", [(i, i ^ flip) for i in range(n)])

    raw = {t: (swap(dst_emb, t), swap(grad_next, t)) for t in g.early[2:]}
    src_pack, dst_pack = pack(g, tile_dst, tile_count, src_emb, beliefs, dst_emb, grad_next)
    src_others = [swap(src_pack, g.row_flip(s)) for s in range(1, g.n_row)]
    packets = {2: swap(dst_pack, 2)}
    for t, (block, small) in raw.items():
        packets[t] = paired(block, small)
    src_kept, packets[0] = keep(src_pack, dst_pack, *[packets[t] for t in raw])
    src_packs = [src_kept] + src_others
    for t in sorted(g.late, key=lambda t: bin(t).count("1")):
        packets[t] = swap(packets[t ^ low_bit(t)], low_bit(t))
    stacks = []
    for k, slots in enumerate(g.groups):
        own = stack([packets[t] for t in slots], *(src_others if k == 1 else ()))
        stacks += [own, swap(own, 1)]

    own, others = [0], list(range(1, g.n_row))
    scored = [scores(g, own, g.parts[0], src_packs, stacks[:-2])]
    scored.append(scores(g, others, g.parts[0], src_packs, stacks[:-2], scored[0][2]))
    scored.append(scores(g, own + others, g.parts[1], src_packs, stacks[-2:], scored[1][2]))
    probs, grad_sums, stats = ([list(each[:2]), list(each[2:])] for each in zip(*scored))
    message = join(g, stats)
    messages = [message] + [swap(message, g.row_flip(s)) for s in range(1, g.n_row)]
    src_all, bel_all, *prob_grads = stage(g, src_packs, stacks)
    factors, belief_sum = norms(g, stats, grad_sums, messages)

    def columns(slots, kind, *after):
        return column_shares(g, slots, kind, factors, probs, prob_grads, src_all, bel_all, *after)

    odd_far, odd_near = ([t + 1 for t in slots] for slots in (g.far, g.near))
    change_of_far_odd, far_send = columns(odd_far, bf16)
    far_got = swap(far_send, 1)
    change_of_far, far_own = columns(g.far, f32, far_send)
    change_of_near_odd, near_send = columns(odd_near, bf16, far_own)
    near_got = swap(near_send, 1)
    change_of_near, near_own = columns(g.near, f32, near_send)
    changes = [change_of_far_odd, change_of_far, change_of_near_odd, change_of_near]
    order = [odd_far, g.far, odd_near, g.near]

    got = {t: [] for t in range(0, g.n_col, 2)}
    last = near_send
    for t in reversed(range(2, g.n_col, 2)):
        own, near, slots = (far_own, far_got, g.far) if t in g.far else (near_own, near_got, g.near)
        send = fold(own, near, slots.index(t), got[t], last)
        one = swap(send, low_bit(t))
        got[t ^ low_bit(t)].append(hand(one) if low_bit(t) > 2 else one)
        if t == g.n_col - 2:
            rest = list(range(1, g.n_row))
            src_send = row_shares(g, rest, bf16, changes, order, stacks, belief_sum, send)
            src_got = [swap(one, g.row_flip(s)) for one, s in zip(src_send, rest)]
        elif t == 4:
            (src_own,) = row_shares(g, [0], f32, changes, order, stacks, belief_sum, send)
            send = src_own
        last = send
    grad_src, grad_belief, grad_dst, next_belief = totals(
        g, src_own, src_got, near_own, near_got, got[0]
    )
    return (next_belief, grad_belief, grad_src, grad_dst)


def solution(mesh):
    placed = (
        P(("groups", "src"), None),
        P(("groups", "src"), None),
        P(("groups", "src"), None),
        P(("groups", "src")),
        P("groups", "src"),
        P("groups", "src"),
    )
    return jax.shard_map(
        functools.partial(per_device, mesh.shape["src"]),
        mesh=mesh,
        in_specs=placed,
        out_specs=(
            P("groups", "src"),
            P("groups", "src"),
            P(("groups", "src"), None),
            P(("groups", "src"), None),
        ),
        check_vma=False,
    )
```

```python
import functools

import jax
import jax.numpy as jnp
from jax import lax
from jax.experimental import pallas as pl
from jax.experimental.pallas import tpu as pltpu
from jax.sharding import PartitionSpec as P

f32 = jnp.float32
bf16 = jnp.bfloat16
unlisted = 1e30
mib = 1 << 20


class Grid:
    def __init__(self, n, rows, width, batch):
        bits = n.bit_length() - 1
        row_bits = max(1, bits // 2 - 1)
        self.n, self.rows, self.width, self.batch = n, rows, width, batch
        self.n_row = 1 << row_bits
        self.n_col = n // self.n_row
        self.span = self.n_row * rows
        self.packet = rows + batch
        self.head = (3 * self.n_row + 7) // 8 * 8
        even = range(0, self.n_col, 2)
        self.early = [t for t in even if t & (t - 1) == 0]
        self.late = [t for t in even if t & (t - 1)]
        self.groups = [self.early[2:], [2], [0], self.late]
        both = [group + [t + 1 for t in group] for group in self.groups]
        self.parts = [both[0] + both[1] + both[2], both[3]]
        self.spots = {t: (2 * k + (t & 1), group.index(t & ~1)) for k, group in enumerate(self.groups) for t in both[k]}
        top = self.n_col // 2
        self.far = [t for t in range(top, self.n_col, 2)]
        self.near = [t for t in range(0, top, 2)]

    def row_flip(self, s):
        return s * self.n_col

    def where(self, t):
        part = 0 if t in self.parts[0] else 1
        return part, self.parts[part].index(t)


def low_bit(t):
    return t & -t


def dot(a, b, dims):
    return lax.dot_general(a, b, (dims, ((), ())), preferred_element_type=f32)


NN = ((1,), (0,))
NT = ((1,), (1,))
TN = ((0,), (0,))


def in_vmem():
    return pl.BlockSpec(memory_space=pltpu.VMEM)


def anywhere():
    return pl.BlockSpec(memory_space=pl.ANY)


def in_smem():
    return pl.BlockSpec(memory_space=pltpu.SMEM)


shape = jax.ShapeDtypeStruct


def call(name, kernel, out_shape, operands, after=(), scratch=(), limit=8 * mib):
    many = isinstance(out_shape, tuple)
    return pl.pallas_call(
        kernel,
        out_shape=out_shape,
        in_specs=[in_vmem()] * len(operands) + [anywhere()] * len(after),
        out_specs=(in_vmem(),) * len(out_shape) if many else in_vmem(),
        scratch_shapes=list(scratch),
        compiler_params=pltpu.CompilerParams(vmem_limit_bytes=limit),
        name=name,
    )(*operands, *after)


def pack_kernel(g, tile_ref, count_ref, src_ref, bel_ref, dst_ref, grad_ref, src_pack, dst_pack, flags):
    rows, batch = g.rows, g.batch
    me = lax.axis_index("src")
    count = jnp.broadcast_to(count_ref[...], (1, g.width))
    for k in range(g.n):
        flags[pl.ds(tile_ref[0, k] ^ me, 1), :] = jnp.where(count > k, 1.0, 0.0).astype(f32)
    src_pack[:rows] = src_ref[...]
    src_pack[rows : rows + batch] = bel_ref[...]
    src_pack[rows + batch :] = flags[...].astype(bf16)
    dst_pack[:rows] = dst_ref[...]
    dst_pack[rows:] = grad_ref[...]


def pack(g, tile_dst, tile_count, src_emb, beliefs, dst_emb, grad_next):
    return pl.pallas_call(
        functools.partial(pack_kernel, g),
        out_shape=(
            shape((g.rows + g.batch + g.n, g.width), bf16),
            shape((g.rows + g.batch, g.width), bf16),
        ),
        in_specs=[in_smem()] + [in_vmem()] * 5,
        out_specs=(in_vmem(),) * 2,
        scratch_shapes=[pltpu.VMEM((g.n, g.width), f32)],
        compiler_params=pltpu.CompilerParams(vmem_limit_bytes=60 * mib),
        name="pack",
    )(tile_dst, tile_count.reshape(1, 1), src_emb, beliefs, dst_emb, grad_next)


def keep(src_pack, dst_pack, *after):
    def kernel(src_ref, dst_ref, *refs):
        refs[-2][...] = src_ref[...]
        refs[-1][...] = dst_ref[...]

    outs = (shape(src_pack.shape, bf16), shape(dst_pack.shape, bf16))
    return call("keep", kernel, outs, [src_pack, dst_pack], after, limit=2 * mib)


def hand(one, *after):
    def kernel(one_ref, *refs):
        refs[-1][...] = one_ref[...]

    return call("hand", kernel, shape(one.shape, one.dtype), [one], after, limit=2 * mib)


def paired(block, small, *after):
    def kernel(block_ref, small_ref, *refs):
        refs[-1][: block.shape[0]] = block_ref[...]
        refs[-1][block.shape[0] :] = small_ref[...]

    out = shape((block.shape[0] + small.shape[0], block.shape[1]), bf16)
    return call("paired", kernel, out, [block, small], after, limit=2 * mib)


def stack(packs, *after):
    def kernel(*refs):
        for i in range(len(packs)):
            refs[-1][i] = refs[i][...]

    out = shape((len(packs),) + packs[0].shape, packs[0].dtype)
    return call("stack", kernel, out, packs, after)


def score_kernel(g, row_slots, slots, *refs):
    rows, batch, span = g.rows, g.batch, len(row_slots) * g.rows
    src_packs, stacks = refs[: len(row_slots)], refs[len(row_slots) :]
    prob_ref, grad_sum, stats, src_all, bel_all = refs[-5:]
    first = g.spots[slots[0]][0]
    listed = []
    for p, one in enumerate(src_packs):
        lanes = slice(p * rows, (p + 1) * rows)
        src_all[lanes] = one[:rows]
        bel_all[:, lanes] = one[rows : rows + batch]
        listed.append((one[rows + batch :].astype(f32) - 1.0) * unlisted)

    def packet(t):
        stack, place = g.spots[t]
        return stacks[stack - first].at[place]

    top = jnp.full((8, span), -unlisted, f32)
    for i, t in enumerate(slots):
        flips = [g.row_flip(s) | t for s in row_slots]
        bias = jnp.concatenate([one[v : v + 1] for one, v in zip(listed, flips)], axis=1)
        logits = dot(packet(t)[:rows], src_all[...], NT) + bias
        prob_ref[i * rows : (i + 1) * rows] = logits
        top = jnp.maximum(top, jnp.max(logits.reshape(rows // 8, 8, span), axis=0))
    top = jnp.max(top, axis=0, keepdims=True)
    total = jnp.zeros((8, span), f32)
    grad_sum[...] = jnp.zeros(grad_sum.shape, f32)
    for i, t in enumerate(slots):
        here = slice(i * rows, (i + 1) * rows)
        prob = jnp.exp(prob_ref[here] - top)
        prob_ref[here] = prob
        grad_sum[...] += dot(packet(t)[rows:], prob.astype(bf16), NN)
        total = total + jnp.sum(prob.reshape(rows // 8, 8, span), axis=0)
    stats[0:1] = top
    stats[1:2] = jnp.sum(total, axis=0, keepdims=True)
    stats[2:3] = jnp.sum(bel_all[...].astype(f32) * grad_sum[...], axis=0, keepdims=True)


def scores(g, row_slots, slots, src_packs, stacks, *after):
    tall, span = len(slots) * g.rows, len(row_slots) * g.rows
    outs = (shape((tall, span), f32), shape((g.batch, span), f32), shape((3, span), f32))
    scratch = [pltpu.VMEM((span, g.width), bf16), pltpu.VMEM((g.batch, span), bf16)]
    kernel = functools.partial(score_kernel, g, row_slots, slots)
    operands = [*[src_packs[s] for s in row_slots], *stacks]
    return call("scores", kernel, outs, operands, after, scratch, tall * span * 8 + 6 * mib)


def flat(parts):
    return [one for part in parts for one in part]


def unflat(refs, parts):
    out = []
    for part in parts:
        out.append(refs[: len(part)])
        refs = refs[len(part) :]
    return out, refs


def wide(refs, here=slice(None)):
    return jnp.concatenate([one[here] for one in refs], axis=1)


def merged(stats):
    tops = [one[0:1] for one in stats]
    top = functools.reduce(jnp.maximum, tops)
    factors = [jnp.exp(one - top) for one in tops]
    total = sum(factor * one[1:2] for factor, one in zip(factors, stats))
    dots = sum(factor * one[2:3] for factor, one in zip(factors, stats))
    return top, total, dots


def join(g, stats):
    def kernel(*refs):
        out = refs[-1]
        parts, _ = unflat(refs, stats)
        for kind, value in enumerate(merged([wide(one) for one in parts])):
            for s in range(g.n_row):
                at = kind * g.n_row + s
                out[at : at + 1] = value[:, s * g.rows : (s + 1) * g.rows]
        if g.head > 3 * g.n_row:
            out[3 * g.n_row :] = jnp.zeros((g.head - 3 * g.n_row, g.rows), f32)

    return call("join", kernel, shape((g.head, g.rows), f32), flat(stats), limit=2 * mib)


def stage(g, src_packs, stacks):
    rows, batch = g.rows, g.batch

    def kernel(*refs):
        src_refs, stack_refs = refs[: g.n_row], refs[g.n_row : -4]
        src_all, bel_all, *prob_grads = refs[-4:]
        for s, one in enumerate(src_refs):
            lanes = slice(s * rows, (s + 1) * rows)
            src_all[lanes] = one[:rows]
            bel_all[:, lanes] = one[rows : rows + batch]
        for slots, out in zip(g.parts, prob_grads):
            for i, t in enumerate(slots):
                stack, place = g.spots[t]
                out[i * rows : (i + 1) * rows] = dot(stack_refs[stack][place, rows:], bel_all[...], TN)

    outs = (
        shape((g.span, g.width), bf16),
        shape((batch, g.span), bf16),
        *[shape((len(part) * rows, g.span), f32) for part in g.parts],
    )
    limit = g.n * rows * rows * 4 + 8 * mib
    return call("stage", kernel, outs, [*src_packs, *stacks], limit=limit)


def norms(g, stats, grad_sums, messages):
    def kernel(*refs):
        part_stats, refs = unflat(refs, stats)
        part_sums, refs = unflat(refs, grad_sums)
        everyone, (factors, belief_sum) = refs[: g.n_row], refs[-2:]
        part_stats = [wide(one) for one in part_stats]
        for s in range(g.n_row):
            lanes = slice(s * g.rows, (s + 1) * g.rows)

            def row(u, kind):
                at = kind * g.n_row + (s ^ u)
                return everyone[u][at : at + 1]

            tops = [row(u, 0) for u in range(g.n_row)]
            top = functools.reduce(jnp.maximum, tops)
            shares = [jnp.exp(one - top) for one in tops]
            inverse = 1.0 / sum(share * row(u, 1) for u, share in enumerate(shares))
            for part, one in enumerate(part_stats):
                factors[part : part + 1, lanes] = jnp.exp(one[0:1, lanes] - top) * inverse
            dots = sum(share * row(u, 2) for u, share in enumerate(shares))
            factors[2:3, lanes] = dots * inverse
        belief_sum[...] = wide(part_sums[0]) * factors[0:1] + wide(part_sums[1]) * factors[1:2]

    outs = (shape((8, g.span), f32), shape((g.batch, g.span), f32))
    return call("norms", kernel, outs, [*flat(stats), *flat(grad_sums), *messages], limit=4 * mib)


def column_shares(g, slots, kind, factors, probs, prob_grads, src_all, bel_all, *after):
    rows = g.rows

    def kernel(factors, *refs):
        prob_refs, refs = unflat(refs, probs)
        prob_grads, (src_all, bel_all), (change_ref, share_ref) = refs[:2], refs[2:4], refs[-2:]
        for i, t in enumerate(slots):
            part, place = g.where(t)
            here = slice(place * rows, (place + 1) * rows)
            prob = wide(prob_refs[part], here) * factors[part : part + 1]
            change = (prob * (prob_grads[part][here] - factors[2:3])).astype(bf16)
            change_ref[i * rows : (i + 1) * rows] = change
            share_ref[i, :rows] = dot(change, src_all[...], NN).astype(kind)
            share_ref[i, rows:] = dot(bel_all[...], prob.astype(bf16), NT).astype(kind)

    outs = (
        shape((len(slots) * rows, g.span), bf16),
        shape((len(slots), g.packet, g.width), kind),
    )
    operands = [factors, *flat(probs), *prob_grads, src_all, bel_all]
    return call("column_shares", kernel, outs, operands, after, limit=g.n * rows * rows * 8 + 6 * mib)


def row_shares(g, slots, kind, changes, order, stacks, belief_sum, *after):
    rows = g.rows

    def kernel(*refs):
        changes = refs[: len(order)]
        stack_refs = refs[len(order) : len(order) + len(stacks)]
        belief_sum = refs[len(order) + len(stacks)]
        for s, out in zip(slots, refs[-len(slots) :]):
            lanes = slice(s * rows, (s + 1) * rows)
            total = 0.0
            for change, columns in zip(changes, order):
                for i, t in enumerate(columns):
                    stack, place = g.spots[t]
                    packet = stack_refs[stack][place, :rows]
                    total = total + dot(change[i * rows : (i + 1) * rows, lanes], packet, TN)
            out[:rows] = total.astype(kind)
            out[rows:] = belief_sum[:, lanes].astype(kind)

    outs = (shape((g.packet, g.width), kind),) * len(slots)
    operands = [*changes, *stacks, belief_sum]
    return call("row_shares", kernel, outs, operands, after, limit=g.n * rows * rows * 4 + 6 * mib)


def fold(own, near, i, others, *after):
    def kernel(own_ref, near_ref, *refs):
        total = own_ref[i] + near_ref[i].astype(f32)
        for one in refs[: len(others)]:
            total = total + one[...].astype(f32)
        refs[-1][...] = total.astype(bf16)

    return call("fold", kernel, shape(own.shape[1:], bf16), [own, near, *others], after)


def totals(g, src_own, src_others, dst_own, dst_near, dst_others):
    def kernel(*refs):
        src_out, belief_out, dst_out, next_out = refs[-4:]
        src_refs, dst_refs = refs[: 1 + len(src_others)], refs[1 + len(src_others) : -4]

        def added(out, here, own, others):
            total = own[here] + sum(one[here].astype(f32) for one in others)
            out[...] = total.astype(out.dtype)

        big, small = slice(0, g.rows), slice(g.rows, g.packet)
        dst_refs = [dst_refs[0].at[0], dst_refs[1].at[0], *dst_refs[2:]]
        added(src_out, big, src_refs[0], src_refs[1:])
        added(belief_out, small, src_refs[0], src_refs[1:])
        added(dst_out, big, dst_refs[0], dst_refs[1:])
        added(next_out, small, dst_refs[0], dst_refs[1:])

    outs = (
        shape((g.rows, g.width), f32),
        shape((g.batch, g.rows), bf16),
        shape((g.rows, g.width), f32),
        shape((g.batch, g.rows), f32),
    )
    operands = [src_own, *src_others, dst_own, dst_near, *dst_others]
    return call("totals", kernel, outs, operands, limit=12 * mib)


def per_device(n, src_emb, dst_emb, tile_dst, tile_count, beliefs, grad_next):
    g = Grid(n, *src_emb.shape, beliefs.shape[0])

    def swap(array, flip):
        return lax.ppermute(array, "src", [(i, i ^ flip) for i in range(n)])

    raw = {t: (swap(dst_emb, t), swap(grad_next, t)) for t in g.early[2:]}
    src_pack, dst_pack = pack(g, tile_dst, tile_count, src_emb, beliefs, dst_emb, grad_next)
    src_others = [swap(src_pack, g.row_flip(s)) for s in range(1, g.n_row)]
    packets = {2: swap(dst_pack, 2)}
    for t, (block, small) in raw.items():
        packets[t] = paired(block, small)
    src_kept, packets[0] = keep(src_pack, dst_pack, *[packets[t] for t in raw])
    src_packs = [src_kept] + src_others
    for t in sorted(g.late, key=lambda t: bin(t).count("1")):
        packets[t] = swap(packets[t ^ low_bit(t)], low_bit(t))
    stacks = []
    for slots in g.groups:
        pile = stack([packets[t] for t in slots], *(src_others if slots is g.late else ()))
        stacks += [pile, swap(pile, 1)]

    everyone = list(range(g.n_row))
    scored = [scores(g, everyone, g.parts[0], src_packs, stacks[:-2])]
    scored.append(scores(g, everyone, g.parts[1], src_packs, stacks[-2:], scored[0][2]))
    probs, grad_sums, stats = ([[one] for one in each] for each in zip(*scored))
    message = join(g, stats)
    messages = [message] + [swap(message, g.row_flip(s)) for s in range(1, g.n_row)]
    src_all, bel_all, *prob_grads = stage(g, src_packs, stacks)
    factors, belief_sum = norms(g, stats, grad_sums, messages)

    def columns(slots, kind, *after):
        return column_shares(g, slots, kind, factors, probs, prob_grads, src_all, bel_all, *after)

    odd_far, odd_near = ([t + 1 for t in slots] for slots in (g.far, g.near))
    change_of_far_odd, far_send = columns(odd_far, bf16)
    far_got = swap(far_send, 1)
    change_of_far, far_own = columns(g.far, f32, far_send)
    change_of_near_odd, near_send = columns(odd_near, bf16, far_own)
    near_got = swap(near_send, 1)
    change_of_near, near_own = columns(g.near, f32, near_send)
    changes = [change_of_far_odd, change_of_far, change_of_near_odd, change_of_near]
    order = [odd_far, g.far, odd_near, g.near]

    got = {t: [] for t in range(0, g.n_col, 2)}
    last = near_send
    for t in reversed(range(2, g.n_col, 2)):
        own, near, slots = (far_own, far_got, g.far) if t in g.far else (near_own, near_got, g.near)
        send = fold(own, near, slots.index(t), got[t], last)
        one = swap(send, low_bit(t))
        got[t ^ low_bit(t)].append(hand(one) if low_bit(t) > 2 else one)
        if t == g.n_col - 2:
            rest = list(range(1, g.n_row))
            src_send = row_shares(g, rest, bf16, changes, order, stacks, belief_sum, send)
            src_got = [swap(one, g.row_flip(s)) for one, s in zip(src_send, rest)]
        elif t == 4:
            (src_own,) = row_shares(g, [0], f32, changes, order, stacks, belief_sum, send)
            send = src_own
        last = send
    grad_src, grad_belief, grad_dst, next_belief = totals(
        g, src_own, src_got, near_own, near_got, got[0]
    )
    return (next_belief, grad_belief, grad_src, grad_dst)


def solution(mesh):
    placed = (
        P(("groups", "src"), None),
        P(("groups", "src"), None),
        P(("groups", "src"), None),
        P(("groups", "src")),
        P("groups", "src"),
        P("groups", "src"),
    )
    return jax.shard_map(
        functools.partial(per_device, mesh.shape["src"]),
        mesh=mesh,
        in_specs=placed,
        out_specs=(
            P("groups", "src"),
            P("groups", "src"),
            P(("groups", "src"), None),
            P(("groups", "src"), None),
        ),
        check_vma=False,
    )
```

```python
import functools

import jax
import jax.numpy as jnp
from jax import lax
from jax.experimental import pallas as pl
from jax.experimental.pallas import tpu as pltpu
from jax.sharding import PartitionSpec as P

f32 = jnp.float32
bf16 = jnp.bfloat16
unlisted = 1e30
mib = 1 << 20


class Grid:
    def __init__(self, n, rows, width, batch):
        bits = n.bit_length() - 1
        row_bits = max(1, bits // 2 - 1)
        self.n, self.rows, self.width, self.batch = n, rows, width, batch
        self.n_row = 1 << row_bits
        self.n_col = n // self.n_row
        self.span = self.n_row * rows
        self.packet = rows + batch
        self.head = (3 * self.n_row + 7) // 8 * 8
        even = range(0, self.n_col, 2)
        self.early = [t for t in even if t & (t - 1) == 0]
        self.late = [t for t in even if t & (t - 1)]
        self.groups = [self.early[2:], [2], [0], self.late]
        both = [group + [t + 1 for t in group] for group in self.groups]
        self.parts = [both[0] + both[1] + both[2], both[3]]
        self.spots = {t: (2 * k + (t & 1), group.index(t & ~1)) for k, group in enumerate(self.groups) for t in both[k]}
        top = self.n_col // 2
        self.far = [t for t in range(top, self.n_col, 2)]
        self.near = [t for t in range(0, top, 2)]

    def row_flip(self, s):
        return s * self.n_col

    def where(self, t):
        part = 0 if t in self.parts[0] else 1
        return part, self.parts[part].index(t)


def low_bit(t):
    return t & -t


def dot(a, b, dims):
    return lax.dot_general(a, b, (dims, ((), ())), preferred_element_type=f32)


NN = ((1,), (0,))
NT = ((1,), (1,))
TN = ((0,), (0,))


def in_vmem():
    return pl.BlockSpec(memory_space=pltpu.VMEM)


def anywhere():
    return pl.BlockSpec(memory_space=pl.ANY)


def in_smem():
    return pl.BlockSpec(memory_space=pltpu.SMEM)


shape = jax.ShapeDtypeStruct


def call(name, kernel, out_shape, operands, after=(), scratch=(), limit=8 * mib, cost=None):
    many = isinstance(out_shape, tuple)
    return pl.pallas_call(
        kernel,
        out_shape=out_shape,
        in_specs=[in_vmem()] * len(operands) + [anywhere()] * len(after),
        out_specs=(in_vmem(),) * len(out_shape) if many else in_vmem(),
        scratch_shapes=list(scratch),
        compiler_params=pltpu.CompilerParams(vmem_limit_bytes=limit),
        cost_estimate=cost,
        name=name,
    )(*operands, *after)


def pack_kernel(g, tile_ref, count_ref, src_ref, bel_ref, dst_ref, grad_ref, src_pack, dst_pack, src_small, flags):
    rows, batch = g.rows, g.batch
    me = lax.axis_index("src")
    count = jnp.broadcast_to(count_ref[...], (1, g.width))
    for k in range(g.n):
        flags[pl.ds(tile_ref[0, k] ^ me, 1), :] = jnp.where(count > k, 1.0, 0.0).astype(f32)
    src_pack[:rows] = src_ref[...]
    src_pack[rows : rows + batch] = bel_ref[...]
    src_pack[rows + batch :] = flags[...].astype(bf16)
    dst_pack[:rows] = dst_ref[...]
    dst_pack[rows:] = grad_ref[...]
    src_small[:batch] = bel_ref[...]
    src_small[batch:] = flags[...].astype(bf16)


def pack(g, tile_dst, tile_count, src_emb, beliefs, dst_emb, grad_next):
    return pl.pallas_call(
        functools.partial(pack_kernel, g),
        out_shape=(
            shape((g.rows + g.batch + g.n, g.width), bf16),
            shape((g.rows + g.batch, g.width), bf16),
            shape((g.batch + g.n, g.width), bf16),
        ),
        in_specs=[in_smem()] + [in_vmem()] * 5,
        out_specs=(in_vmem(),) * 3,
        scratch_shapes=[pltpu.VMEM((g.n, g.width), f32)],
        compiler_params=pltpu.CompilerParams(vmem_limit_bytes=60 * mib),
        name="pack",
    )(tile_dst, tile_count.reshape(1, 1), src_emb, beliefs, dst_emb, grad_next)


def keep(src_pack, dst_pack, *after):
    def kernel(src_ref, dst_ref, *refs):
        refs[-2][...] = src_ref[...]
        refs[-1][...] = dst_ref[...]

    outs = (shape(src_pack.shape, bf16), shape(dst_pack.shape, bf16))
    return call("keep", kernel, outs, [src_pack, dst_pack], after, limit=2 * mib)


def hand(one, *after):
    def kernel(one_ref, *refs):
        refs[-1][...] = one_ref[...]

    return call("hand", kernel, shape(one.shape, one.dtype), [one], after, limit=2 * mib)


def paired(block, small, cost=None):
    def kernel(block_ref, small_ref, *refs):
        refs[-1][: block.shape[0]] = block_ref[...]
        refs[-1][block.shape[0] :] = small_ref[...]

    out = shape((block.shape[0] + small.shape[0], block.shape[1]), bf16)
    return call("paired", kernel, out, [block, small], limit=2 * mib, cost=cost)


def stack(packs, *after):
    def kernel(*refs):
        for i in range(len(packs)):
            refs[-1][i] = refs[i][...]

    out = shape((len(packs),) + packs[0].shape, packs[0].dtype)
    return call("stack", kernel, out, packs, after)


def score_kernel(g, row_slots, slots, *refs):
    rows, batch, span = g.rows, g.batch, len(row_slots) * g.rows
    src_packs, stacks = refs[: len(row_slots)], refs[len(row_slots) :]
    prob_ref, grad_sum, stats, src_all, bel_all = refs[-5:]
    first = g.spots[slots[0]][0]
    listed = []
    for p, one in enumerate(src_packs):
        lanes = slice(p * rows, (p + 1) * rows)
        src_all[lanes] = one[:rows]
        bel_all[:, lanes] = one[rows : rows + batch]
        listed.append((one[rows + batch :].astype(f32) - 1.0) * unlisted)

    def packet(t):
        stack, place = g.spots[t]
        return stacks[stack - first].at[place]

    top = jnp.full((8, span), -unlisted, f32)
    for i, t in enumerate(slots):
        flips = [g.row_flip(s) | t for s in row_slots]
        bias = jnp.concatenate([one[v : v + 1] for one, v in zip(listed, flips)], axis=1)
        logits = dot(packet(t)[:rows], src_all[...], NT) + bias
        prob_ref[i * rows : (i + 1) * rows] = logits
        top = jnp.maximum(top, jnp.max(logits.reshape(rows // 8, 8, span), axis=0))
    top = jnp.max(top, axis=0, keepdims=True)
    total = jnp.zeros((8, span), f32)
    grad_sum[...] = jnp.zeros(grad_sum.shape, f32)
    for i, t in enumerate(slots):
        here = slice(i * rows, (i + 1) * rows)
        prob = jnp.exp(prob_ref[here] - top)
        prob_ref[here] = prob
        grad_sum[...] += dot(packet(t)[rows:], prob.astype(bf16), NN)
        total = total + jnp.sum(prob.reshape(rows // 8, 8, span), axis=0)
    stats[0:1] = top
    stats[1:2] = jnp.sum(total, axis=0, keepdims=True)
    stats[2:3] = jnp.sum(bel_all[...].astype(f32) * grad_sum[...], axis=0, keepdims=True)


def scores(g, row_slots, slots, src_packs, stacks, *after):
    tall, span = len(slots) * g.rows, len(row_slots) * g.rows
    outs = (shape((tall, span), f32), shape((g.batch, span), f32), shape((3, span), f32))
    scratch = [pltpu.VMEM((span, g.width), bf16), pltpu.VMEM((g.batch, span), bf16)]
    kernel = functools.partial(score_kernel, g, row_slots, slots)
    operands = [*[src_packs[s] for s in row_slots], *stacks]
    cost = pl.CostEstimate(
        flops=2 * tall * span * (g.width + g.batch), bytes_accessed=8 * tall * span, transcendentals=tall * span
    )
    return call("scores", kernel, outs, operands, after, scratch, tall * span * 8 + 6 * mib, cost)


def flat(parts):
    return [one for part in parts for one in part]


def unflat(refs, parts):
    out = []
    for part in parts:
        out.append(refs[: len(part)])
        refs = refs[len(part) :]
    return out, refs


def wide(refs, here=slice(None)):
    return jnp.concatenate([one[here] for one in refs], axis=1)


def merged(stats):
    tops = [one[0:1] for one in stats]
    top = functools.reduce(jnp.maximum, tops)
    factors = [jnp.exp(one - top) for one in tops]
    total = sum(factor * one[1:2] for factor, one in zip(factors, stats))
    dots = sum(factor * one[2:3] for factor, one in zip(factors, stats))
    return top, total, dots


def join(g, stats):
    def kernel(*refs):
        out = refs[-1]
        parts, _ = unflat(refs, stats)
        for kind, value in enumerate(merged([wide(one) for one in parts])):
            for s in range(g.n_row):
                at = kind * g.n_row + s
                out[at : at + 1] = value[:, s * g.rows : (s + 1) * g.rows]
        if g.head > 3 * g.n_row:
            out[3 * g.n_row :] = jnp.zeros((g.head - 3 * g.n_row, g.rows), f32)

    return call("join", kernel, shape((g.head, g.rows), f32), flat(stats), limit=2 * mib)


def stage(g, src_packs, stacks):
    rows, batch = g.rows, g.batch

    def kernel(*refs):
        src_refs, stack_refs = refs[: g.n_row], refs[g.n_row : -4]
        src_all, bel_all, *prob_grads = refs[-4:]
        for s, one in enumerate(src_refs):
            lanes = slice(s * rows, (s + 1) * rows)
            src_all[lanes] = one[:rows]
            bel_all[:, lanes] = one[rows : rows + batch]
        for slots, out in zip(g.parts, prob_grads):
            for i, t in enumerate(slots):
                stack, place = g.spots[t]
                out[i * rows : (i + 1) * rows] = dot(stack_refs[stack][place, rows:], bel_all[...], TN)

    outs = (
        shape((g.span, g.width), bf16),
        shape((batch, g.span), bf16),
        *[shape((len(part) * rows, g.span), f32) for part in g.parts],
    )
    limit = g.n * rows * rows * 4 + 8 * mib
    return call("stage", kernel, outs, [*src_packs, *stacks], limit=limit)


def norms(g, stats, grad_sums, messages):
    def kernel(*refs):
        part_stats, refs = unflat(refs, stats)
        part_sums, refs = unflat(refs, grad_sums)
        everyone, (factors, belief_sum) = refs[: g.n_row], refs[-2:]
        part_stats = [wide(one) for one in part_stats]
        for s in range(g.n_row):
            lanes = slice(s * g.rows, (s + 1) * g.rows)

            def row(u, kind):
                at = kind * g.n_row + (s ^ u)
                return everyone[u][at : at + 1]

            tops = [row(u, 0) for u in range(g.n_row)]
            top = functools.reduce(jnp.maximum, tops)
            shares = [jnp.exp(one - top) for one in tops]
            inverse = 1.0 / sum(share * row(u, 1) for u, share in enumerate(shares))
            for part, one in enumerate(part_stats):
                factors[part : part + 1, lanes] = jnp.exp(one[0:1, lanes] - top) * inverse
            dots = sum(share * row(u, 2) for u, share in enumerate(shares))
            factors[2:3, lanes] = dots * inverse
        belief_sum[...] = wide(part_sums[0]) * factors[0:1] + wide(part_sums[1]) * factors[1:2]

    outs = (shape((8, g.span), f32), shape((g.batch, g.span), f32))
    return call("norms", kernel, outs, [*flat(stats), *flat(grad_sums), *messages], limit=4 * mib)


def column_shares(g, slots, kind, factors, probs, prob_grads, src_all, bel_all, *after):
    rows = g.rows

    def kernel(factors, *refs):
        prob_refs, refs = unflat(refs, probs)
        prob_grads, (src_all, bel_all), (change_ref, share_ref) = refs[:2], refs[2:4], refs[-2:]
        for i, t in enumerate(slots):
            part, place = g.where(t)
            here = slice(place * rows, (place + 1) * rows)
            prob = wide(prob_refs[part], here) * factors[part : part + 1]
            change = (prob * (prob_grads[part][here] - factors[2:3])).astype(bf16)
            change_ref[i * rows : (i + 1) * rows] = change
            share_ref[i, :rows] = dot(change, src_all[...], NN).astype(kind)
            share_ref[i, rows:] = dot(bel_all[...], prob.astype(bf16), NT).astype(kind)

    outs = (
        shape((len(slots) * rows, g.span), bf16),
        shape((len(slots), g.packet, g.width), kind),
    )
    operands = [factors, *flat(probs), *prob_grads, src_all, bel_all]
    return call("column_shares", kernel, outs, operands, after, limit=g.n * rows * rows * 8 + 6 * mib)


def row_shares(g, slots, kind, changes, order, stacks, belief_sum, *after):
    rows = g.rows

    def kernel(*refs):
        changes = refs[: len(order)]
        stack_refs = refs[len(order) : len(order) + len(stacks)]
        belief_sum = refs[len(order) + len(stacks)]
        for s, out in zip(slots, refs[-len(slots) :]):
            lanes = slice(s * rows, (s + 1) * rows)
            total = 0.0
            for change, columns in zip(changes, order):
                for i, t in enumerate(columns):
                    stack, place = g.spots[t]
                    packet = stack_refs[stack][place, :rows]
                    total = total + dot(change[i * rows : (i + 1) * rows, lanes], packet, TN)
            out[:rows] = total.astype(kind)
            out[rows:] = belief_sum[:, lanes].astype(kind)

    outs = (shape((g.packet, g.width), kind),) * len(slots)
    operands = [*changes, *stacks, belief_sum]
    return call("row_shares", kernel, outs, operands, after, limit=g.n * rows * rows * 4 + 6 * mib)


def fold(own, near, i, others, *after):
    def kernel(own_ref, near_ref, *refs):
        total = own_ref[i] + near_ref[i].astype(f32)
        for one in refs[: len(others)]:
            total = total + one[...].astype(f32)
        refs[-1][...] = total.astype(bf16)

    return call("fold", kernel, shape(own.shape[1:], bf16), [own, near, *others], after)


def totals(g, src_own, src_others, dst_own, dst_near, dst_others):
    def kernel(*refs):
        src_out, belief_out, dst_out, next_out = refs[-4:]
        src_refs, dst_refs = refs[: 1 + len(src_others)], refs[1 + len(src_others) : -4]

        def added(out, here, own, others):
            total = own[here] + sum(one[here].astype(f32) for one in others)
            out[...] = total.astype(out.dtype)

        big, small = slice(0, g.rows), slice(g.rows, g.packet)
        dst_refs = [dst_refs[0].at[0], dst_refs[1].at[0], *dst_refs[2:]]
        added(src_out, big, src_refs[0], src_refs[1:])
        added(belief_out, small, src_refs[0], src_refs[1:])
        added(dst_out, big, dst_refs[0], dst_refs[1:])
        added(next_out, small, dst_refs[0], dst_refs[1:])

    outs = (
        shape((g.rows, g.width), f32),
        shape((g.batch, g.rows), bf16),
        shape((g.rows, g.width), f32),
        shape((g.batch, g.rows), f32),
    )
    operands = [src_own, *src_others, dst_own, dst_near, *dst_others]
    return call("totals", kernel, outs, operands, limit=12 * mib)


def per_device(n, src_emb, dst_emb, tile_dst, tile_count, beliefs, grad_next):
    g = Grid(n, *src_emb.shape, beliefs.shape[0])

    def swap(array, flip):
        return lax.ppermute(array, "src", [(i, i ^ flip) for i in range(n)])

    raw = {t: (swap(dst_emb, t), swap(grad_next, t)) for t in reversed(g.early[1:])}
    raw_src = [swap(src_emb, g.row_flip(s)) for s in range(1, g.n_row)]
    src_pack, dst_pack, src_small = pack(g, tile_dst, tile_count, src_emb, beliefs, dst_emb, grad_next)
    small = [swap(src_small, g.row_flip(s)) for s in range(1, g.n_row)]
    moved = pl.CostEstimate(flops=2 << 30, bytes_accessed=1 << 20, transcendentals=0)
    src_others = [paired(*pair, moved) for pair in zip(raw_src, small)]
    packets = {t: paired(*pair) for t, pair in raw.items()}
    src_kept, packets[0] = keep(src_pack, dst_pack, *[packets[t] for t in g.early[2:]])
    src_packs = [src_kept] + src_others
    for t in sorted(g.late, key=lambda t: bin(t).count("1")):
        packets[t] = swap(packets[t ^ low_bit(t)], low_bit(t))
    stacks = []
    for slots in g.groups:
        pile = stack([packets[t] for t in slots], *(src_others if slots is g.late else ()))
        stacks += [pile, swap(pile, 1)]

    everyone = list(range(g.n_row))
    scored = [scores(g, everyone, g.parts[0], src_packs, stacks[:-2])]
    scored.append(scores(g, everyone, g.parts[1], src_packs, stacks[-2:], scored[0][2]))
    probs, grad_sums, stats = ([[one] for one in each] for each in zip(*scored))
    message = join(g, stats)
    messages = [message] + [swap(message, g.row_flip(s)) for s in range(1, g.n_row)]
    src_all, bel_all, *prob_grads = stage(g, src_packs, stacks)
    factors, belief_sum = norms(g, stats, grad_sums, messages)

    def columns(slots, kind, *after):
        return column_shares(g, slots, kind, factors, probs, prob_grads, src_all, bel_all, *after)

    odd_far, odd_near = ([t + 1 for t in slots] for slots in (g.far, g.near))
    change_of_far_odd, far_send = columns(odd_far, bf16)
    far_got = swap(far_send, 1)
    change_of_far, far_own = columns(g.far, f32, far_send)
    change_of_near_odd, near_send = columns(odd_near, bf16, far_own)
    near_got = swap(near_send, 1)
    change_of_near, near_own = columns(g.near, f32, near_send)
    changes = [change_of_far_odd, change_of_far, change_of_near_odd, change_of_near]
    order = [odd_far, g.far, odd_near, g.near]

    got = {t: [] for t in range(0, g.n_col, 2)}
    last = near_send
    for t in reversed(range(2, g.n_col, 2)):
        own, near, slots = (far_own, far_got, g.far) if t in g.far else (near_own, near_got, g.near)
        send = fold(own, near, slots.index(t), got[t], last)
        one = swap(send, low_bit(t))
        got[t ^ low_bit(t)].append(hand(one) if low_bit(t) > 2 else one)
        if t == g.n_col - 2:
            rest = list(range(1, g.n_row))
            src_send = row_shares(g, rest, bf16, changes, order, stacks, belief_sum, send)
            src_got = [swap(one, g.row_flip(s)) for one, s in zip(src_send, rest)]
        elif t == 4:
            (src_own,) = row_shares(g, [0], f32, changes, order, stacks, belief_sum, send)
            send = src_own
        last = send
    grad_src, grad_belief, grad_dst, next_belief = totals(
        g, src_own, src_got, near_own, near_got, got[0]
    )
    return (next_belief, grad_belief, grad_src, grad_dst)


def solution(mesh):
    placed = (
        P(("groups", "src"), None),
        P(("groups", "src"), None),
        P(("groups", "src"), None),
        P(("groups", "src")),
        P("groups", "src"),
        P("groups", "src"),
    )
    return jax.shard_map(
        functools.partial(per_device, mesh.shape["src"]),
        mesh=mesh,
        in_specs=placed,
        out_specs=(
            P("groups", "src"),
            P("groups", "src"),
            P(("groups", "src"), None),
            P(("groups", "src"), None),
        ),
        check_vma=False,
    )
```

```python
import functools

import jax
import jax.numpy as jnp
from jax import lax
from jax.experimental import pallas as pl
from jax.experimental.pallas import tpu as pltpu
from jax.sharding import PartitionSpec as P

f32 = jnp.float32
bf16 = jnp.bfloat16
unlisted = 1e30
mib = 1 << 20


class Grid:
    def __init__(self, n, rows, width, batch):
        bits = n.bit_length() - 1
        row_bits = max(1, bits // 2 - 1)
        self.n, self.rows, self.width, self.batch = n, rows, width, batch
        self.n_row = 1 << row_bits
        self.n_col = n // self.n_row
        self.span = self.n_row * rows
        self.packet = rows + batch
        self.head = (3 * self.n_row + 7) // 8 * 8
        even = range(0, self.n_col, 2)
        self.early = [t for t in even if t & (t - 1) == 0]
        self.late = [t for t in even if t & (t - 1)]
        self.groups = [self.early[2:], [2], [0], self.late]
        both = [group + [t + 1 for t in group] for group in self.groups]
        self.parts = [both[0] + both[1] + both[2], both[3]]
        self.spots = {t: (2 * k + (t & 1), group.index(t & ~1)) for k, group in enumerate(self.groups) for t in both[k]}
        top = self.n_col // 2
        self.far = [t for t in range(top, self.n_col, 2)]
        self.near = [t for t in range(0, top, 2)]

    def row_flip(self, s):
        return s * self.n_col

    def where(self, t):
        part = 0 if t in self.parts[0] else 1
        return part, self.parts[part].index(t)


def low_bit(t):
    return t & -t


def dot(a, b, dims):
    return lax.dot_general(a, b, (dims, ((), ())), preferred_element_type=f32)


NN = ((1,), (0,))
NT = ((1,), (1,))
TN = ((0,), (0,))


def in_vmem():
    return pl.BlockSpec(memory_space=pltpu.VMEM)


def anywhere():
    return pl.BlockSpec(memory_space=pl.ANY)


def in_smem():
    return pl.BlockSpec(memory_space=pltpu.SMEM)


shape = jax.ShapeDtypeStruct


def call(name, kernel, out_shape, operands, after=(), scratch=(), limit=8 * mib, cost=None):
    many = isinstance(out_shape, tuple)
    return pl.pallas_call(
        kernel,
        out_shape=out_shape,
        in_specs=[in_vmem()] * len(operands) + [anywhere()] * len(after),
        out_specs=(in_vmem(),) * len(out_shape) if many else in_vmem(),
        scratch_shapes=list(scratch),
        compiler_params=pltpu.CompilerParams(vmem_limit_bytes=limit),
        cost_estimate=cost,
        name=name,
    )(*operands, *after)


def pack_kernel(g, tile_ref, count_ref, src_ref, bel_ref, dst_ref, grad_ref, src_pack, dst_pack, flags, count, sem):
    rows, batch = g.rows, g.batch
    me = lax.axis_index("src")
    copy = pltpu.make_async_copy(count_ref, count, sem)
    copy.start()
    copy.wait()
    for k in range(g.n):
        flags[pl.ds(tile_ref[0, k] ^ me, 1), :] = jnp.broadcast_to(jnp.where(k < count[0], 1.0, 0.0), (1, g.width)).astype(f32)
    src_pack[:rows] = src_ref[...]
    src_pack[rows : rows + batch] = bel_ref[...]
    src_pack[rows + batch :] = flags[...].astype(bf16)
    dst_pack[:rows] = dst_ref[...]
    dst_pack[rows:] = grad_ref[...]


def pack(g, tile_dst, tile_count, src_emb, beliefs, dst_emb, grad_next):
    return pl.pallas_call(
        functools.partial(pack_kernel, g),
        out_shape=(
            shape((g.rows + g.batch + g.n, g.width), bf16),
            shape((g.rows + g.batch, g.width), bf16),
        ),
        in_specs=[in_smem(), anywhere()] + [in_vmem()] * 4,
        out_specs=(in_vmem(),) * 2,
        scratch_shapes=[
            pltpu.VMEM((g.n, g.width), f32),
            pltpu.SMEM((1,), jnp.int32),
            pltpu.SemaphoreType.DMA,
        ],
        compiler_params=pltpu.CompilerParams(vmem_limit_bytes=60 * mib),
        name="pack",
    )(tile_dst, tile_count, src_emb, beliefs, dst_emb, grad_next)


def keep(src_pack, dst_pack, *after):
    def kernel(src_ref, dst_ref, *refs):
        refs[-2][...] = src_ref[...]
        refs[-1][...] = dst_ref[...]

    outs = (shape(src_pack.shape, bf16), shape(dst_pack.shape, bf16))
    return call("keep", kernel, outs, [src_pack, dst_pack], after, limit=2 * mib)


def hand(one, *after, cost=None):
    def kernel(one_ref, *refs):
        refs[-1][...] = one_ref[...]

    return call("hand", kernel, shape(one.shape, one.dtype), [one], after, limit=4 * mib, cost=cost)


def paired(block, small, *after):
    def kernel(block_ref, small_ref, *refs):
        refs[-1][: block.shape[0]] = block_ref[...]
        refs[-1][block.shape[0] :] = small_ref[...]

    out = shape((block.shape[0] + small.shape[0], block.shape[1]), bf16)
    return call("paired", kernel, out, [block, small], after, limit=2 * mib)


def stack(packs, *after):
    def kernel(*refs):
        for i in range(len(packs)):
            refs[-1][i] = refs[i][...]

    out = shape((len(packs),) + packs[0].shape, packs[0].dtype)
    return call("stack", kernel, out, packs, after)


def score_kernel(g, row_slots, slots, *refs):
    rows, batch, span = g.rows, g.batch, len(row_slots) * g.rows
    src_packs, stacks = refs[: len(row_slots)], refs[len(row_slots) :]
    prob_ref, grad_sum, stats, src_all, bel_all = refs[-5:]
    first = g.spots[slots[0]][0]
    listed = []
    for p, one in enumerate(src_packs):
        lanes = slice(p * rows, (p + 1) * rows)
        src_all[lanes] = one[:rows]
        bel_all[:, lanes] = one[rows : rows + batch]
        listed.append((one[rows + batch :].astype(f32) - 1.0) * unlisted)

    def packet(t):
        stack, place = g.spots[t]
        return stacks[stack - first].at[place]

    top = jnp.full((8, span), -unlisted, f32)
    for i, t in enumerate(slots):
        flips = [g.row_flip(s) | t for s in row_slots]
        bias = jnp.concatenate([one[v : v + 1] for one, v in zip(listed, flips)], axis=1)
        logits = dot(packet(t)[:rows], src_all[...], NT) + bias
        prob_ref[i * rows : (i + 1) * rows] = logits
        top = jnp.maximum(top, jnp.max(logits.reshape(rows // 8, 8, span), axis=0))
    top = jnp.max(top, axis=0, keepdims=True)
    total = jnp.zeros((8, span), f32)
    grad_sum[...] = jnp.zeros(grad_sum.shape, f32)
    for i, t in enumerate(slots):
        here = slice(i * rows, (i + 1) * rows)
        prob = jnp.exp(prob_ref[here] - top)
        prob_ref[here] = prob
        grad_sum[...] += dot(packet(t)[rows:], prob.astype(bf16), NN)
        total = total + jnp.sum(prob.reshape(rows // 8, 8, span), axis=0)
    stats[0:1] = top
    stats[1:2] = jnp.sum(total, axis=0, keepdims=True)
    stats[2:3] = jnp.sum(bel_all[...].astype(f32) * grad_sum[...], axis=0, keepdims=True)


def scores(g, row_slots, slots, src_packs, stacks, *after):
    tall, span = len(slots) * g.rows, len(row_slots) * g.rows
    outs = (shape((tall, span), f32), shape((g.batch, span), f32), shape((3, span), f32))
    scratch = [pltpu.VMEM((span, g.width), bf16), pltpu.VMEM((g.batch, span), bf16)]
    kernel = functools.partial(score_kernel, g, row_slots, slots)
    operands = [*[src_packs[s] for s in row_slots], *stacks]
    return call("scores", kernel, outs, operands, after, scratch, tall * span * 8 + 6 * mib)


def flat(parts):
    return [one for part in parts for one in part]


def unflat(refs, parts):
    out = []
    for part in parts:
        out.append(refs[: len(part)])
        refs = refs[len(part) :]
    return out, refs


def wide(refs, here=slice(None)):
    return jnp.concatenate([one[here] for one in refs], axis=1)


def merged(stats):
    tops = [one[0:1] for one in stats]
    top = functools.reduce(jnp.maximum, tops)
    factors = [jnp.exp(one - top) for one in tops]
    total = sum(factor * one[1:2] for factor, one in zip(factors, stats))
    dots = sum(factor * one[2:3] for factor, one in zip(factors, stats))
    return top, total, dots


def join(g, stats):
    def kernel(*refs):
        out = refs[-1]
        parts, _ = unflat(refs, stats)
        for kind, value in enumerate(merged([wide(one) for one in parts])):
            for s in range(g.n_row):
                at = kind * g.n_row + s
                out[at : at + 1] = value[:, s * g.rows : (s + 1) * g.rows]
        if g.head > 3 * g.n_row:
            out[3 * g.n_row :] = jnp.zeros((g.head - 3 * g.n_row, g.rows), f32)

    return call("join", kernel, shape((g.head, g.rows), f32), flat(stats), limit=2 * mib)


def stage(g, src_packs, stacks):
    rows, batch = g.rows, g.batch

    def kernel(*refs):
        src_refs, stack_refs = refs[: g.n_row], refs[g.n_row : -4]
        src_all, bel_all, *prob_grads = refs[-4:]
        for s, one in enumerate(src_refs):
            lanes = slice(s * rows, (s + 1) * rows)
            src_all[lanes] = one[:rows]
            bel_all[:, lanes] = one[rows : rows + batch]
        for slots, out in zip(g.parts, prob_grads):
            for i, t in enumerate(slots):
                stack, place = g.spots[t]
                out[i * rows : (i + 1) * rows] = dot(stack_refs[stack][place, rows:], bel_all[...], TN)

    outs = (
        shape((g.span, g.width), bf16),
        shape((batch, g.span), bf16),
        *[shape((len(part) * rows, g.span), f32) for part in g.parts],
    )
    limit = g.n * rows * rows * 4 + 8 * mib
    return call("stage", kernel, outs, [*src_packs, *stacks], limit=limit)


def norms(g, stats, grad_sums, messages):
    def kernel(*refs):
        part_stats, refs = unflat(refs, stats)
        part_sums, refs = unflat(refs, grad_sums)
        everyone, (factors, belief_sum) = refs[: g.n_row], refs[-2:]
        part_stats = [wide(one) for one in part_stats]
        for s in range(g.n_row):
            lanes = slice(s * g.rows, (s + 1) * g.rows)

            def row(u, kind):
                at = kind * g.n_row + (s ^ u)
                return everyone[u][at : at + 1]

            tops = [row(u, 0) for u in range(g.n_row)]
            top = functools.reduce(jnp.maximum, tops)
            shares = [jnp.exp(one - top) for one in tops]
            inverse = 1.0 / sum(share * row(u, 1) for u, share in enumerate(shares))
            for part, one in enumerate(part_stats):
                factors[part : part + 1, lanes] = jnp.exp(one[0:1, lanes] - top) * inverse
            dots = sum(share * row(u, 2) for u, share in enumerate(shares))
            factors[2:3, lanes] = dots * inverse
        belief_sum[...] = wide(part_sums[0]) * factors[0:1] + wide(part_sums[1]) * factors[1:2]

    outs = (shape((8, g.span), f32), shape((g.batch, g.span), f32))
    return call("norms", kernel, outs, [*flat(stats), *flat(grad_sums), *messages], limit=4 * mib)


def column_shares(g, slots, kind, factors, probs, prob_grads, src_all, bel_all, *after):
    rows = g.rows

    def kernel(factors, *refs):
        prob_refs, refs = unflat(refs, probs)
        prob_grads, (src_all, bel_all), (change_ref, share_ref) = refs[:2], refs[2:4], refs[-2:]
        for i, t in enumerate(slots):
            part, place = g.where(t)
            here = slice(place * rows, (place + 1) * rows)
            prob = wide(prob_refs[part], here) * factors[part : part + 1]
            change = (prob * (prob_grads[part][here] - factors[2:3])).astype(bf16)
            change_ref[i * rows : (i + 1) * rows] = change
            share_ref[i, :rows] = dot(change, src_all[...], NN).astype(kind)
            share_ref[i, rows:] = dot(bel_all[...], prob.astype(bf16), NT).astype(kind)

    outs = (
        shape((len(slots) * rows, g.span), bf16),
        shape((len(slots), g.packet, g.width), kind),
    )
    operands = [factors, *flat(probs), *prob_grads, src_all, bel_all]
    return call("column_shares", kernel, outs, operands, after, limit=g.n * rows * rows * 8 + 6 * mib)


def row_shares(g, slots, kind, changes, order, stacks, belief_sum, *after):
    rows = g.rows

    def kernel(*refs):
        changes = refs[: len(order)]
        stack_refs = refs[len(order) : len(order) + len(stacks)]
        belief_sum = refs[len(order) + len(stacks)]
        for s, out in zip(slots, refs[-len(slots) :]):
            lanes = slice(s * rows, (s + 1) * rows)
            total = 0.0
            for change, columns in zip(changes, order):
                for i, t in enumerate(columns):
                    stack, place = g.spots[t]
                    packet = stack_refs[stack][place, :rows]
                    total = total + dot(change[i * rows : (i + 1) * rows, lanes], packet, TN)
            out[:rows] = total.astype(kind)
            out[rows:] = belief_sum[:, lanes].astype(kind)

    outs = (shape((g.packet, g.width), kind),) * len(slots)
    operands = [*changes, *stacks, belief_sum]
    return call("row_shares", kernel, outs, operands, after, limit=g.n * rows * rows * 4 + 6 * mib)


def fold(own, near, i, others, *after):
    def kernel(own_ref, near_ref, *refs):
        total = own_ref[i] + near_ref[i].astype(f32)
        for one in refs[: len(others)]:
            total = total + one[...].astype(f32)
        refs[-1][...] = total.astype(bf16)

    return call("fold", kernel, shape(own.shape[1:], bf16), [own, near, *others], after)


def totals(g, src_own, src_others, dst_own, dst_near, dst_others):
    def kernel(*refs):
        src_out, belief_out, dst_out, next_out = refs[-4:]
        src_refs, dst_refs = refs[: 1 + len(src_others)], refs[1 + len(src_others) : -4]

        def added(out, here, own, others):
            total = own[here] + sum(one[here].astype(f32) for one in others)
            out[...] = total.astype(out.dtype)

        big, small = slice(0, g.rows), slice(g.rows, g.packet)
        dst_refs = [dst_refs[0].at[0], dst_refs[1].at[0], *dst_refs[2:]]
        added(src_out, big, src_refs[0], src_refs[1:])
        added(belief_out, small, src_refs[0], src_refs[1:])
        added(dst_out, big, dst_refs[0], dst_refs[1:])
        added(next_out, small, dst_refs[0], dst_refs[1:])

    outs = (
        shape((g.rows, g.width), f32),
        shape((g.batch, g.rows), bf16),
        shape((g.rows, g.width), f32),
        shape((g.batch, g.rows), f32),
    )
    operands = [src_own, *src_others, dst_own, dst_near, *dst_others]
    return call("totals", kernel, outs, operands, limit=12 * mib)


def per_device(n, src_emb, dst_emb, tile_dst, tile_count, beliefs, grad_next):
    g = Grid(n, *src_emb.shape, beliefs.shape[0])

    def swap(array, flip):
        return lax.ppermute(array, "src", [(i, i ^ flip) for i in range(n)])

    raw = {t: (swap(dst_emb, t), swap(grad_next, t)) for t in g.early[2:]}
    src_pack, dst_pack = pack(g, tile_dst, tile_count, src_emb, beliefs, dst_emb, grad_next)
    src_others = [swap(src_pack, g.row_flip(s)) for s in range(1, g.n_row)]
    packets = {2: swap(dst_pack, 2)}
    for t, (block, small) in raw.items():
        packets[t] = paired(block, small)
    src_kept, packets[0] = keep(src_pack, dst_pack, *[packets[t] for t in raw])
    src_packs = [src_kept] + src_others
    for t in sorted(g.late, key=lambda t: bin(t).count("1")):
        packets[t] = swap(packets[t ^ low_bit(t)], low_bit(t))
    stacks = []
    for slots in g.groups:
        pile = stack([packets[t] for t in slots], *(src_others if slots is g.late else ()))
        stacks += [pile, swap(pile, 1)]

    everyone = list(range(g.n_row))
    scored = [scores(g, everyone, g.parts[0], src_packs, stacks[:-2])]
    scored.append(scores(g, everyone, g.parts[1], src_packs, stacks[-2:], scored[0][2]))
    probs, grad_sums, stats = ([[one] for one in each] for each in zip(*scored))
    message = join(g, stats)
    messages = [message] + [swap(message, g.row_flip(s)) for s in range(1, g.n_row)]
    src_all, bel_all, *prob_grads = stage(g, src_packs, stacks)
    factors, belief_sum = norms(g, stats, grad_sums, messages)

    def columns(slots, kind, *after):
        return column_shares(g, slots, kind, factors, probs, prob_grads, src_all, bel_all, *after)

    odd_far, odd_near = ([t + 1 for t in slots] for slots in (g.far, g.near))
    change_of_far_odd, far_send = columns(odd_far, bf16)
    far_got = swap(far_send, 1)
    change_of_far, far_own = columns(g.far, f32, far_send)
    change_of_near_odd, near_send = columns(odd_near, bf16, far_own)
    change_of_near, near_own = columns(g.near, f32, near_send)
    changes = [change_of_far_odd, change_of_far, change_of_near_odd, change_of_near]
    order = [odd_far, g.far, odd_near, g.near]
    rest = list(range(1, g.n_row))
    src_send = row_shares(g, rest, bf16, changes, order, stacks, belief_sum)

    got = {t: [] for t in range(0, g.n_col, 2)}
    last = src_send[0]
    for t in reversed(range(2, g.n_col, 2)):
        if t in g.near and t + 2 in g.far:
            (src_own,) = row_shares(g, [0], f32, changes, order, stacks, belief_sum, last)
            last = src_own
        own, near, slots = (far_own, far_got, g.far) if t in g.far else (near_own, near_got, g.near)
        last = fold(own, near, slots.index(t), got[t], last)
        if t == g.n_col - 2:
            src_got = [swap(hand(one, last), g.row_flip(s)) for one, s in zip(src_send, rest)]
            near_got = swap(hand(near_send, last), 1)
        one = swap(last, low_bit(t))
        got[t ^ low_bit(t)].append(hand(one) if low_bit(t) > 2 else one)
    grad_src, grad_belief, grad_dst, next_belief = totals(
        g, src_own, src_got, near_own, near_got, got[0]
    )
    return (next_belief, grad_belief, grad_src, grad_dst)


def solution(mesh):
    placed = (
        P(("groups", "src"), None),
        P(("groups", "src"), None),
        P(("groups", "src"), None),
        P(("groups", "src")),
        P("groups", "src"),
        P("groups", "src"),
    )
    return jax.shard_map(
        functools.partial(per_device, mesh.shape["src"]),
        mesh=mesh,
        in_specs=placed,
        out_specs=(
            P("groups", "src"),
            P("groups", "src"),
            P(("groups", "src"), None),
            P(("groups", "src"), None),
        ),
        check_vma=False,
    )
```

```python
import functools

import jax
import jax.numpy as jnp
from jax import lax
from jax.experimental import pallas as pl
from jax.experimental.pallas import tpu as pltpu
from jax.sharding import PartitionSpec as P

f32 = jnp.float32
bf16 = jnp.bfloat16
unlisted = 1e30
mib = 1 << 20


class Grid:
    def __init__(self, n, rows, width, batch):
        bits = n.bit_length() - 1
        row_bits = max(1, bits // 2 - 1)
        self.n, self.rows, self.width, self.batch = n, rows, width, batch
        self.n_row = 1 << row_bits
        self.n_col = n // self.n_row
        self.span = self.n_row * rows
        self.packet = rows + batch
        self.head = (3 * self.n_row + 7) // 8 * 8
        cut = self.packet // 32 * 16 + 16
        self.pieces = [(0, cut), (cut, self.packet)]
        even = range(0, self.n_col, 2)
        self.early = [t for t in even if t & (t - 1) == 0]
        self.late = [t for t in even if t & (t - 1)]
        self.groups = [self.early[2:], [2], [0], self.late]
        both = [group + [t + 1 for t in group] for group in self.groups]
        self.parts = [both[0] + both[1] + both[2], both[3]]
        self.spots = {t: (2 * k + (t & 1), group.index(t & ~1)) for k, group in enumerate(self.groups) for t in both[k]}
        top = self.n_col // 2
        self.far = [t for t in range(top, self.n_col, 2)]
        self.near = [t for t in range(0, top, 2)]

    def row_flip(self, s):
        return s * self.n_col

    def where(self, t):
        part = 0 if t in self.parts[0] else 1
        return part, self.parts[part].index(t)


def low_bit(t):
    return t & -t


def dot(a, b, dims):
    return lax.dot_general(a, b, (dims, ((), ())), preferred_element_type=f32)


NN = ((1,), (0,))
NT = ((1,), (1,))
TN = ((0,), (0,))


def in_vmem():
    return pl.BlockSpec(memory_space=pltpu.VMEM)


def anywhere():
    return pl.BlockSpec(memory_space=pl.ANY)


def in_smem():
    return pl.BlockSpec(memory_space=pltpu.SMEM)


shape = jax.ShapeDtypeStruct


def call(name, kernel, out_shape, operands, after=(), scratch=(), limit=8 * mib, cost=None):
    many = isinstance(out_shape, tuple)
    return pl.pallas_call(
        kernel,
        out_shape=out_shape,
        in_specs=[in_vmem()] * len(operands) + [anywhere()] * len(after),
        out_specs=(in_vmem(),) * len(out_shape) if many else in_vmem(),
        scratch_shapes=list(scratch),
        compiler_params=pltpu.CompilerParams(vmem_limit_bytes=limit),
        cost_estimate=cost,
        name=name,
    )(*operands, *after)


def pack_kernel(g, tile_ref, count_ref, src_ref, bel_ref, dst_ref, grad_ref, src_pack, dst_pack, flags):
    rows, batch = g.rows, g.batch
    me = lax.axis_index("src")
    count = jnp.broadcast_to(count_ref[...], (1, g.width))
    for k in range(g.n):
        flags[pl.ds(tile_ref[0, k] ^ me, 1), :] = jnp.where(count > k, 1.0, 0.0).astype(f32)
    src_pack[:rows] = src_ref[...]
    src_pack[rows : rows + batch] = bel_ref[...]
    src_pack[rows + batch :] = flags[...].astype(bf16)
    dst_pack[:rows] = dst_ref[...]
    dst_pack[rows:] = grad_ref[...]


def pack(g, tile_dst, tile_count, src_emb, beliefs, dst_emb, grad_next):
    return pl.pallas_call(
        functools.partial(pack_kernel, g),
        out_shape=(
            shape((g.rows + g.batch + g.n, g.width), bf16),
            shape((g.rows + g.batch, g.width), bf16),
        ),
        in_specs=[in_smem()] + [in_vmem()] * 5,
        out_specs=(in_vmem(),) * 2,
        scratch_shapes=[pltpu.VMEM((g.n, g.width), f32)],
        compiler_params=pltpu.CompilerParams(vmem_limit_bytes=60 * mib),
        name="pack",
    )(tile_dst, tile_count.reshape(1, 1), src_emb, beliefs, dst_emb, grad_next)


def keep(src_pack, dst_pack, *after):
    def kernel(src_ref, dst_ref, *refs):
        refs[-2][...] = src_ref[...]
        refs[-1][...] = dst_ref[...]

    outs = (shape(src_pack.shape, bf16), shape(dst_pack.shape, bf16))
    return call("keep", kernel, outs, [src_pack, dst_pack], after, limit=2 * mib)


def hand(one, *after, cost=None):
    def kernel(one_ref, *refs):
        refs[-1][...] = one_ref[...]

    return call("hand", kernel, shape(one.shape, one.dtype), [one], after, limit=2 * mib, cost=cost)


def paired(block, small, *after):
    def kernel(block_ref, small_ref, *refs):
        refs[-1][: block.shape[0]] = block_ref[...]
        refs[-1][block.shape[0] :] = small_ref[...]

    out = shape((block.shape[0] + small.shape[0], block.shape[1]), bf16)
    return call("paired", kernel, out, [block, small], after, limit=2 * mib)


def stack(packs, *after):
    def kernel(*refs):
        for i in range(len(packs)):
            refs[-1][i] = refs[i][...]

    out = shape((len(packs),) + packs[0].shape, packs[0].dtype)
    return call("stack", kernel, out, packs, after)


def score_kernel(g, row_slots, slots, *refs):
    rows, batch, span = g.rows, g.batch, len(row_slots) * g.rows
    src_packs, stacks = refs[: len(row_slots)], refs[len(row_slots) :]
    prob_ref, grad_sum, stats, src_all, bel_all = refs[-5:]
    first = g.spots[slots[0]][0]
    listed = []
    for p, one in enumerate(src_packs):
        lanes = slice(p * rows, (p + 1) * rows)
        src_all[lanes] = one[:rows]
        bel_all[:, lanes] = one[rows : rows + batch]
        listed.append((one[rows + batch :].astype(f32) - 1.0) * unlisted)

    def packet(t):
        stack, place = g.spots[t]
        return stacks[stack - first].at[place]

    top = jnp.full((8, span), -unlisted, f32)
    for i, t in enumerate(slots):
        flips = [g.row_flip(s) | t for s in row_slots]
        bias = jnp.concatenate([one[v : v + 1] for one, v in zip(listed, flips)], axis=1)
        logits = dot(packet(t)[:rows], src_all[...], NT) + bias
        prob_ref[i * rows : (i + 1) * rows] = logits
        top = jnp.maximum(top, jnp.max(logits.reshape(rows // 8, 8, span), axis=0))
    top = jnp.max(top, axis=0, keepdims=True)
    total = jnp.zeros((8, span), f32)
    grad_sum[...] = jnp.zeros(grad_sum.shape, f32)
    for i, t in enumerate(slots):
        here = slice(i * rows, (i + 1) * rows)
        prob = jnp.exp(prob_ref[here] - top)
        prob_ref[here] = prob
        grad_sum[...] += dot(packet(t)[rows:], prob.astype(bf16), NN)
        total = total + jnp.sum(prob.reshape(rows // 8, 8, span), axis=0)
    stats[0:1] = top
    stats[1:2] = jnp.sum(total, axis=0, keepdims=True)
    stats[2:3] = jnp.sum(bel_all[...].astype(f32) * grad_sum[...], axis=0, keepdims=True)


def scores(g, row_slots, slots, src_packs, stacks, *after):
    tall, span = len(slots) * g.rows, len(row_slots) * g.rows
    outs = (shape((tall, span), f32), shape((g.batch, span), f32), shape((3, span), f32))
    scratch = [pltpu.VMEM((span, g.width), bf16), pltpu.VMEM((g.batch, span), bf16)]
    kernel = functools.partial(score_kernel, g, row_slots, slots)
    operands = [*[src_packs[s] for s in row_slots], *stacks]
    return call("scores", kernel, outs, operands, after, scratch, tall * span * 8 + 6 * mib)


def flat(parts):
    return [one for part in parts for one in part]


def unflat(refs, parts):
    out = []
    for part in parts:
        out.append(refs[: len(part)])
        refs = refs[len(part) :]
    return out, refs


def wide(refs, here=slice(None)):
    return jnp.concatenate([one[here] for one in refs], axis=1)


def merged(stats):
    tops = [one[0:1] for one in stats]
    top = functools.reduce(jnp.maximum, tops)
    factors = [jnp.exp(one - top) for one in tops]
    total = sum(factor * one[1:2] for factor, one in zip(factors, stats))
    dots = sum(factor * one[2:3] for factor, one in zip(factors, stats))
    return top, total, dots


def join(g, stats):
    def kernel(*refs):
        out = refs[-1]
        parts, _ = unflat(refs, stats)
        for kind, value in enumerate(merged([wide(one) for one in parts])):
            for s in range(g.n_row):
                at = kind * g.n_row + s
                out[at : at + 1] = value[:, s * g.rows : (s + 1) * g.rows]
        if g.head > 3 * g.n_row:
            out[3 * g.n_row :] = jnp.zeros((g.head - 3 * g.n_row, g.rows), f32)

    return call("join", kernel, shape((g.head, g.rows), f32), flat(stats), limit=2 * mib)


def stage(g, src_packs, stacks):
    rows, batch = g.rows, g.batch

    def kernel(*refs):
        src_refs, stack_refs = refs[: g.n_row], refs[g.n_row : -4]
        src_all, bel_all, *prob_grads = refs[-4:]
        for s, one in enumerate(src_refs):
            lanes = slice(s * rows, (s + 1) * rows)
            src_all[lanes] = one[:rows]
            bel_all[:, lanes] = one[rows : rows + batch]
        for slots, out in zip(g.parts, prob_grads):
            for i, t in enumerate(slots):
                stack, place = g.spots[t]
                out[i * rows : (i + 1) * rows] = dot(stack_refs[stack][place, rows:], bel_all[...], TN)

    outs = (
        shape((g.span, g.width), bf16),
        shape((batch, g.span), bf16),
        *[shape((len(part) * rows, g.span), f32) for part in g.parts],
    )
    limit = g.n * rows * rows * 4 + 8 * mib
    return call("stage", kernel, outs, [*src_packs, *stacks], limit=limit)


def norms(g, stats, grad_sums, messages):
    def kernel(*refs):
        part_stats, refs = unflat(refs, stats)
        part_sums, refs = unflat(refs, grad_sums)
        everyone, (factors, belief_sum) = refs[: g.n_row], refs[-2:]
        part_stats = [wide(one) for one in part_stats]
        for s in range(g.n_row):
            lanes = slice(s * g.rows, (s + 1) * g.rows)

            def row(u, kind):
                at = kind * g.n_row + (s ^ u)
                return everyone[u][at : at + 1]

            tops = [row(u, 0) for u in range(g.n_row)]
            top = functools.reduce(jnp.maximum, tops)
            shares = [jnp.exp(one - top) for one in tops]
            inverse = 1.0 / sum(share * row(u, 1) for u, share in enumerate(shares))
            for part, one in enumerate(part_stats):
                factors[part : part + 1, lanes] = jnp.exp(one[0:1, lanes] - top) * inverse
            dots = sum(share * row(u, 2) for u, share in enumerate(shares))
            factors[2:3, lanes] = dots * inverse
        belief_sum[...] = wide(part_sums[0]) * factors[0:1] + wide(part_sums[1]) * factors[1:2]

    outs = (shape((8, g.span), f32), shape((g.batch, g.span), f32))
    return call("norms", kernel, outs, [*flat(stats), *flat(grad_sums), *messages], limit=4 * mib)


def column_shares(g, slots, kind, factors, probs, prob_grads, src_all, bel_all, *after):
    rows = g.rows

    def kernel(factors, *refs):
        prob_refs, refs = unflat(refs, probs)
        prob_grads, (src_all, bel_all), (change_ref, share_ref) = refs[:2], refs[2:4], refs[-2:]
        for i, t in enumerate(slots):
            part, place = g.where(t)
            here = slice(place * rows, (place + 1) * rows)
            prob = wide(prob_refs[part], here) * factors[part : part + 1]
            change = (prob * (prob_grads[part][here] - factors[2:3])).astype(bf16)
            change_ref[i * rows : (i + 1) * rows] = change
            share_ref[i, :rows] = dot(change, src_all[...], NN).astype(kind)
            share_ref[i, rows:] = dot(bel_all[...], prob.astype(bf16), NT).astype(kind)

    outs = (
        shape((len(slots) * rows, g.span), bf16),
        shape((len(slots), g.packet, g.width), kind),
    )
    operands = [factors, *flat(probs), *prob_grads, src_all, bel_all]
    return call("column_shares", kernel, outs, operands, after, limit=g.n * rows * rows * 8 + 6 * mib)


def row_shares(g, slots, kind, changes, order, stacks, belief_sum, *after):
    rows = g.rows

    def kernel(*refs):
        changes = refs[: len(order)]
        stack_refs = refs[len(order) : len(order) + len(stacks)]
        belief_sum = refs[len(order) + len(stacks)]
        for s, out in zip(slots, refs[-len(slots) :]):
            lanes = slice(s * rows, (s + 1) * rows)
            total = 0.0
            for change, columns in zip(changes, order):
                for i, t in enumerate(columns):
                    stack, place = g.spots[t]
                    packet = stack_refs[stack][place, :rows]
                    total = total + dot(change[i * rows : (i + 1) * rows, lanes], packet, TN)
            out[:rows] = total.astype(kind)
            out[rows:] = belief_sum[:, lanes].astype(kind)

    outs = (shape((g.packet, g.width), kind),) * len(slots)
    operands = [*changes, *stacks, belief_sum]
    return call("row_shares", kernel, outs, operands, after, limit=g.n * rows * rows * 4 + 6 * mib)


def fold(own, near, i, piece, others, cost, *after):
    start, stop = piece

    def kernel(own_ref, near_ref, *refs):
        total = own_ref[i, start:stop] + near_ref[i, start:stop].astype(f32)
        for one in refs[: len(others)]:
            total = total + one[...].astype(f32)
        refs[-1][...] = total.astype(bf16)

    out = shape((stop - start, own.shape[2]), bf16)
    return call("fold", kernel, out, [own, near, *others], after, cost=cost)


def totals(g, src_own, src_others, dst_own, dst_near, dst_others):
    def kernel(*refs):
        src_out, belief_out, dst_out, next_out = refs[-4:]
        src_refs, refs = refs[: 1 + len(src_others)], refs[1 + len(src_others) : -4]
        own, near, parts = refs[0], refs[1], refs[2:]

        def src_total(here):
            return src_refs[0][here] + sum(one[here].astype(f32) for one in src_refs[1:])

        src_out[...] = src_total(slice(0, g.rows))
        belief_out[...] = src_total(slice(g.rows, g.packet)).astype(bf16)
        for start, stop in g.pieces:
            total = own[0, start:stop] + near[0, start:stop].astype(f32)
            for ((first, last), _), part in zip(dst_others, parts):
                if first <= start and stop <= last:
                    total = total + part[start - first : stop - first].astype(f32)
            edge = min(stop, g.rows)
            dst_out[start:edge] = total[: edge - start]
            if stop > g.rows:
                next_out[...] = total[g.rows - start :]

    outs = (
        shape((g.rows, g.width), f32),
        shape((g.batch, g.rows), bf16),
        shape((g.rows, g.width), f32),
        shape((g.batch, g.rows), f32),
    )
    operands = [src_own, *src_others, dst_own, dst_near, *[part for _, part in dst_others]]
    return call("totals", kernel, outs, operands, limit=12 * mib)


def per_device(n, src_emb, dst_emb, tile_dst, tile_count, beliefs, grad_next):
    g = Grid(n, *src_emb.shape, beliefs.shape[0])

    def swap(array, flip):
        return lax.ppermute(array, "src", [(i, i ^ flip) for i in range(n)])

    raw = {t: (swap(dst_emb, t), swap(grad_next, t)) for t in g.early[2:]}
    src_pack, dst_pack = pack(g, tile_dst, tile_count, src_emb, beliefs, dst_emb, grad_next)
    src_others = [swap(src_pack, g.row_flip(s)) for s in range(1, g.n_row)]
    packets = {2: swap(dst_pack, 2)}
    for t, (block, small) in raw.items():
        packets[t] = paired(block, small)
    src_kept, packets[0] = keep(src_pack, dst_pack, *[packets[t] for t in raw])
    src_packs = [src_kept] + src_others
    for t in sorted(g.late, key=lambda t: bin(t).count("1")):
        packets[t] = swap(packets[t ^ low_bit(t)], low_bit(t))
    stacks = []
    for slots in g.groups:
        pile = stack([packets[t] for t in slots], *(src_others if slots is g.late else ()))
        stacks += [pile, swap(pile, 1)]

    everyone = list(range(g.n_row))
    scored = [scores(g, everyone, g.parts[0], src_packs, stacks[:-2])]
    scored.append(scores(g, everyone, g.parts[1], src_packs, stacks[-2:], scored[0][2]))
    probs, grad_sums, stats = ([[one] for one in each] for each in zip(*scored))
    message = join(g, stats)
    messages = [message] + [swap(message, g.row_flip(s)) for s in range(1, g.n_row)]
    src_all, bel_all, *prob_grads = stage(g, src_packs, stacks)
    factors, belief_sum = norms(g, stats, grad_sums, messages)

    def columns(slots, kind, *after):
        return column_shares(g, slots, kind, factors, probs, prob_grads, src_all, bel_all, *after)

    odd_far, odd_near = ([t + 1 for t in slots] for slots in (g.far, g.near))
    change_of_far_odd, far_send = columns(odd_far, bf16)
    far_got = swap(far_send, 1)
    change_of_far, far_own = columns(g.far, f32, far_send)
    change_of_near_odd, near_send = columns(odd_near, bf16, far_own)
    near_got = swap(near_send, 1)
    change_of_near, near_own = columns(g.near, f32, near_send)
    changes = [change_of_far_odd, change_of_far, change_of_near_odd, change_of_near]
    order = [odd_far, g.far, odd_near, g.near]

    got = {t: [] for t in range(0, g.n_col, 2)}
    last = near_send
    early = pl.CostEstimate(flops=1000000000, bytes_accessed=1 << 20, transcendentals=0)
    slow = pl.CostEstimate(flops=3000000000, bytes_accessed=1 << 20, transcendentals=0)
    for t in reversed(range(2, g.n_col, 2)):
        own, near, slots = (far_own, far_got, g.far) if t in g.far else (near_own, near_got, g.near)
        for piece in g.pieces if t in g.far else [(0, g.packet)]:
            others = [one for at, one in got[t] if at == piece]
            cost = slow if low_bit(t) > 2 and piece[0] else None
            last = fold(own, near, slots.index(t), piece, others, cost, last)
            one = swap(last, low_bit(t))
            got[t ^ low_bit(t)].append((piece, hand(one, cost=early) if low_bit(t) > 2 else one))
        if t == g.n_col - 2:
            rest = list(range(1, g.n_row))
            src_send = row_shares(g, rest, bf16, changes, order, stacks, belief_sum, last)
            src_got = [hand(swap(one, g.row_flip(s)), cost=early) for one, s in zip(src_send, rest)]
        elif t == 4:
            (src_own,) = row_shares(g, [0], f32, changes, order, stacks, belief_sum, last)
            last = src_own
    grad_src, grad_belief, grad_dst, next_belief = totals(
        g, src_own, src_got, near_own, near_got, got[0][1::-1] + got[0][2:]
    )
    return (next_belief, grad_belief, grad_src, grad_dst)


def solution(mesh):
    placed = (
        P(("groups", "src"), None),
        P(("groups", "src"), None),
        P(("groups", "src"), None),
        P(("groups", "src")),
        P("groups", "src"),
        P("groups", "src"),
    )
    return jax.shard_map(
        functools.partial(per_device, mesh.shape["src"]),
        mesh=mesh,
        in_specs=placed,
        out_specs=(
            P("groups", "src"),
            P("groups", "src"),
            P(("groups", "src"), None),
            P(("groups", "src"), None),
        ),
        check_vma=False,
    )
```

```python
import functools

import jax
import jax.numpy as jnp
from jax import lax
from jax.experimental import pallas as pl
from jax.experimental.pallas import tpu as pltpu
from jax.sharding import PartitionSpec as P

f32 = jnp.float32
bf16 = jnp.bfloat16
unlisted = 1e30
mib = 1 << 20


class Grid:
    def __init__(self, n, rows, width, batch):
        bits = n.bit_length() - 1
        row_bits = max(1, bits // 2 - 1)
        self.n, self.rows, self.width, self.batch = n, rows, width, batch
        self.n_row = 1 << row_bits
        self.n_col = n // self.n_row
        self.span = self.n_row * rows
        self.packet = rows + batch
        self.head = (3 * self.n_row + 7) // 8 * 8
        cut = self.packet // 32 * 16 + 16
        self.pieces = [(0, cut), (cut, self.packet)]
        even = range(0, self.n_col, 2)
        self.early = [t for t in even if t & (t - 1) == 0]
        self.late = [t for t in even if t & (t - 1)]
        self.groups = [self.early[2:], [2], [0], self.late]
        both = [group + [t + 1 for t in group] for group in self.groups]
        self.parts = [both[0] + both[1] + both[2], both[3]]
        self.spots = {t: (2 * k + (t & 1), group.index(t & ~1)) for k, group in enumerate(self.groups) for t in both[k]}
        top = self.n_col // 2
        self.far = [t for t in range(top, self.n_col, 2)]
        self.near = [t for t in range(0, top, 2)]

    def row_flip(self, s):
        return s * self.n_col

    def where(self, t):
        part = 0 if t in self.parts[0] else 1
        return part, self.parts[part].index(t)


def low_bit(t):
    return t & -t


def dot(a, b, dims):
    return lax.dot_general(a, b, (dims, ((), ())), preferred_element_type=f32)


NN = ((1,), (0,))
NT = ((1,), (1,))
TN = ((0,), (0,))


def in_vmem():
    return pl.BlockSpec(memory_space=pltpu.VMEM)


def anywhere():
    return pl.BlockSpec(memory_space=pl.ANY)


def in_smem():
    return pl.BlockSpec(memory_space=pltpu.SMEM)


shape = jax.ShapeDtypeStruct


def call(name, kernel, out_shape, operands, after=(), scratch=(), limit=8 * mib, cost=None):
    many = isinstance(out_shape, tuple)
    return pl.pallas_call(
        kernel,
        out_shape=out_shape,
        in_specs=[in_vmem()] * len(operands) + [anywhere()] * len(after),
        out_specs=(in_vmem(),) * len(out_shape) if many else in_vmem(),
        scratch_shapes=list(scratch),
        compiler_params=pltpu.CompilerParams(vmem_limit_bytes=limit),
        cost_estimate=cost,
        name=name,
    )(*operands, *after)


def pack_kernel(g, tile_ref, count_ref, src_ref, bel_ref, dst_ref, grad_ref, src_pack, dst_pack, flags):
    rows, batch = g.rows, g.batch
    me = lax.axis_index("src")
    count = jnp.broadcast_to(count_ref[...], (1, g.width))
    for k in range(g.n):
        flags[pl.ds(tile_ref[0, k] ^ me, 1), :] = jnp.where(count > k, 1.0, 0.0).astype(f32)
    src_pack[:rows] = src_ref[...]
    src_pack[rows : rows + batch] = bel_ref[...]
    src_pack[rows + batch :] = flags[...].astype(bf16)
    dst_pack[:rows] = dst_ref[...]
    dst_pack[rows:] = grad_ref[...]


def pack(g, tile_dst, tile_count, src_emb, beliefs, dst_emb, grad_next):
    return pl.pallas_call(
        functools.partial(pack_kernel, g),
        out_shape=(
            shape((g.rows + g.batch + g.n, g.width), bf16),
            shape((g.rows + g.batch, g.width), bf16),
        ),
        in_specs=[in_smem()] + [in_vmem()] * 5,
        out_specs=(in_vmem(),) * 2,
        scratch_shapes=[pltpu.VMEM((g.n, g.width), f32)],
        compiler_params=pltpu.CompilerParams(vmem_limit_bytes=60 * mib),
        name="pack",
    )(tile_dst, tile_count.reshape(1, 1), src_emb, beliefs, dst_emb, grad_next)


def keep(src_pack, dst_pack, *after):
    def kernel(src_ref, dst_ref, *refs):
        refs[-2][...] = src_ref[...]
        refs[-1][...] = dst_ref[...]

    outs = (shape(src_pack.shape, bf16), shape(dst_pack.shape, bf16))
    return call("keep", kernel, outs, [src_pack, dst_pack], after, limit=2 * mib)


def hand(one, *after, cost=None):
    def kernel(one_ref, *refs):
        refs[-1][...] = one_ref[...]

    return call("hand", kernel, shape(one.shape, one.dtype), [one], after, limit=2 * mib, cost=cost)


def paired(block, small, *after):
    def kernel(block_ref, small_ref, *refs):
        refs[-1][: block.shape[0]] = block_ref[...]
        refs[-1][block.shape[0] :] = small_ref[...]

    out = shape((block.shape[0] + small.shape[0], block.shape[1]), bf16)
    return call("paired", kernel, out, [block, small], after, limit=2 * mib)


def stack(packs, *after):
    def kernel(*refs):
        for i in range(len(packs)):
            refs[-1][i] = refs[i][...]

    out = shape((len(packs),) + packs[0].shape, packs[0].dtype)
    return call("stack", kernel, out, packs, after)


def score_kernel(g, row_slots, slots, *refs):
    rows, batch, span = g.rows, g.batch, len(row_slots) * g.rows
    src_packs, stacks = refs[: len(row_slots)], refs[len(row_slots) :]
    prob_ref, grad_sum, stats, src_all, bel_all = refs[-5:]
    first = g.spots[slots[0]][0]
    listed = []
    for p, one in enumerate(src_packs):
        lanes = slice(p * rows, (p + 1) * rows)
        src_all[lanes] = one[:rows]
        bel_all[:, lanes] = one[rows : rows + batch]
        listed.append((one[rows + batch :].astype(f32) - 1.0) * unlisted)

    def packet(t):
        stack, place = g.spots[t]
        return stacks[stack - first].at[place]

    top = jnp.full((8, span), -unlisted, f32)
    for i, t in enumerate(slots):
        flips = [g.row_flip(s) | t for s in row_slots]
        bias = jnp.concatenate([one[v : v + 1] for one, v in zip(listed, flips)], axis=1)
        logits = dot(packet(t)[:rows], src_all[...], NT) + bias
        prob_ref[i * rows : (i + 1) * rows] = logits
        top = jnp.maximum(top, jnp.max(logits.reshape(rows // 8, 8, span), axis=0))
    top = jnp.max(top, axis=0, keepdims=True)
    total = jnp.zeros((8, span), f32)
    grad_sum[...] = jnp.zeros(grad_sum.shape, f32)
    for i, t in enumerate(slots):
        here = slice(i * rows, (i + 1) * rows)
        prob = jnp.exp(prob_ref[here] - top)
        prob_ref[here] = prob
        grad_sum[...] += dot(packet(t)[rows:], prob.astype(bf16), NN)
        total = total + jnp.sum(prob.reshape(rows // 8, 8, span), axis=0)
    stats[0:1] = top
    stats[1:2] = jnp.sum(total, axis=0, keepdims=True)
    stats[2:3] = jnp.sum(bel_all[...].astype(f32) * grad_sum[...], axis=0, keepdims=True)


def scores(g, row_slots, slots, src_packs, stacks, *after):
    tall, span = len(slots) * g.rows, len(row_slots) * g.rows
    outs = (shape((tall, span), f32), shape((g.batch, span), f32), shape((3, span), f32))
    scratch = [pltpu.VMEM((span, g.width), bf16), pltpu.VMEM((g.batch, span), bf16)]
    kernel = functools.partial(score_kernel, g, row_slots, slots)
    operands = [*[src_packs[s] for s in row_slots], *stacks]
    return call("scores", kernel, outs, operands, after, scratch, tall * span * 8 + 6 * mib)


def flat(parts):
    return [one for part in parts for one in part]


def unflat(refs, parts):
    out = []
    for part in parts:
        out.append(refs[: len(part)])
        refs = refs[len(part) :]
    return out, refs


def wide(refs, here=slice(None)):
    return jnp.concatenate([one[here] for one in refs], axis=1)


def merged(stats):
    tops = [one[0:1] for one in stats]
    top = functools.reduce(jnp.maximum, tops)
    factors = [jnp.exp(one - top) for one in tops]
    total = sum(factor * one[1:2] for factor, one in zip(factors, stats))
    dots = sum(factor * one[2:3] for factor, one in zip(factors, stats))
    return top, total, dots


def join(g, stats):
    def kernel(*refs):
        out = refs[-1]
        parts, _ = unflat(refs, stats)
        for kind, value in enumerate(merged([wide(one) for one in parts])):
            for s in range(g.n_row):
                at = kind * g.n_row + s
                out[at : at + 1] = value[:, s * g.rows : (s + 1) * g.rows]
        if g.head > 3 * g.n_row:
            out[3 * g.n_row :] = jnp.zeros((g.head - 3 * g.n_row, g.rows), f32)

    return call("join", kernel, shape((g.head, g.rows), f32), flat(stats), limit=2 * mib)


def stage(g, src_packs, stacks):
    rows, batch = g.rows, g.batch

    def kernel(*refs):
        src_refs, stack_refs = refs[: g.n_row], refs[g.n_row : -4]
        src_all, bel_all, *prob_grads = refs[-4:]
        for s, one in enumerate(src_refs):
            lanes = slice(s * rows, (s + 1) * rows)
            src_all[lanes] = one[:rows]
            bel_all[:, lanes] = one[rows : rows + batch]
        for slots, out in zip(g.parts, prob_grads):
            for i, t in enumerate(slots):
                stack, place = g.spots[t]
                out[i * rows : (i + 1) * rows] = dot(stack_refs[stack][place, rows:], bel_all[...], TN)

    outs = (
        shape((g.span, g.width), bf16),
        shape((batch, g.span), bf16),
        *[shape((len(part) * rows, g.span), f32) for part in g.parts],
    )
    limit = g.n * rows * rows * 4 + 8 * mib
    return call("stage", kernel, outs, [*src_packs, *stacks], limit=limit)


def norms(g, stats, grad_sums, messages):
    def kernel(*refs):
        part_stats, refs = unflat(refs, stats)
        part_sums, refs = unflat(refs, grad_sums)
        everyone, (factors, belief_sum) = refs[: g.n_row], refs[-2:]
        part_stats = [wide(one) for one in part_stats]
        for s in range(g.n_row):
            lanes = slice(s * g.rows, (s + 1) * g.rows)

            def row(u, kind):
                at = kind * g.n_row + (s ^ u)
                return everyone[u][at : at + 1]

            tops = [row(u, 0) for u in range(g.n_row)]
            top = functools.reduce(jnp.maximum, tops)
            shares = [jnp.exp(one - top) for one in tops]
            inverse = 1.0 / sum(share * row(u, 1) for u, share in enumerate(shares))
            for part, one in enumerate(part_stats):
                factors[part : part + 1, lanes] = jnp.exp(one[0:1, lanes] - top) * inverse
            dots = sum(share * row(u, 2) for u, share in enumerate(shares))
            factors[2:3, lanes] = dots * inverse
        belief_sum[...] = wide(part_sums[0]) * factors[0:1] + wide(part_sums[1]) * factors[1:2]

    outs = (shape((8, g.span), f32), shape((g.batch, g.span), f32))
    return call("norms", kernel, outs, [*flat(stats), *flat(grad_sums), *messages], limit=4 * mib)


def column_shares(g, slots, kind, factors, probs, prob_grads, src_all, bel_all, *after):
    rows = g.rows

    def kernel(factors, *refs):
        prob_refs, refs = unflat(refs, probs)
        prob_grads, (src_all, bel_all), (change_ref, share_ref) = refs[:2], refs[2:4], refs[-2:]
        for i, t in enumerate(slots):
            part, place = g.where(t)
            here = slice(place * rows, (place + 1) * rows)
            prob = wide(prob_refs[part], here) * factors[part : part + 1]
            change = (prob * (prob_grads[part][here] - factors[2:3])).astype(bf16)
            change_ref[i * rows : (i + 1) * rows] = change
            share_ref[i, :rows] = dot(change, src_all[...], NN).astype(kind)
            share_ref[i, rows:] = dot(bel_all[...], prob.astype(bf16), NT).astype(kind)

    outs = (
        shape((len(slots) * rows, g.span), bf16),
        shape((len(slots), g.packet, g.width), kind),
    )
    operands = [factors, *flat(probs), *prob_grads, src_all, bel_all]
    return call("column_shares", kernel, outs, operands, after, limit=g.n * rows * rows * 8 + 6 * mib)


def row_shares(g, slots, kind, changes, order, stacks, belief_sum, *after):
    rows = g.rows

    def kernel(*refs):
        changes = refs[: len(order)]
        stack_refs = refs[len(order) : len(order) + len(stacks)]
        belief_sum = refs[len(order) + len(stacks)]
        for s, out in zip(slots, refs[-len(slots) :]):
            lanes = slice(s * rows, (s + 1) * rows)
            total = 0.0
            for change, columns in zip(changes, order):
                for i, t in enumerate(columns):
                    stack, place = g.spots[t]
                    packet = stack_refs[stack][place, :rows]
                    total = total + dot(change[i * rows : (i + 1) * rows, lanes], packet, TN)
            out[:rows] = total.astype(kind)
            out[rows:] = belief_sum[:, lanes].astype(kind)

    outs = (shape((g.packet, g.width), kind),) * len(slots)
    operands = [*changes, *stacks, belief_sum]
    return call("row_shares", kernel, outs, operands, after, limit=g.n * rows * rows * 4 + 6 * mib)


def fold(own, near, i, piece, others, cost, *after):
    start, stop = piece

    def kernel(own_ref, near_ref, *refs):
        total = own_ref[i, start:stop] + near_ref[i, start:stop].astype(f32)
        for one in refs[: len(others)]:
            total = total + one[...].astype(f32)
        refs[-1][...] = total.astype(bf16)

    out = shape((stop - start, own.shape[2]), bf16)
    return call("fold", kernel, out, [own, near, *others], after, cost=cost)


def totals(g, src_own, src_others, dst_own, dst_near, dst_others):
    def kernel(*refs):
        src_out, belief_out, dst_out, next_out = refs[-4:]
        src_refs, refs = refs[: 1 + len(src_others)], refs[1 + len(src_others) : -4]
        own, near, parts = refs[0], refs[1], refs[2:]

        def src_total(here):
            return src_refs[0][here] + sum(one[here].astype(f32) for one in src_refs[1:])

        src_out[...] = src_total(slice(0, g.rows))
        belief_out[...] = src_total(slice(g.rows, g.packet)).astype(bf16)
        for start, stop in g.pieces:
            total = own[0, start:stop] + near[0, start:stop].astype(f32)
            for ((first, last), _), part in zip(dst_others, parts):
                if first <= start and stop <= last:
                    total = total + part[start - first : stop - first].astype(f32)
            edge = min(stop, g.rows)
            dst_out[start:edge] = total[: edge - start]
            if stop > g.rows:
                next_out[...] = total[g.rows - start :]

    outs = (
        shape((g.rows, g.width), f32),
        shape((g.batch, g.rows), bf16),
        shape((g.rows, g.width), f32),
        shape((g.batch, g.rows), f32),
    )
    operands = [src_own, *src_others, dst_own, dst_near, *[part for _, part in dst_others]]
    return call("totals", kernel, outs, operands, limit=12 * mib)


def per_device(n, src_emb, dst_emb, tile_dst, tile_count, beliefs, grad_next):
    g = Grid(n, *src_emb.shape, beliefs.shape[0])

    def swap(array, flip):
        return lax.ppermute(array, "src", [(i, i ^ flip) for i in range(n)])

    raw = {t: (swap(dst_emb, t), swap(grad_next, t)) for t in g.early[2:]}
    src_pack, dst_pack = pack(g, tile_dst, tile_count, src_emb, beliefs, dst_emb, grad_next)
    src_others = [swap(src_pack, g.row_flip(s)) for s in range(1, g.n_row)]
    packets = {2: swap(dst_pack, 2)}
    for t, (block, small) in raw.items():
        packets[t] = paired(block, small)
    src_kept, packets[0] = keep(src_pack, dst_pack, *[packets[t] for t in raw])
    src_packs = [src_kept] + src_others
    for t in sorted(g.late, key=lambda t: bin(t).count("1")):
        packets[t] = swap(packets[t ^ low_bit(t)], low_bit(t))
    stacks = []
    for slots in g.groups:
        pile = stack([packets[t] for t in slots], *(src_others if slots is g.late else ()))
        stacks += [pile, swap(pile, 1)]

    everyone = list(range(g.n_row))
    scored = [scores(g, everyone, g.parts[0], src_packs, stacks[:-2])]
    scored.append(scores(g, everyone, g.parts[1], src_packs, stacks[-2:], scored[0][2]))
    probs, grad_sums, stats = ([[one] for one in each] for each in zip(*scored))
    message = join(g, stats)
    messages = [message] + [swap(message, g.row_flip(s)) for s in range(1, g.n_row)]
    src_all, bel_all, *prob_grads = stage(g, src_packs, stacks)
    factors, belief_sum = norms(g, stats, grad_sums, messages)

    def columns(slots, kind, *after):
        return column_shares(g, slots, kind, factors, probs, prob_grads, src_all, bel_all, *after)

    odd_far, odd_near = ([t + 1 for t in slots] for slots in (g.far, g.near))
    change_of_far_odd, far_send = columns(odd_far, bf16)
    far_got = swap(far_send, 1)
    change_of_far, far_own = columns(g.far, f32, far_send)
    change_of_near_odd, near_send = columns(odd_near, bf16, far_own)
    near_got = swap(near_send, 1)
    change_of_near, near_own = columns(g.near, f32, near_send)
    changes = [change_of_far_odd, change_of_far, change_of_near_odd, change_of_near]
    order = [odd_far, g.far, odd_near, g.near]

    rest = list(range(1, g.n_row))
    src_send = row_shares(g, rest, bf16, changes, order, stacks, belief_sum)

    got = {t: [] for t in range(0, g.n_col, 2)}
    last = src_send[0]
    early = pl.CostEstimate(flops=1000000000, bytes_accessed=1 << 20, transcendentals=0)
    slow = pl.CostEstimate(flops=3000000000, bytes_accessed=1 << 20, transcendentals=0)
    for t in reversed(range(2, g.n_col, 2)):
        own, near, slots = (far_own, far_got, g.far) if t in g.far else (near_own, near_got, g.near)
        for piece in g.pieces if t in g.far else [(0, g.packet)]:
            others = [one for at, one in got[t] if at == piece]
            cost = slow if low_bit(t) > 2 and piece[0] else None
            last = fold(own, near, slots.index(t), piece, others, cost, last)
            one = swap(last, low_bit(t))
            got[t ^ low_bit(t)].append((piece, hand(one, cost=early) if low_bit(t) > 2 else one))
        if t == g.n_col - 2:
            src_got = [
                hand(swap(hand(one, last), g.row_flip(s)), cost=early) for one, s in zip(src_send, rest)
            ]
        elif t == 4:
            (src_own,) = row_shares(g, [0], f32, changes, order, stacks, belief_sum, last)
            last = src_own
    grad_src, grad_belief, grad_dst, next_belief = totals(
        g, src_own, src_got, near_own, near_got, got[0][1::-1] + got[0][2:]
    )
    return (next_belief, grad_belief, grad_src, grad_dst)


def solution(mesh):
    placed = (
        P(("groups", "src"), None),
        P(("groups", "src"), None),
        P(("groups", "src"), None),
        P(("groups", "src")),
        P("groups", "src"),
        P("groups", "src"),
    )
    return jax.shard_map(
        functools.partial(per_device, mesh.shape["src"]),
        mesh=mesh,
        in_specs=placed,
        out_specs=(
            P("groups", "src"),
            P("groups", "src"),
            P(("groups", "src"), None),
            P(("groups", "src"), None),
        ),
        check_vma=False,
    )
```

```python
import functools

import jax
import jax.numpy as jnp
from jax import lax
from jax.experimental import pallas as pl
from jax.experimental.pallas import tpu as pltpu
from jax.sharding import PartitionSpec as P

f32 = jnp.float32
bf16 = jnp.bfloat16
unlisted = 1e30
mib = 1 << 20


class Grid:
    def __init__(self, n, rows, width, batch):
        bits = n.bit_length() - 1
        row_bits = max(1, bits // 2 - 1)
        self.n, self.rows, self.width, self.batch = n, rows, width, batch
        self.n_row = 1 << row_bits
        self.n_col = n // self.n_row
        self.span = self.n_row * rows
        self.packet = rows + batch
        self.head = (3 * self.n_row + 7) // 8 * 8
        cut = self.packet // 32 * 16 + 16
        self.pieces = [(0, cut), (cut, self.packet)]
        even = range(0, self.n_col, 2)
        self.early = [t for t in even if t & (t - 1) == 0]
        self.late = [t for t in even if t & (t - 1)]
        self.groups = [self.early[2:], [2], [0], self.late]
        both = [group + [t + 1 for t in group] for group in self.groups]
        self.parts = [both[0] + both[1] + both[2], both[3]]
        self.spots = {t: (2 * k + (t & 1), group.index(t & ~1)) for k, group in enumerate(self.groups) for t in both[k]}
        top = self.n_col // 2
        self.far = [t for t in range(top, self.n_col, 2)]
        self.near = [t for t in range(0, top, 2)]

    def row_flip(self, s):
        return s * self.n_col

    def where(self, t):
        part = 0 if t in self.parts[0] else 1
        return part, self.parts[part].index(t)


def low_bit(t):
    return t & -t


def dot(a, b, dims):
    return lax.dot_general(a, b, (dims, ((), ())), preferred_element_type=f32)


NN = ((1,), (0,))
NT = ((1,), (1,))
TN = ((0,), (0,))


def in_vmem():
    return pl.BlockSpec(memory_space=pltpu.VMEM)


def anywhere():
    return pl.BlockSpec(memory_space=pl.ANY)


def in_smem():
    return pl.BlockSpec(memory_space=pltpu.SMEM)


shape = jax.ShapeDtypeStruct


def call(name, kernel, out_shape, operands, after=(), scratch=(), limit=8 * mib, cost=None):
    many = isinstance(out_shape, tuple)
    return pl.pallas_call(
        kernel,
        out_shape=out_shape,
        in_specs=[in_vmem()] * len(operands) + [anywhere()] * len(after),
        out_specs=(in_vmem(),) * len(out_shape) if many else in_vmem(),
        scratch_shapes=list(scratch),
        compiler_params=pltpu.CompilerParams(vmem_limit_bytes=limit),
        cost_estimate=cost,
        name=name,
    )(*operands, *after)


def pack_kernel(g, tile_ref, count_ref, src_ref, bel_ref, dst_ref, grad_ref, src_pack, dst_pack, flags):
    rows, batch = g.rows, g.batch
    me = lax.axis_index("src")
    count = jnp.broadcast_to(count_ref[...], (1, g.width))
    for k in range(g.n):
        flags[pl.ds(tile_ref[0, k] ^ me, 1), :] = jnp.where(count > k, 1.0, 0.0).astype(f32)
    src_pack[:rows] = src_ref[...]
    src_pack[rows : rows + batch] = bel_ref[...]
    src_pack[rows + batch :] = flags[...].astype(bf16)
    dst_pack[:rows] = dst_ref[...]
    dst_pack[rows:] = grad_ref[...]


def pack(g, tile_dst, tile_count, src_emb, beliefs, dst_emb, grad_next):
    return pl.pallas_call(
        functools.partial(pack_kernel, g),
        out_shape=(
            shape((g.rows + g.batch + g.n, g.width), bf16),
            shape((g.rows + g.batch, g.width), bf16),
        ),
        in_specs=[in_smem()] + [in_vmem()] * 5,
        out_specs=(in_vmem(),) * 2,
        scratch_shapes=[pltpu.VMEM((g.n, g.width), f32)],
        compiler_params=pltpu.CompilerParams(vmem_limit_bytes=60 * mib),
        name="pack",
    )(tile_dst, tile_count.reshape(1, 1), src_emb, beliefs, dst_emb, grad_next)


def keep(src_pack, dst_pack, *after):
    def kernel(src_ref, dst_ref, *refs):
        refs[-2][...] = src_ref[...]
        refs[-1][...] = dst_ref[...]

    outs = (shape(src_pack.shape, bf16), shape(dst_pack.shape, bf16))
    return call("keep", kernel, outs, [src_pack, dst_pack], after, limit=2 * mib)


def hand(one, *after, cost=None):
    def kernel(one_ref, *refs):
        refs[-1][...] = one_ref[...]

    return call("hand", kernel, shape(one.shape, one.dtype), [one], after, limit=2 * mib, cost=cost)


def paired(block, small, *after):
    def kernel(block_ref, small_ref, *refs):
        refs[-1][: block.shape[0]] = block_ref[...]
        refs[-1][block.shape[0] :] = small_ref[...]

    out = shape((block.shape[0] + small.shape[0], block.shape[1]), bf16)
    return call("paired", kernel, out, [block, small], after, limit=2 * mib)


def stack(packs, *after):
    def kernel(*refs):
        for i in range(len(packs)):
            refs[-1][i] = refs[i][...]

    out = shape((len(packs),) + packs[0].shape, packs[0].dtype)
    return call("stack", kernel, out, packs, after)


def score_kernel(g, row_slots, slots, *refs):
    rows, batch, span = g.rows, g.batch, len(row_slots) * g.rows
    src_packs, stacks = refs[: len(row_slots)], refs[len(row_slots) :]
    prob_ref, grad_sum, stats, src_all, bel_all = refs[-5:]
    first = g.spots[slots[0]][0]
    listed = []
    for p, one in enumerate(src_packs):
        lanes = slice(p * rows, (p + 1) * rows)
        src_all[lanes] = one[:rows]
        bel_all[:, lanes] = one[rows : rows + batch]
        listed.append((one[rows + batch :].astype(f32) - 1.0) * unlisted)

    def packet(t):
        stack, place = g.spots[t]
        return stacks[stack - first].at[place]

    top = jnp.full((8, span), -unlisted, f32)
    for i, t in enumerate(slots):
        flips = [g.row_flip(s) | t for s in row_slots]
        bias = jnp.concatenate([one[v : v + 1] for one, v in zip(listed, flips)], axis=1)
        logits = dot(packet(t)[:rows], src_all[...], NT) + bias
        prob_ref[i * rows : (i + 1) * rows] = logits
        top = jnp.maximum(top, jnp.max(logits.reshape(rows // 8, 8, span), axis=0))
    top = jnp.max(top, axis=0, keepdims=True)
    total = jnp.zeros((8, span), f32)
    grad_sum[...] = jnp.zeros(grad_sum.shape, f32)
    for i, t in enumerate(slots):
        here = slice(i * rows, (i + 1) * rows)
        prob = jnp.exp(prob_ref[here] - top)
        prob_ref[here] = prob
        grad_sum[...] += dot(packet(t)[rows:], prob.astype(bf16), NN)
        total = total + jnp.sum(prob.reshape(rows // 8, 8, span), axis=0)
    stats[0:1] = top
    stats[1:2] = jnp.sum(total, axis=0, keepdims=True)
    stats[2:3] = jnp.sum(bel_all[...].astype(f32) * grad_sum[...], axis=0, keepdims=True)


def scores(g, row_slots, slots, src_packs, stacks, *after):
    tall, span = len(slots) * g.rows, len(row_slots) * g.rows
    outs = (shape((tall, span), f32), shape((g.batch, span), f32), shape((3, span), f32))
    scratch = [pltpu.VMEM((span, g.width), bf16), pltpu.VMEM((g.batch, span), bf16)]
    kernel = functools.partial(score_kernel, g, row_slots, slots)
    operands = [*[src_packs[s] for s in row_slots], *stacks]
    return call("scores", kernel, outs, operands, after, scratch, tall * span * 8 + 6 * mib)


def flat(parts):
    return [one for part in parts for one in part]


def unflat(refs, parts):
    out = []
    for part in parts:
        out.append(refs[: len(part)])
        refs = refs[len(part) :]
    return out, refs


def wide(refs, here=slice(None)):
    return jnp.concatenate([one[here] for one in refs], axis=1)


def merged(stats):
    tops = [one[0:1] for one in stats]
    top = functools.reduce(jnp.maximum, tops)
    factors = [jnp.exp(one - top) for one in tops]
    total = sum(factor * one[1:2] for factor, one in zip(factors, stats))
    dots = sum(factor * one[2:3] for factor, one in zip(factors, stats))
    return top, total, dots


def join(g, stats):
    def kernel(*refs):
        out = refs[-1]
        parts, _ = unflat(refs, stats)
        for kind, value in enumerate(merged([wide(one) for one in parts])):
            for s in range(g.n_row):
                at = kind * g.n_row + s
                out[at : at + 1] = value[:, s * g.rows : (s + 1) * g.rows]
        if g.head > 3 * g.n_row:
            out[3 * g.n_row :] = jnp.zeros((g.head - 3 * g.n_row, g.rows), f32)

    return call("join", kernel, shape((g.head, g.rows), f32), flat(stats), limit=2 * mib)


def stage(g, src_packs, stacks):
    rows, batch = g.rows, g.batch

    def kernel(*refs):
        src_refs, stack_refs = refs[: g.n_row], refs[g.n_row : -4]
        src_all, bel_all, *prob_grads = refs[-4:]
        for s, one in enumerate(src_refs):
            lanes = slice(s * rows, (s + 1) * rows)
            src_all[lanes] = one[:rows]
            bel_all[:, lanes] = one[rows : rows + batch]
        for slots, out in zip(g.parts, prob_grads):
            for i, t in enumerate(slots):
                stack, place = g.spots[t]
                out[i * rows : (i + 1) * rows] = dot(stack_refs[stack][place, rows:], bel_all[...], TN)

    outs = (
        shape((g.span, g.width), bf16),
        shape((batch, g.span), bf16),
        *[shape((len(part) * rows, g.span), f32) for part in g.parts],
    )
    limit = g.n * rows * rows * 4 + 8 * mib
    return call("stage", kernel, outs, [*src_packs, *stacks], limit=limit)


def norms(g, stats, grad_sums, messages):
    def kernel(*refs):
        part_stats, refs = unflat(refs, stats)
        part_sums, refs = unflat(refs, grad_sums)
        everyone, (factors, belief_sum) = refs[: g.n_row], refs[-2:]
        part_stats = [wide(one) for one in part_stats]
        for s in range(g.n_row):
            lanes = slice(s * g.rows, (s + 1) * g.rows)

            def row(u, kind):
                at = kind * g.n_row + (s ^ u)
                return everyone[u][at : at + 1]

            tops = [row(u, 0) for u in range(g.n_row)]
            top = functools.reduce(jnp.maximum, tops)
            shares = [jnp.exp(one - top) for one in tops]
            inverse = 1.0 / sum(share * row(u, 1) for u, share in enumerate(shares))
            for part, one in enumerate(part_stats):
                factors[part : part + 1, lanes] = jnp.exp(one[0:1, lanes] - top) * inverse
            dots = sum(share * row(u, 2) for u, share in enumerate(shares))
            factors[2:3, lanes] = dots * inverse
        belief_sum[...] = wide(part_sums[0]) * factors[0:1] + wide(part_sums[1]) * factors[1:2]

    outs = (shape((8, g.span), f32), shape((g.batch, g.span), f32))
    return call("norms", kernel, outs, [*flat(stats), *flat(grad_sums), *messages], limit=4 * mib)


def column_shares(g, slots, kind, factors, probs, prob_grads, src_all, bel_all, *after):
    rows = g.rows

    def kernel(factors, *refs):
        prob_refs, refs = unflat(refs, probs)
        prob_grads, (src_all, bel_all), (change_ref, share_ref) = refs[:2], refs[2:4], refs[-2:]
        for i, t in enumerate(slots):
            part, place = g.where(t)
            here = slice(place * rows, (place + 1) * rows)
            prob = wide(prob_refs[part], here) * factors[part : part + 1]
            change = (prob * (prob_grads[part][here] - factors[2:3])).astype(bf16)
            change_ref[i * rows : (i + 1) * rows] = change
            share_ref[i, :rows] = dot(change, src_all[...], NN).astype(kind)
            share_ref[i, rows:] = dot(bel_all[...], prob.astype(bf16), NT).astype(kind)

    outs = (
        shape((len(slots) * rows, g.span), bf16),
        shape((len(slots), g.packet, g.width), kind),
    )
    operands = [factors, *flat(probs), *prob_grads, src_all, bel_all]
    return call("column_shares", kernel, outs, operands, after, limit=g.n * rows * rows * 8 + 6 * mib)


def row_shares(g, slots, kind, changes, order, stacks, belief_sum, *after):
    rows = g.rows

    def kernel(*refs):
        changes = refs[: len(order)]
        stack_refs = refs[len(order) : len(order) + len(stacks)]
        belief_sum = refs[len(order) + len(stacks)]
        for s, out in zip(slots, refs[-len(slots) :]):
            lanes = slice(s * rows, (s + 1) * rows)
            total = 0.0
            for change, columns in zip(changes, order):
                for i, t in enumerate(columns):
                    stack, place = g.spots[t]
                    packet = stack_refs[stack][place, :rows]
                    total = total + dot(change[i * rows : (i + 1) * rows, lanes], packet, TN)
            out[:rows] = total.astype(kind)
            out[rows:] = belief_sum[:, lanes].astype(kind)

    outs = (shape((g.packet, g.width), kind),) * len(slots)
    operands = [*changes, *stacks, belief_sum]
    return call("row_shares", kernel, outs, operands, after, limit=g.n * rows * rows * 4 + 6 * mib)


def fold(own, near, i, piece, others, cost, *after):
    start, stop = piece

    def kernel(own_ref, near_ref, *refs):
        total = own_ref[i, start:stop] + near_ref[i, start:stop].astype(f32)
        for one in refs[: len(others)]:
            total = total + one[...].astype(f32)
        refs[-1][...] = total.astype(bf16)

    out = shape((stop - start, own.shape[2]), bf16)
    return call("fold", kernel, out, [own, near, *others], after, cost=cost)


def totals(g, src_own, src_others, dst_own, dst_near, dst_others):
    def kernel(*refs):
        src_out, belief_out, dst_out, next_out = refs[-4:]
        src_refs, refs = refs[: 1 + len(src_others)], refs[1 + len(src_others) : -4]
        own, near, parts = refs[0], refs[1], refs[2:]

        def src_total(here):
            return src_refs[0][here] + sum(one[here].astype(f32) for one in src_refs[1:])

        src_out[...] = src_total(slice(0, g.rows))
        belief_out[...] = src_total(slice(g.rows, g.packet)).astype(bf16)
        for start, stop in g.pieces:
            total = own[0, start:stop] + near[0, start:stop].astype(f32)
            for ((first, last), _), part in zip(dst_others, parts):
                if first <= start and stop <= last:
                    total = total + part[start - first : stop - first].astype(f32)
            edge = min(stop, g.rows)
            dst_out[start:edge] = total[: edge - start]
            if stop > g.rows:
                next_out[...] = total[g.rows - start :]

    outs = (
        shape((g.rows, g.width), f32),
        shape((g.batch, g.rows), bf16),
        shape((g.rows, g.width), f32),
        shape((g.batch, g.rows), f32),
    )
    operands = [src_own, *src_others, dst_own, dst_near, *[part for _, part in dst_others]]
    return call("totals", kernel, outs, operands, limit=12 * mib)


def per_device(n, src_emb, dst_emb, tile_dst, tile_count, beliefs, grad_next):
    g = Grid(n, *src_emb.shape, beliefs.shape[0])

    def swap(array, flip):
        return lax.ppermute(array, "src", [(i, i ^ flip) for i in range(n)])

    raw = {t: (swap(dst_emb, t), swap(grad_next, t)) for t in g.early[2:]}
    src_pack, dst_pack = pack(g, tile_dst, tile_count, src_emb, beliefs, dst_emb, grad_next)
    src_others = [swap(src_pack, g.row_flip(s)) for s in range(1, g.n_row)]
    packets = {2: swap(dst_pack, 2)}
    for t, (block, small) in raw.items():
        packets[t] = paired(block, small)
    src_kept, packets[0] = keep(src_pack, dst_pack, *[packets[t] for t in raw])
    src_packs = [src_kept] + src_others
    for t in sorted(g.late, key=lambda t: bin(t).count("1")):
        packets[t] = swap(packets[t ^ low_bit(t)], low_bit(t))
    stacks = []
    for slots in g.groups:
        pile = stack([packets[t] for t in slots], *(src_others if slots is g.late else ()))
        stacks += [pile, swap(pile, 1)]

    everyone = list(range(g.n_row))
    scored = [scores(g, everyone, g.parts[0], src_packs, stacks[:-2])]
    scored.append(scores(g, everyone, g.parts[1], src_packs, stacks[-2:], scored[0][2]))
    probs, grad_sums, stats = ([[one] for one in each] for each in zip(*scored))
    message = join(g, stats)
    messages = [message] + [swap(message, g.row_flip(s)) for s in range(1, g.n_row)]
    src_all, bel_all, *prob_grads = stage(g, src_packs, stacks)
    factors, belief_sum = norms(g, stats, grad_sums, messages)

    def columns(slots, kind, *after):
        return column_shares(g, slots, kind, factors, probs, prob_grads, src_all, bel_all, *after)

    odd_far, odd_near = ([t + 1 for t in slots] for slots in (g.far, g.near))
    change_of_far_odd, far_send = columns(odd_far, bf16)
    far_got = swap(far_send, 1)
    change_of_far, far_own = columns(g.far, f32, far_send)
    change_of_near_odd, near_send = columns(odd_near, bf16, far_own)
    near_got = swap(near_send, 1)
    change_of_near, near_own = columns(g.near, f32, near_send)
    changes = [change_of_far_odd, change_of_far, change_of_near_odd, change_of_near]
    order = [odd_far, g.far, odd_near, g.near]

    rest = list(range(1, g.n_row))
    src_send = row_shares(g, rest, bf16, changes, order, stacks, belief_sum)

    got = {t: [] for t in range(0, g.n_col, 2)}
    last = src_send[0]
    early = pl.CostEstimate(flops=1000000000, bytes_accessed=1 << 20, transcendentals=0)
    slow = pl.CostEstimate(flops=3000000000, bytes_accessed=1 << 20, transcendentals=0)
    for t in reversed(range(2, g.n_col, 2)):
        own, near, slots = (far_own, far_got, g.far) if t in g.far else (near_own, near_got, g.near)
        for piece in g.pieces if t in g.far else [(0, g.packet)]:
            others = [one for at, one in got[t] if at == piece]
            cost = slow if low_bit(t) > 2 and piece[0] else None
            last = fold(own, near, slots.index(t), piece, others, cost, last)
            one = swap(last, low_bit(t))
            got[t ^ low_bit(t)].append((piece, hand(one, cost=early) if low_bit(t) > 2 else one))
        if t == g.n_col - 2:
            src_got = [
                hand(swap(hand(one, last), g.row_flip(s)), cost=early) for one, s in zip(src_send, rest)
            ]
        elif t == 4:
            (src_own,) = row_shares(g, [0], f32, changes, order, stacks, belief_sum, last)
    grad_src, grad_belief, grad_dst, next_belief = totals(
        g, src_own, src_got, near_own, near_got, got[0][1::-1] + got[0][2:]
    )
    return (next_belief, grad_belief, grad_src, grad_dst)


def solution(mesh):
    placed = (
        P(("groups", "src"), None),
        P(("groups", "src"), None),
        P(("groups", "src"), None),
        P(("groups", "src")),
        P("groups", "src"),
        P("groups", "src"),
    )
    return jax.shard_map(
        functools.partial(per_device, mesh.shape["src"]),
        mesh=mesh,
        in_specs=placed,
        out_specs=(
            P("groups", "src"),
            P("groups", "src"),
            P(("groups", "src"), None),
            P(("groups", "src"), None),
        ),
        check_vma=False,
    )
```

```python
import functools

import jax
import jax.numpy as jnp
from jax import lax
from jax.experimental import pallas as pl
from jax.experimental.pallas import tpu as pltpu
from jax.sharding import PartitionSpec as P

f32 = jnp.float32
bf16 = jnp.bfloat16
unlisted = 1e30
mib = 1 << 20


class Grid:
    def __init__(self, n, rows, width, batch):
        bits = n.bit_length() - 1
        row_bits = max(1, bits // 2 - 1)
        self.n, self.rows, self.width, self.batch = n, rows, width, batch
        self.n_row = 1 << row_bits
        self.n_col = n // self.n_row
        self.span = self.n_row * rows
        self.packet = rows + batch
        self.head = (3 * self.n_row + 7) // 8 * 8
        cut = self.packet // 32 * 16 + 16
        self.pieces = [(0, cut), (cut, self.packet)]
        even = range(0, self.n_col, 2)
        self.early = [t for t in even if t & (t - 1) == 0]
        self.late = [t for t in even if t & (t - 1)]
        self.groups = [self.early[2:], [2], [0], self.late]
        both = [group + [t + 1 for t in group] for group in self.groups]
        self.parts = [both[0] + both[1] + both[2], both[3]]
        self.spots = {t: (2 * k + (t & 1), group.index(t & ~1)) for k, group in enumerate(self.groups) for t in both[k]}
        top = self.n_col // 2
        self.far = [t for t in range(top, self.n_col, 2)]
        self.near = [t for t in range(0, top, 2)]

    def row_flip(self, s):
        return s * self.n_col

    def where(self, t):
        part = 0 if t in self.parts[0] else 1
        return part, self.parts[part].index(t)


def low_bit(t):
    return t & -t


def dot(a, b, dims):
    return lax.dot_general(a, b, (dims, ((), ())), preferred_element_type=f32)


NN = ((1,), (0,))
NT = ((1,), (1,))
TN = ((0,), (0,))


def in_vmem():
    return pl.BlockSpec(memory_space=pltpu.VMEM)


def anywhere():
    return pl.BlockSpec(memory_space=pl.ANY)


def in_smem():
    return pl.BlockSpec(memory_space=pltpu.SMEM)


shape = jax.ShapeDtypeStruct


def call(name, kernel, out_shape, operands, after=(), scratch=(), limit=8 * mib, cost=None):
    many = isinstance(out_shape, tuple)
    return pl.pallas_call(
        kernel,
        out_shape=out_shape,
        in_specs=[in_vmem()] * len(operands) + [anywhere()] * len(after),
        out_specs=(in_vmem(),) * len(out_shape) if many else in_vmem(),
        scratch_shapes=list(scratch),
        compiler_params=pltpu.CompilerParams(vmem_limit_bytes=limit),
        cost_estimate=cost,
        name=name,
    )(*operands, *after)


def pack_kernel(g, tile_ref, count_ref, src_ref, bel_ref, dst_ref, grad_ref, src_pack, dst_pack, flags):
    rows, batch = g.rows, g.batch
    me = lax.axis_index("src")
    count = jnp.broadcast_to(count_ref[...], (1, g.width))
    for k in range(g.n):
        flags[pl.ds(tile_ref[0, k] ^ me, 1), :] = jnp.where(count > k, 1.0, 0.0).astype(f32)
    src_pack[:rows] = src_ref[...]
    src_pack[rows : rows + batch] = bel_ref[...]
    src_pack[rows + batch :] = flags[...].astype(bf16)
    dst_pack[:rows] = dst_ref[...]
    dst_pack[rows:] = grad_ref[...]


def pack(g, tile_dst, tile_count, src_emb, beliefs, dst_emb, grad_next):
    return pl.pallas_call(
        functools.partial(pack_kernel, g),
        out_shape=(
            shape((g.rows + g.batch + g.n, g.width), bf16),
            shape((g.rows + g.batch, g.width), bf16),
        ),
        in_specs=[in_smem()] + [in_vmem()] * 5,
        out_specs=(in_vmem(),) * 2,
        scratch_shapes=[pltpu.VMEM((g.n, g.width), f32)],
        compiler_params=pltpu.CompilerParams(vmem_limit_bytes=60 * mib),
        name="pack",
    )(tile_dst, tile_count.reshape(1, 1), src_emb, beliefs, dst_emb, grad_next)


def keep(src_pack, dst_pack, *after):
    def kernel(src_ref, dst_ref, *refs):
        refs[-2][...] = src_ref[...]
        refs[-1][...] = dst_ref[...]

    outs = (shape(src_pack.shape, bf16), shape(dst_pack.shape, bf16))
    return call("keep", kernel, outs, [src_pack, dst_pack], after, limit=2 * mib)


def hand(one, *after, cost=None):
    def kernel(one_ref, *refs):
        refs[-1][...] = one_ref[...]

    return call("hand", kernel, shape(one.shape, one.dtype), [one], after, limit=2 * mib, cost=cost)


def paired(block, small, *after):
    def kernel(block_ref, small_ref, *refs):
        refs[-1][: block.shape[0]] = block_ref[...]
        refs[-1][block.shape[0] :] = small_ref[...]

    out = shape((block.shape[0] + small.shape[0], block.shape[1]), bf16)
    return call("paired", kernel, out, [block, small], after, limit=2 * mib)


def stack(packs, *after):
    def kernel(*refs):
        for i in range(len(packs)):
            refs[-1][i] = refs[i][...]

    out = shape((len(packs),) + packs[0].shape, packs[0].dtype)
    return call("stack", kernel, out, packs, after)


def score_kernel(g, row_slots, slots, *refs):
    rows, batch, span = g.rows, g.batch, len(row_slots) * g.rows
    src_packs, stacks = refs[: len(row_slots)], refs[len(row_slots) :]
    prob_ref, grad_sum, stats, src_all, bel_all = refs[-5:]
    first = g.spots[slots[0]][0]
    listed = []
    for p, one in enumerate(src_packs):
        lanes = slice(p * rows, (p + 1) * rows)
        src_all[lanes] = one[:rows]
        bel_all[:, lanes] = one[rows : rows + batch]
        listed.append((one[rows + batch :].astype(f32) - 1.0) * unlisted)

    def packet(t):
        stack, place = g.spots[t]
        return stacks[stack - first].at[place]

    top = jnp.full((8, span), -unlisted, f32)
    for i, t in enumerate(slots):
        flips = [g.row_flip(s) | t for s in row_slots]
        bias = jnp.concatenate([one[v : v + 1] for one, v in zip(listed, flips)], axis=1)
        logits = dot(packet(t)[:rows], src_all[...], NT) + bias
        prob_ref[i * rows : (i + 1) * rows] = logits
        top = jnp.maximum(top, jnp.max(logits.reshape(rows // 8, 8, span), axis=0))
    top = jnp.max(top, axis=0, keepdims=True)
    total = jnp.zeros((8, span), f32)
    grad_sum[...] = jnp.zeros(grad_sum.shape, f32)
    for i, t in enumerate(slots):
        here = slice(i * rows, (i + 1) * rows)
        prob = jnp.exp(prob_ref[here] - top)
        prob_ref[here] = prob
        grad_sum[...] += dot(packet(t)[rows:], prob.astype(bf16), NN)
        total = total + jnp.sum(prob.reshape(rows // 8, 8, span), axis=0)
    stats[0:1] = top
    stats[1:2] = jnp.sum(total, axis=0, keepdims=True)
    stats[2:3] = jnp.sum(bel_all[...].astype(f32) * grad_sum[...], axis=0, keepdims=True)


def scores(g, row_slots, slots, src_packs, stacks, *after):
    tall, span = len(slots) * g.rows, len(row_slots) * g.rows
    outs = (shape((tall, span), f32), shape((g.batch, span), f32), shape((3, span), f32))
    scratch = [pltpu.VMEM((span, g.width), bf16), pltpu.VMEM((g.batch, span), bf16)]
    kernel = functools.partial(score_kernel, g, row_slots, slots)
    operands = [*[src_packs[s] for s in row_slots], *stacks]
    cost = pl.CostEstimate(flops=tall * span * 128, bytes_accessed=4 * tall * span, transcendentals=0)
    return call("scores", kernel, outs, operands, after, scratch, tall * span * 8 + 6 * mib, cost)


def flat(parts):
    return [one for part in parts for one in part]


def unflat(refs, parts):
    out = []
    for part in parts:
        out.append(refs[: len(part)])
        refs = refs[len(part) :]
    return out, refs


def wide(refs, here=slice(None)):
    return jnp.concatenate([one[here] for one in refs], axis=1)


def merged(stats):
    tops = [one[0:1] for one in stats]
    top = functools.reduce(jnp.maximum, tops)
    factors = [jnp.exp(one - top) for one in tops]
    total = sum(factor * one[1:2] for factor, one in zip(factors, stats))
    dots = sum(factor * one[2:3] for factor, one in zip(factors, stats))
    return top, total, dots


def join(g, stats):
    def kernel(*refs):
        out = refs[-1]
        parts, _ = unflat(refs, stats)
        for kind, value in enumerate(merged([wide(one) for one in parts])):
            for s in range(g.n_row):
                at = kind * g.n_row + s
                out[at : at + 1] = value[:, s * g.rows : (s + 1) * g.rows]
        if g.head > 3 * g.n_row:
            out[3 * g.n_row :] = jnp.zeros((g.head - 3 * g.n_row, g.rows), f32)

    return call("join", kernel, shape((g.head, g.rows), f32), flat(stats), limit=2 * mib)


def stage(g, src_packs, stacks):
    rows, batch = g.rows, g.batch

    def kernel(*refs):
        src_refs, stack_refs = refs[: g.n_row], refs[g.n_row : -4]
        src_all, bel_all, *prob_grads = refs[-4:]
        for s, one in enumerate(src_refs):
            lanes = slice(s * rows, (s + 1) * rows)
            src_all[lanes] = one[:rows]
            bel_all[:, lanes] = one[rows : rows + batch]
        for slots, out in zip(g.parts, prob_grads):
            for i, t in enumerate(slots):
                stack, place = g.spots[t]
                out[i * rows : (i + 1) * rows] = dot(stack_refs[stack][place, rows:], bel_all[...], TN)

    outs = (
        shape((g.span, g.width), bf16),
        shape((batch, g.span), bf16),
        *[shape((len(part) * rows, g.span), f32) for part in g.parts],
    )
    limit = g.n * rows * rows * 4 + 8 * mib
    return call("stage", kernel, outs, [*src_packs, *stacks], limit=limit)


def norms(g, stats, grad_sums, messages):
    def kernel(*refs):
        part_stats, refs = unflat(refs, stats)
        part_sums, refs = unflat(refs, grad_sums)
        everyone, (factors, belief_sum) = refs[: g.n_row], refs[-2:]
        part_stats = [wide(one) for one in part_stats]
        for s in range(g.n_row):
            lanes = slice(s * g.rows, (s + 1) * g.rows)

            def row(u, kind):
                at = kind * g.n_row + (s ^ u)
                return everyone[u][at : at + 1]

            tops = [row(u, 0) for u in range(g.n_row)]
            top = functools.reduce(jnp.maximum, tops)
            shares = [jnp.exp(one - top) for one in tops]
            inverse = 1.0 / sum(share * row(u, 1) for u, share in enumerate(shares))
            for part, one in enumerate(part_stats):
                factors[part : part + 1, lanes] = jnp.exp(one[0:1, lanes] - top) * inverse
            dots = sum(share * row(u, 2) for u, share in enumerate(shares))
            factors[2:3, lanes] = dots * inverse
        belief_sum[...] = wide(part_sums[0]) * factors[0:1] + wide(part_sums[1]) * factors[1:2]

    outs = (shape((8, g.span), f32), shape((g.batch, g.span), f32))
    return call("norms", kernel, outs, [*flat(stats), *flat(grad_sums), *messages], limit=4 * mib)


def column_shares(g, slots, kind, factors, probs, prob_grads, src_all, bel_all, *after):
    rows = g.rows

    def kernel(factors, *refs):
        prob_refs, refs = unflat(refs, probs)
        prob_grads, (src_all, bel_all), (change_ref, share_ref) = refs[:2], refs[2:4], refs[-2:]
        for i, t in enumerate(slots):
            part, place = g.where(t)
            here = slice(place * rows, (place + 1) * rows)
            prob = wide(prob_refs[part], here) * factors[part : part + 1]
            change = (prob * (prob_grads[part][here] - factors[2:3])).astype(bf16)
            change_ref[i * rows : (i + 1) * rows] = change
            share_ref[i, :rows] = dot(change, src_all[...], NN).astype(kind)
            share_ref[i, rows:] = dot(bel_all[...], prob.astype(bf16), NT).astype(kind)

    outs = (
        shape((len(slots) * rows, g.span), bf16),
        shape((len(slots), g.packet, g.width), kind),
    )
    operands = [factors, *flat(probs), *prob_grads, src_all, bel_all]
    return call("column_shares", kernel, outs, operands, after, limit=g.n * rows * rows * 8 + 6 * mib)


def row_shares(g, slots, kind, changes, order, stacks, belief_sum, *after):
    rows = g.rows

    def kernel(*refs):
        changes = refs[: len(order)]
        stack_refs = refs[len(order) : len(order) + len(stacks)]
        belief_sum = refs[len(order) + len(stacks)]
        for s, out in zip(slots, refs[-len(slots) :]):
            lanes = slice(s * rows, (s + 1) * rows)
            total = 0.0
            for change, columns in zip(changes, order):
                for i, t in enumerate(columns):
                    stack, place = g.spots[t]
                    packet = stack_refs[stack][place, :rows]
                    total = total + dot(change[i * rows : (i + 1) * rows, lanes], packet, TN)
            out[:rows] = total.astype(kind)
            out[rows:] = belief_sum[:, lanes].astype(kind)

    outs = (shape((g.packet, g.width), kind),) * len(slots)
    operands = [*changes, *stacks, belief_sum]
    return call("row_shares", kernel, outs, operands, after, limit=g.n * rows * rows * 4 + 6 * mib)


def fold(own, near, i, piece, others, cost, *after):
    start, stop = piece

    def kernel(own_ref, near_ref, *refs):
        total = own_ref[i, start:stop] + near_ref[i, start:stop].astype(f32)
        for one in refs[: len(others)]:
            total = total + one[...].astype(f32)
        refs[-1][...] = total.astype(bf16)

    out = shape((stop - start, own.shape[2]), bf16)
    return call("fold", kernel, out, [own, near, *others], after, cost=cost)


def totals(g, src_own, src_others, dst_own, dst_near, dst_others):
    def kernel(*refs):
        src_out, belief_out, dst_out, next_out = refs[-4:]
        src_refs, refs = refs[: 1 + len(src_others)], refs[1 + len(src_others) : -4]
        own, near, parts = refs[0], refs[1], refs[2:]

        def src_total(here):
            return src_refs[0][here] + sum(one[here].astype(f32) for one in src_refs[1:])

        src_out[...] = src_total(slice(0, g.rows))
        belief_out[...] = src_total(slice(g.rows, g.packet)).astype(bf16)
        for start, stop in g.pieces:
            total = own[0, start:stop] + near[0, start:stop].astype(f32)
            for ((first, last), _), part in zip(dst_others, parts):
                if first <= start and stop <= last:
                    total = total + part[start - first : stop - first].astype(f32)
            edge = min(stop, g.rows)
            dst_out[start:edge] = total[: edge - start]
            if stop > g.rows:
                next_out[...] = total[g.rows - start :]

    outs = (
        shape((g.rows, g.width), f32),
        shape((g.batch, g.rows), bf16),
        shape((g.rows, g.width), f32),
        shape((g.batch, g.rows), f32),
    )
    operands = [src_own, *src_others, dst_own, dst_near, *[part for _, part in dst_others]]
    return call("totals", kernel, outs, operands, limit=12 * mib)


def per_device(n, src_emb, dst_emb, tile_dst, tile_count, beliefs, grad_next):
    g = Grid(n, *src_emb.shape, beliefs.shape[0])

    def swap(array, flip):
        return lax.ppermute(array, "src", [(i, i ^ flip) for i in range(n)])

    raw = {t: (swap(dst_emb, t), swap(grad_next, t)) for t in g.early[2:]}
    src_pack, dst_pack = pack(g, tile_dst, tile_count, src_emb, beliefs, dst_emb, grad_next)
    src_others = [swap(src_pack, g.row_flip(s)) for s in range(1, g.n_row)]
    packets = {2: swap(dst_pack, 2)}
    for t, (block, small) in raw.items():
        packets[t] = paired(block, small)
    src_kept, packets[0] = keep(src_pack, dst_pack, *[packets[t] for t in raw])
    src_packs = [src_kept] + src_others
    for t in sorted(g.late, key=lambda t: bin(t).count("1")):
        packets[t] = swap(packets[t ^ low_bit(t)], low_bit(t))
    stacks = []
    for slots in g.groups:
        pile = stack([packets[t] for t in slots], *(src_others if slots is g.late else ()))
        stacks += [pile, swap(pile, 1)]

    everyone = list(range(g.n_row))
    scored = [scores(g, everyone, g.parts[0], src_packs, stacks[:-2])]
    scored.append(scores(g, everyone, g.parts[1], src_packs, stacks[-2:], scored[0][2]))
    probs, grad_sums, stats = ([[one] for one in each] for each in zip(*scored))
    message = join(g, stats)
    messages = [message] + [swap(message, g.row_flip(s)) for s in range(1, g.n_row)]
    src_all, bel_all, *prob_grads = stage(g, src_packs, stacks)
    factors, belief_sum = norms(g, stats, grad_sums, messages)

    def columns(slots, kind, *after):
        return column_shares(g, slots, kind, factors, probs, prob_grads, src_all, bel_all, *after)

    odd_far, odd_near = ([t + 1 for t in slots] for slots in (g.far, g.near))
    change_of_far_odd, far_send = columns(odd_far, bf16)
    far_got = swap(far_send, 1)
    change_of_far, far_own = columns(g.far, f32, far_send)
    change_of_near_odd, near_send = columns(odd_near, bf16, far_own)
    near_got = swap(near_send, 1)
    change_of_near, near_own = columns(g.near, f32, near_send)
    changes = [change_of_far_odd, change_of_far, change_of_near_odd, change_of_near]
    order = [odd_far, g.far, odd_near, g.near]

    rest = list(range(1, g.n_row))
    src_send = row_shares(g, rest, bf16, changes, order, stacks, belief_sum)

    got = {t: [] for t in range(0, g.n_col, 2)}
    last = src_send[0]
    early = pl.CostEstimate(flops=1000000000, bytes_accessed=1 << 20, transcendentals=0)
    slow = pl.CostEstimate(flops=3000000000, bytes_accessed=1 << 20, transcendentals=0)
    for t in reversed(range(2, g.n_col, 2)):
        own, near, slots = (far_own, far_got, g.far) if t in g.far else (near_own, near_got, g.near)
        for piece in g.pieces if t in g.far else [(0, g.packet)]:
            others = [one for at, one in got[t] if at == piece]
            cost = slow if low_bit(t) > 2 and piece[0] else None
            last = fold(own, near, slots.index(t), piece, others, cost, last)
            one = swap(last, low_bit(t))
            got[t ^ low_bit(t)].append((piece, hand(one, cost=early) if low_bit(t) > 2 else one))
        if t == g.n_col - 2:
            src_got = [
                hand(swap(hand(one, last), g.row_flip(s)), cost=early) for one, s in zip(src_send, rest)
            ]
        elif t == 4:
            (src_own,) = row_shares(g, [0], f32, changes, order, stacks, belief_sum, last)
    grad_src, grad_belief, grad_dst, next_belief = totals(
        g, src_own, src_got, near_own, near_got, got[0][1::-1] + got[0][2:]
    )
    return (next_belief, grad_belief, grad_src, grad_dst)


def solution(mesh):
    placed = (
        P(("groups", "src"), None),
        P(("groups", "src"), None),
        P(("groups", "src"), None),
        P(("groups", "src")),
        P("groups", "src"),
        P("groups", "src"),
    )
    return jax.shard_map(
        functools.partial(per_device, mesh.shape["src"]),
        mesh=mesh,
        in_specs=placed,
        out_specs=(
            P("groups", "src"),
            P("groups", "src"),
            P(("groups", "src"), None),
            P(("groups", "src"), None),
        ),
        check_vma=False,
    )
```

```python
import functools

import jax
import jax.numpy as jnp
from jax import lax
from jax.experimental import pallas as pl
from jax.experimental.pallas import tpu as pltpu
from jax.sharding import PartitionSpec as P

f32 = jnp.float32
bf16 = jnp.bfloat16
unlisted = 1e30
mib = 1 << 20


class Grid:
    def __init__(self, n, rows, width, batch):
        bits = n.bit_length() - 1
        row_bits = max(1, bits // 2 - 1)
        self.n, self.rows, self.width, self.batch = n, rows, width, batch
        self.n_row = 1 << row_bits
        self.n_col = n // self.n_row
        self.span = self.n_row * rows
        self.packet = rows + batch
        self.head = (3 * self.n_row + 7) // 8 * 8
        even = range(0, self.n_col, 2)
        self.early = [t for t in even if t & (t - 1) == 0]
        self.late = [t for t in even if t & (t - 1)]
        self.groups = [self.early[2:], [2], [0], self.late]
        both = [group + [t + 1 for t in group] for group in self.groups]
        self.parts = [both[0] + both[1] + both[2], both[3]]
        self.spots = {t: (2 * k + (t & 1), group.index(t & ~1)) for k, group in enumerate(self.groups) for t in both[k]}
        top = self.n_col // 2
        self.far = [t for t in range(top, self.n_col, 2)]
        self.near = [t for t in range(0, top, 2)]

    def row_flip(self, s):
        return s * self.n_col

    def where(self, t):
        part = 0 if t in self.parts[0] else 1
        return part, self.parts[part].index(t)


def low_bit(t):
    return t & -t


def dot(a, b, dims):
    return lax.dot_general(a, b, (dims, ((), ())), preferred_element_type=f32)


NN = ((1,), (0,))
NT = ((1,), (1,))
TN = ((0,), (0,))


def in_vmem():
    return pl.BlockSpec(memory_space=pltpu.VMEM)


def anywhere():
    return pl.BlockSpec(memory_space=pl.ANY)


def in_smem():
    return pl.BlockSpec(memory_space=pltpu.SMEM)


shape = jax.ShapeDtypeStruct


def call(name, kernel, out_shape, operands, after=(), scratch=(), limit=8 * mib, cost=None):
    many = isinstance(out_shape, tuple)
    return pl.pallas_call(
        kernel,
        out_shape=out_shape,
        in_specs=[in_vmem()] * len(operands) + [anywhere()] * len(after),
        out_specs=(in_vmem(),) * len(out_shape) if many else in_vmem(),
        scratch_shapes=list(scratch),
        compiler_params=pltpu.CompilerParams(vmem_limit_bytes=limit),
        cost_estimate=cost,
        name=name,
    )(*operands, *after)


def pack_kernel(g, tile_ref, count_ref, src_ref, bel_ref, dst_ref, grad_ref, src_pack, dst_pack, flags):
    rows, batch = g.rows, g.batch
    me = lax.axis_index("src")
    count = jnp.broadcast_to(count_ref[...], (1, g.width))
    for k in range(g.n):
        flags[pl.ds(tile_ref[0, k] ^ me, 1), :] = jnp.where(count > k, 1.0, 0.0).astype(f32)
    src_pack[:rows] = src_ref[...]
    src_pack[rows : rows + batch] = bel_ref[...]
    src_pack[rows + batch :] = flags[...].astype(bf16)
    dst_pack[:rows] = dst_ref[...]
    dst_pack[rows:] = grad_ref[...]


def pack(g, tile_dst, tile_count, src_emb, beliefs, dst_emb, grad_next):
    return pl.pallas_call(
        functools.partial(pack_kernel, g),
        out_shape=(
            shape((g.rows + g.batch + g.n, g.width), bf16),
            shape((g.rows + g.batch, g.width), bf16),
        ),
        in_specs=[in_smem()] + [in_vmem()] * 5,
        out_specs=(in_vmem(),) * 2,
        scratch_shapes=[pltpu.VMEM((g.n, g.width), f32)],
        compiler_params=pltpu.CompilerParams(vmem_limit_bytes=60 * mib),
        name="pack",
    )(tile_dst, tile_count.reshape(1, 1), src_emb, beliefs, dst_emb, grad_next)


def keep(src_pack, dst_pack, *after):
    def kernel(src_ref, dst_ref, *refs):
        refs[-2][...] = src_ref[...]
        refs[-1][...] = dst_ref[...]

    outs = (shape(src_pack.shape, bf16), shape(dst_pack.shape, bf16))
    return call("keep", kernel, outs, [src_pack, dst_pack], after, limit=2 * mib)


def hand(one, *after):
    def kernel(one_ref, *refs):
        refs[-1][...] = one_ref[...]

    return call("hand", kernel, shape(one.shape, one.dtype), [one], after, limit=2 * mib)


def paired(block, small, *after):
    def kernel(block_ref, small_ref, *refs):
        refs[-1][: block.shape[0]] = block_ref[...]
        refs[-1][block.shape[0] :] = small_ref[...]

    out = shape((block.shape[0] + small.shape[0], block.shape[1]), bf16)
    return call("paired", kernel, out, [block, small], after, limit=2 * mib)


def stack(packs, *after):
    def kernel(*refs):
        for i in range(len(packs)):
            refs[-1][i] = refs[i][...]

    out = shape((len(packs),) + packs[0].shape, packs[0].dtype)
    return call("stack", kernel, out, packs, after)


def score_kernel(g, row_slots, slots, *refs):
    rows, batch, span = g.rows, g.batch, len(row_slots) * g.rows
    src_packs, stacks = refs[: len(row_slots)], refs[len(row_slots) :]
    prob_ref, grad_sum, stats, src_all, bel_all = refs[-5:]
    first = g.spots[slots[0]][0]
    listed = []
    for p, one in enumerate(src_packs):
        lanes = slice(p * rows, (p + 1) * rows)
        src_all[lanes] = one[:rows]
        bel_all[:, lanes] = one[rows : rows + batch]
        listed.append((one[rows + batch :].astype(f32) - 1.0) * unlisted)

    def packet(t):
        stack, place = g.spots[t]
        return stacks[stack - first].at[place]

    top = jnp.full((8, span), -unlisted, f32)
    for i, t in enumerate(slots):
        flips = [g.row_flip(s) | t for s in row_slots]
        bias = jnp.concatenate([one[v : v + 1] for one, v in zip(listed, flips)], axis=1)
        logits = dot(packet(t)[:rows], src_all[...], NT) + bias
        prob_ref[i * rows : (i + 1) * rows] = logits
        top = jnp.maximum(top, jnp.max(logits.reshape(rows // 8, 8, span), axis=0))
    top = jnp.max(top, axis=0, keepdims=True)
    total = jnp.zeros((8, span), f32)
    grad_sum[...] = jnp.zeros(grad_sum.shape, f32)
    for i, t in enumerate(slots):
        here = slice(i * rows, (i + 1) * rows)
        prob = jnp.exp(prob_ref[here] - top)
        prob_ref[here] = prob
        grad_sum[...] += dot(packet(t)[rows:], prob.astype(bf16), NN)
        total = total + jnp.sum(prob.reshape(rows // 8, 8, span), axis=0)
    stats[0:1] = top
    stats[1:2] = jnp.sum(total, axis=0, keepdims=True)
    stats[2:3] = jnp.sum(bel_all[...].astype(f32) * grad_sum[...], axis=0, keepdims=True)


def scores(g, row_slots, slots, src_packs, stacks, *after):
    tall, span = len(slots) * g.rows, len(row_slots) * g.rows
    outs = (shape((tall, span), f32), shape((g.batch, span), f32), shape((3, span), f32))
    scratch = [pltpu.VMEM((span, g.width), bf16), pltpu.VMEM((g.batch, span), bf16)]
    kernel = functools.partial(score_kernel, g, row_slots, slots)
    operands = [*[src_packs[s] for s in row_slots], *stacks]
    return call("scores", kernel, outs, operands, after, scratch, tall * span * 8 + 6 * mib)


def flat(parts):
    return [one for part in parts for one in part]


def unflat(refs, parts):
    out = []
    for part in parts:
        out.append(refs[: len(part)])
        refs = refs[len(part) :]
    return out, refs


def wide(refs, here=slice(None)):
    return jnp.concatenate([one[here] for one in refs], axis=1)


def merged(stats):
    tops = [one[0:1] for one in stats]
    top = functools.reduce(jnp.maximum, tops)
    factors = [jnp.exp(one - top) for one in tops]
    total = sum(factor * one[1:2] for factor, one in zip(factors, stats))
    dots = sum(factor * one[2:3] for factor, one in zip(factors, stats))
    return top, total, dots


def join(g, stats):
    def kernel(*refs):
        out = refs[-1]
        parts, _ = unflat(refs, stats)
        for kind, value in enumerate(merged([wide(one) for one in parts])):
            for s in range(g.n_row):
                at = kind * g.n_row + s
                out[at : at + 1] = value[:, s * g.rows : (s + 1) * g.rows]
        if g.head > 3 * g.n_row:
            out[3 * g.n_row :] = jnp.zeros((g.head - 3 * g.n_row, g.rows), f32)

    return call("join", kernel, shape((g.head, g.rows), f32), flat(stats), limit=2 * mib)


def stage(g, src_packs, stacks):
    rows, batch = g.rows, g.batch

    def kernel(*refs):
        src_refs, stack_refs = refs[: g.n_row], refs[g.n_row : -4]
        src_all, bel_all, *prob_grads = refs[-4:]
        for s, one in enumerate(src_refs):
            lanes = slice(s * rows, (s + 1) * rows)
            src_all[lanes] = one[:rows]
            bel_all[:, lanes] = one[rows : rows + batch]
        for slots, out in zip(g.parts, prob_grads):
            for i, t in enumerate(slots):
                stack, place = g.spots[t]
                out[i * rows : (i + 1) * rows] = dot(stack_refs[stack][place, rows:], bel_all[...], TN)

    outs = (
        shape((g.span, g.width), bf16),
        shape((batch, g.span), bf16),
        *[shape((len(part) * rows, g.span), f32) for part in g.parts],
    )
    limit = g.n * rows * rows * 4 + 8 * mib
    return call("stage", kernel, outs, [*src_packs, *stacks], limit=limit)


def norms(g, stats, grad_sums, messages):
    def kernel(*refs):
        part_stats, refs = unflat(refs, stats)
        part_sums, refs = unflat(refs, grad_sums)
        everyone, (factors, belief_sum) = refs[: g.n_row], refs[-2:]
        part_stats = [wide(one) for one in part_stats]
        for s in range(g.n_row):
            lanes = slice(s * g.rows, (s + 1) * g.rows)

            def row(u, kind):
                at = kind * g.n_row + (s ^ u)
                return everyone[u][at : at + 1]

            tops = [row(u, 0) for u in range(g.n_row)]
            top = functools.reduce(jnp.maximum, tops)
            shares = [jnp.exp(one - top) for one in tops]
            inverse = 1.0 / sum(share * row(u, 1) for u, share in enumerate(shares))
            for part, one in enumerate(part_stats):
                factors[part : part + 1, lanes] = jnp.exp(one[0:1, lanes] - top) * inverse
            dots = sum(share * row(u, 2) for u, share in enumerate(shares))
            factors[2:3, lanes] = dots * inverse
        belief_sum[...] = wide(part_sums[0]) * factors[0:1] + wide(part_sums[1]) * factors[1:2]

    outs = (shape((8, g.span), f32), shape((g.batch, g.span), f32))
    return call("norms", kernel, outs, [*flat(stats), *flat(grad_sums), *messages], limit=4 * mib)


def column_shares(g, slots, kind, factors, probs, prob_grads, src_all, bel_all, *after):
    rows = g.rows

    def kernel(factors, *refs):
        prob_refs, refs = unflat(refs, probs)
        prob_grads, (src_all, bel_all), (change_ref, share_ref) = refs[:2], refs[2:4], refs[-2:]
        for i, t in enumerate(slots):
            part, place = g.where(t)
            here = slice(place * rows, (place + 1) * rows)
            prob = wide(prob_refs[part], here) * factors[part : part + 1]
            change = (prob * (prob_grads[part][here] - factors[2:3])).astype(bf16)
            change_ref[i * rows : (i + 1) * rows] = change
            share_ref[i, :rows] = dot(change, src_all[...], NN).astype(kind)
            share_ref[i, rows:] = dot(bel_all[...], prob.astype(bf16), NT).astype(kind)

    outs = (
        shape((len(slots) * rows, g.span), bf16),
        shape((len(slots), g.packet, g.width), kind),
    )
    operands = [factors, *flat(probs), *prob_grads, src_all, bel_all]
    return call("column_shares", kernel, outs, operands, after, limit=g.n * rows * rows * 8 + 6 * mib)


def row_shares(g, slots, kind, changes, order, stacks, belief_sum, *after):
    rows = g.rows

    def kernel(*refs):
        changes = refs[: len(order)]
        stack_refs = refs[len(order) : len(order) + len(stacks)]
        belief_sum = refs[len(order) + len(stacks)]
        for s, out in zip(slots, refs[-len(slots) :]):
            lanes = slice(s * rows, (s + 1) * rows)
            total = 0.0
            for change, columns in zip(changes, order):
                for i, t in enumerate(columns):
                    stack, place = g.spots[t]
                    packet = stack_refs[stack][place, :rows]
                    total = total + dot(change[i * rows : (i + 1) * rows, lanes], packet, TN)
            out[:rows] = total.astype(kind)
            out[rows:] = belief_sum[:, lanes].astype(kind)

    outs = (shape((g.packet, g.width), kind),) * len(slots)
    operands = [*changes, *stacks, belief_sum]
    return call("row_shares", kernel, outs, operands, after, limit=g.n * rows * rows * 4 + 6 * mib)


def fold(own, near, i, others, cost, *after):
    def kernel(own_ref, near_ref, *refs):
        total = own_ref[i] + near_ref[i].astype(f32)
        for one in refs[: len(others)]:
            total = total + one[...].astype(f32)
        refs[-1][...] = total.astype(bf16)

    return call("fold", kernel, shape(own.shape[1:], bf16), [own, near, *others], after, cost=cost)


def totals(g, src_own, src_others, dst_own, dst_near, dst_others):
    def kernel(*refs):
        src_out, belief_out, dst_out, next_out = refs[-4:]
        src_refs, dst_refs = refs[: 1 + len(src_others)], refs[1 + len(src_others) : -4]

        def added(out, here, own, others):
            total = own[here] + sum(one[here].astype(f32) for one in others)
            out[...] = total.astype(out.dtype)

        big, small = slice(0, g.rows), slice(g.rows, g.packet)
        dst_refs = [dst_refs[0].at[0], dst_refs[1].at[0], *dst_refs[2:]]
        added(src_out, big, src_refs[0], src_refs[1:])
        added(belief_out, small, src_refs[0], src_refs[1:])
        added(dst_out, big, dst_refs[0], dst_refs[1:])
        added(next_out, small, dst_refs[0], dst_refs[1:])

    outs = (
        shape((g.rows, g.width), f32),
        shape((g.batch, g.rows), bf16),
        shape((g.rows, g.width), f32),
        shape((g.batch, g.rows), f32),
    )
    operands = [src_own, *src_others, dst_own, dst_near, *dst_others]
    return call("totals", kernel, outs, operands, limit=12 * mib)


def per_device(n, src_emb, dst_emb, tile_dst, tile_count, beliefs, grad_next):
    g = Grid(n, *src_emb.shape, beliefs.shape[0])

    def swap(array, flip):
        return lax.ppermute(array, "src", [(i, i ^ flip) for i in range(n)])

    raw = {t: (swap(dst_emb, t), swap(grad_next, t)) for t in g.early[2:]}
    src_pack, dst_pack = pack(g, tile_dst, tile_count, src_emb, beliefs, dst_emb, grad_next)
    src_others = [swap(src_pack, g.row_flip(s)) for s in range(1, g.n_row)]
    packets = {2: swap(dst_pack, 2)}
    for t, (block, small) in raw.items():
        packets[t] = paired(block, small)
    src_kept, packets[0] = keep(src_pack, dst_pack, *[packets[t] for t in raw])
    src_packs = [src_kept] + src_others
    for t in sorted(g.late, key=lambda t: bin(t).count("1")):
        packets[t] = swap(packets[t ^ low_bit(t)], low_bit(t))
    stacks = []
    for slots in g.groups:
        pile = stack([packets[t] for t in slots], *(src_others if slots is g.late else ()))
        stacks += [pile, swap(pile, 1)]

    everyone = list(range(g.n_row))
    scored = [scores(g, everyone, g.parts[0], src_packs, stacks[:-2])]
    scored.append(scores(g, everyone, g.parts[1], src_packs, stacks[-2:], scored[0][2]))
    probs, grad_sums, stats = ([[one] for one in each] for each in zip(*scored))
    message = join(g, stats)
    messages = [message] + [swap(message, g.row_flip(s)) for s in range(1, g.n_row)]
    src_all, bel_all, *prob_grads = stage(g, src_packs, stacks)
    factors, belief_sum = norms(g, stats, grad_sums, messages)

    def columns(slots, kind, *after):
        return column_shares(g, slots, kind, factors, probs, prob_grads, src_all, bel_all, *after)

    odd_far, odd_near = ([t + 1 for t in slots] for slots in (g.far, g.near))
    change_of_far_odd, far_send = columns(odd_far, bf16)
    far_got = swap(far_send, 1)
    change_of_far, far_own = columns(g.far, f32, far_send)
    change_of_near_odd, near_send = columns(odd_near, bf16, far_own)
    near_got = swap(near_send, 1)
    change_of_near, near_own = columns(g.near, f32, near_send)
    changes = [change_of_far_odd, change_of_far, change_of_near_odd, change_of_near]
    order = [odd_far, g.far, odd_near, g.near]

    got = {t: [] for t in range(0, g.n_col, 2)}
    last = near_send
    for t in reversed(range(2, g.n_col, 2)):
        own, near, slots = (far_own, far_got, g.far) if t in g.far else (near_own, near_got, g.near)
        slow = pl.CostEstimate(flops=3 * 10**9, bytes_accessed=1 << 20, transcendentals=0)
        send = fold(own, near, slots.index(t), got[t], slow if low_bit(t) > 2 else None, last)
        one = swap(send, low_bit(t))
        got[t ^ low_bit(t)].append(hand(one) if low_bit(t) > 2 else one)
        if t == g.n_col - 2:
            rest = list(range(1, g.n_row))
            src_send = row_shares(g, rest, bf16, changes, order, stacks, belief_sum, send)
            src_got = [swap(one, g.row_flip(s)) for one, s in zip(src_send, rest)]
        elif t == 4:
            (src_own,) = row_shares(g, [0], f32, changes, order, stacks, belief_sum, send)
        last = send
    grad_src, grad_belief, grad_dst, next_belief = totals(
        g, src_own, src_got, near_own, near_got, got[0]
    )
    return (next_belief, grad_belief, grad_src, grad_dst)


def solution(mesh):
    placed = (
        P(("groups", "src"), None),
        P(("groups", "src"), None),
        P(("groups", "src"), None),
        P(("groups", "src")),
        P("groups", "src"),
        P("groups", "src"),
    )
    return jax.shard_map(
        functools.partial(per_device, mesh.shape["src"]),
        mesh=mesh,
        in_specs=placed,
        out_specs=(
            P("groups", "src"),
            P("groups", "src"),
            P(("groups", "src"), None),
            P(("groups", "src"), None),
        ),
        check_vma=False,
    )
```
